32 devices in a mesh: groups: 2 (over y), seq: 4 (over z), head: 2 (over x), sub: 2 (over core).
Axes of the slice: x: 2, y: 2, z: 4, core: 2. Of those that a mesh axis runs over, the one named last changes fastest.
Arguments:
- frames_in: bfloat16 [2048, 1536], P(('groups', 'seq', 'head', 'sub')), parts along dimension 0, may hold values from -30 to 30
- attn_gain: float32 [1536], replicated, may hold values from 0.25 to 1.75
- w_qkv: bfloat16 [1536, 24, 192], P(None, ('head', 'sub')), may hold values from -1 to 1
- w_out: bfloat16 [1536, 1536], P(('head', 'sub')), may hold values from -0.3125 to 0.3125
- vit_gain: float32 [1536], replicated, may hold values from 0.25 to 1.75
- w_pair: bfloat16 [2, 1536, 1024], P(None, None, ('head', 'sub')), may hold values from -0.109375 to 0.109375
- w_act: float32 [1024, 7], P(('head', 'sub')), may hold values from -0.375 to 0.375
- pair_frames: int32 [4, 15], P('groups'), parts along dimension 0, may hold values from 0 to 14, each once within a row
Outputs:
- hidden: bfloat16 [2048, 1536], P(('groups', 'seq', 'head', 'sub')), parts along dimension 0
- actions: float32 [4, 15, 7], P('groups'), parts along dimension 0
The draws below stay inside these ranges and needn't reach their ends.
There are 2 independent parts, one for each index of `groups`. The reference program is written for one: setup_inputs(seed, part) draws one part's arguments, and reference() takes and returns one part's arrays. A program takes and returns all parts, laid end to end along the dimension named above; an argument that names none is the same for every part. Nothing has to cross between parts.
All inputs are finite; a program needn't handle non-finite values.
Results may differ from the reference program's by a relative error of at most 0.01.
Values may be sent and summed in bfloat16 or wider, within the bound.
A program may use at most 64 MiB of HBM per device.

```python
import math
import jax
import jax.numpy as jnp
from jax import lax

HEADS = 24
HEAD_DIM = 64
D = 1536
E = 1024
A = 7
F = 16
ROLLS = 2
P_SIZE = 32
TOKENS = 1024
N_HEAD = 2
N_SUB = 2


def draw_frames_in(key, part):
    key_noise = jax.random.fold_in(key, 11)
    key_row = jax.random.fold_in(key, 12)
    key_col = jax.random.fold_in(key, 13)
    columns = TOKENS // F
    noise_part = jax.random.normal(key_noise, (F, columns, D), jnp.float32)
    row_scale = jnp.exp(jax.random.uniform(key_row, (F, columns, 1), jnp.float32, math.log(0.3), math.log(3.0)))
    col_scale = jnp.exp(jax.random.uniform(key_col, (1, 1, D), jnp.float32, math.log(0.3), math.log(3.0)))
    base_part = noise_part
    values_out = jnp.clip(row_scale * col_scale * base_part, -30.0, 30.0)
    return values_out.reshape(TOKENS, D).astype(jnp.bfloat16)


def draw_w_qkv(key, part):
    key_base = jax.random.fold_in(key, 21)
    base_part = jax.random.normal(key_base, (D, HEADS, 3 * HEAD_DIM), jnp.float32) * D ** (-0.5)
    return jnp.clip(base_part, -1.0, 1.0).astype(jnp.bfloat16)


def steps_of(own_key, shape, shards, low, high):
    def one(dim, parts):
        heights = jax.random.uniform(jax.random.fold_in(jax.random.fold_in(own_key, 6), dim), (parts,), jnp.float32, low / len(shards), high / len(shards))
        return jnp.repeat(jnp.exp(heights), shape[dim] // parts).reshape((-1,) + (1,) * (len(shape) - dim - 1))

    gain = one(*shards[0])
    for cut in shards[1:]:
        gain = gain * one(*cut)
    return gain


def bell_draw(rng, shape, deviation, most, cuts=(), kind=jnp.bfloat16):
    drawn = jax.random.normal(rng, shape, jnp.float32) * deviation
    if len(cuts) > 0:
        drawn = steps_of(rng, shape, cuts, -0.22, 0.18) * drawn
    return jnp.clip(drawn, min=-most, max=most).astype(kind)


def setup_inputs(seed: int = 0, part: int = 0) -> dict:
    arg_keys = jax.random.split(jax.random.key(seed), 9)
    own_keys = jax.random.split(jax.random.fold_in(arg_keys[8], part), 9)
    frames_in = draw_frames_in(jax.random.fold_in(jax.random.fold_in(arg_keys[8], part), 71), part)
    attn_gain = jnp.clip(1.0 + 0.15 * jax.random.normal(arg_keys[1], (D,), jnp.float32), 0.25, 1.75)
    w_qkv = draw_w_qkv(jax.random.fold_in(arg_keys[8], 71), part)
    w_out = bell_draw(arg_keys[3], (D, D), (D // 4) ** -0.5, 0.3125, ((0, 4),))
    vit_gain = jnp.clip(1.0 + 0.15 * jax.random.normal(arg_keys[4], (D,), jnp.float32), 0.25, 1.75)
    w_pair = bell_draw(arg_keys[5], (2, D, E), (2 * D) ** -0.5, 0.109375, ((2, 4),))
    w_act = bell_draw(arg_keys[6], (E, A), (E // 4) ** -0.5, 0.375, ((0, 4),), jnp.float32)
    pair_frames = jax.vmap(lambda own: jax.random.permutation(own, F - 1))(jax.random.split(own_keys[7], ROLLS)).reshape((ROLLS, F - 1)).astype(jnp.int32)
    return dict(frames_in=frames_in, attn_gain=attn_gain, w_qkv=w_qkv, w_out=w_out, vit_gain=vit_gain, w_pair=w_pair, w_act=w_act, pair_frames=pair_frames)


def normalize(values_in, gain_vec):
    floats = values_in.astype(jnp.float32)
    mean_sq = lax.optimization_barrier(jnp.mean(floats * floats, axis=-1, keepdims=True))
    return (floats * lax.rsqrt(mean_sq + 1e-06) * gain_vec).astype(jnp.bfloat16)

def reference(frames_in, attn_gain, w_qkv, w_out, vit_gain, w_pair, w_act, pair_frames):
    columns = TOKENS // F
    normed = normalize(frames_in, attn_gain)
    qkv_rows = jnp.dot(normed, w_qkv.reshape(D, HEADS * 3 * HEAD_DIM), preferred_element_type=jnp.float32).astype(jnp.bfloat16)
    qkv_rows = qkv_rows.reshape(F, columns, HEADS, 3 * HEAD_DIM)
    queries = qkv_rows[..., :HEAD_DIM].astype(jnp.float32)
    key_part = qkv_rows[..., HEAD_DIM:2 * HEAD_DIM].astype(jnp.float32)
    value_part = qkv_rows[..., 2 * HEAD_DIM:].astype(jnp.float32)
    scores = jnp.einsum('fchd,gchd->chfg', queries, key_part) * HEAD_DIM ** (-0.5)
    row_peak = lax.optimization_barrier(jnp.max(scores, axis=-1, keepdims=True))
    weights = jnp.exp(scores - row_peak)
    weights = (weights / lax.optimization_barrier(jnp.sum(weights, axis=-1, keepdims=True))).astype(jnp.bfloat16)
    mixed_out = jnp.einsum('chfg,gchd->fchd', weights.astype(jnp.float32), value_part).astype(jnp.bfloat16)
    mixed_out = mixed_out.reshape(TOKENS, D)
    group_count = N_HEAD * N_SUB
    group_rows = D // group_count
    branch = jnp.zeros((TOKENS, D), jnp.float32)
    for group in range(group_count):
        product = jnp.dot(mixed_out[:, group * group_rows:(group + 1) * group_rows], w_out[group * group_rows:(group + 1) * group_rows], preferred_element_type=jnp.float32)
        rounded = lax.optimization_barrier(product.astype(jnp.bfloat16))
        branch = branch + rounded.astype(jnp.float32)
    hidden = (frames_in.astype(jnp.float32) + branch).astype(jnp.bfloat16)
    vit_in = normalize(hidden, vit_gain).reshape(F, columns, D)
    current = jnp.dot(vit_in[:-1].reshape(-1, D), w_pair[0], preferred_element_type=jnp.float32)
    following = jnp.dot(vit_in[1:].reshape(-1, D), w_pair[1], preferred_element_type=jnp.float32)
    activated = jax.nn.gelu(current + following, approximate=False)
    pooled = lax.optimization_barrier(jnp.mean(activated.reshape(F - 1, ROLLS, P_SIZE, E), axis=2))
    pooled = jnp.transpose(pooled, (1, 0, 2))
    chosen = jnp.take_along_axis(pooled, pair_frames[:, :, None].astype(jnp.int32), axis=1)
    actions = jnp.einsum('rje,ea->rja', chosen, w_act, precision=lax.Precision.HIGHEST)
    return (hidden, actions)
```

```python
import functools
import jax
import jax.numpy as jnp
from jax import lax
from jax.experimental import pallas as pl
from jax.experimental.pallas import tpu as pltpu
from jax.sharding import PartitionSpec as P

F = 16
ROLLS = 2


def from_behind(value, axis, steps):
    count = lax.axis_size(axis)
    leading, last = (max(0, -steps), min(count, count - steps))
    return lax.ppermute(value, axis, [(source, source + steps) for source in range(leading, last)])


def normalize(values_in, gain_vec):
    floats = values_in.astype(jnp.float32)
    mean_sq = jnp.mean(floats * floats, axis=-1, keepdims=True)
    return (floats * lax.rsqrt(mean_sq + 1e-06) * gain_vec).astype(jnp.bfloat16)


def shards_by_frame(frames_in, attn_gain, w_qkv, w_out, vit_gain, w_pair, w_act, pair_frames):
    rows_own = frames_in.shape[0]
    model_width = frames_in.shape[1]
    seq_count = lax.axis_size("seq")
    split_count = lax.axis_size(("head", "sub"))
    block_rows = rows_own * split_count
    total_cols = block_rows * seq_count // F
    frames_local = max(1, F // seq_count)
    cols_local = block_rows // frames_local
    frame_step = max(1, seq_count // F)
    heads_local = w_qkv.shape[1]
    triple_dim = w_qkv.shape[2]
    head_dim = triple_dim // 3
    qkv_matrix = w_qkv.reshape(model_width, heads_local * triple_dim)
    normed = lax.all_gather(normalize(frames_in, attn_gain), ("head", "sub"), axis=0, tiled=True)
    qkv_rows = jnp.dot(normed, qkv_matrix, preferred_element_type=jnp.float32).astype(jnp.bfloat16)
    qkv_rows = qkv_rows.reshape(
        frames_local, seq_count, cols_local // seq_count, heads_local, triple_dim
    )
    columns = lax.all_to_all(qkv_rows, "seq", split_axis=1, concat_axis=0, tiled=True)
    item_count = columns.shape[2]
    by_frame = columns.reshape(F, -1, heads_local, triple_dim)
    queries = by_frame[..., :head_dim]
    key_part = by_frame[..., head_dim : 2 * head_dim]
    value_part = by_frame[..., 2 * head_dim :]
    scores = jnp.einsum(
        "fchd,gchd->chfg", queries, key_part, preferred_element_type=jnp.float32
    ) * head_dim ** (-0.5)
    row_peak = jnp.max(scores, axis=-1, keepdims=True)
    weights = jnp.exp(scores - row_peak)
    weights = (weights / jnp.sum(weights, axis=-1, keepdims=True)).astype(jnp.bfloat16)
    mixed_out = jnp.einsum(
        "chfg,gchd->fchd", weights, value_part, preferred_element_type=jnp.float32
    ).astype(jnp.bfloat16)
    mixed_out = mixed_out.reshape(seq_count * frames_local, 1, item_count, heads_local * head_dim)
    attended = lax.all_to_all(mixed_out, "seq", split_axis=0, concat_axis=1, tiled=True)
    attended = attended.reshape(block_rows, heads_local * head_dim)
    branch_sum = lax.psum_scatter(
        jnp.dot(attended, w_out, preferred_element_type=jnp.float32).astype(jnp.bfloat16),
        ("head", "sub"),
        scatter_dimension=0,
        tiled=True,
    ).astype(jnp.float32)
    hidden = (frames_in.astype(jnp.float32) + branch_sum).astype(jnp.bfloat16)
    vit_own = normalize(hidden, vit_gain)
    vit_rows = lax.all_gather(vit_own, ("head", "sub"), axis=0, tiled=True)
    current = jnp.dot(vit_rows, w_pair[0], preferred_element_type=jnp.float32)
    ahead_proj = jnp.dot(vit_rows, w_pair[1], preferred_element_type=jnp.float32)
    ahead_proj = ahead_proj.reshape(frames_local, cols_local, -1)
    arrived = from_behind(ahead_proj[:1].astype(jnp.bfloat16), "seq", -frame_step).astype(
        jnp.float32
    )
    following = jnp.concatenate([ahead_proj[1:], arrived], axis=0).reshape(block_rows, -1)
    embedded = current + following
    activated = jax.nn.gelu(embedded, approximate=False).reshape(frames_local, cols_local, -1)
    seq_index = lax.axis_index("seq")
    first_token = seq_index * block_rows
    frame_first = first_token // total_cols
    col_first = first_token % total_cols
    patches = total_cols // ROLLS
    roll_ids = (col_first + jnp.arange(cols_local, dtype=jnp.int32)) // patches
    member = (roll_ids[None, :] == jnp.arange(ROLLS, dtype=jnp.int32)[:, None]).astype(
        jnp.float32
    ) / patches
    pooled = jnp.einsum("rp,fpe->fre", member, activated, precision=lax.Precision.HIGHEST)
    scored = jnp.einsum("fre,ea->fra", pooled, w_act, precision=lax.Precision.HIGHEST)
    frame_ids = frame_first + jnp.arange(frames_local, dtype=jnp.int32)
    selector = (pair_frames[:, :, None] == frame_ids[None, None, :]).astype(jnp.float32)
    partial_value = jnp.einsum("rjf,fra->rja", selector, scored, precision=lax.Precision.HIGHEST)
    actions = lax.psum(partial_value, ("seq", "head", "sub"))
    return (hidden, actions)


def nt_dot(lhs, rhs, **kw):
    return lax.dot_general(
        lhs, rhs, (((1,), (1,)), ((), ())), preferred_element_type=jnp.float32, **kw
    )


def tn_dot(lhs, rhs):
    return lax.dot_general(
        lhs, rhs, (((0,), (0,)), ((), ())), preferred_element_type=jnp.float32
    )


def fused_kernel(
    sizes,
    frames,
    attn_gain,
    w_qkv,
    w_out,
    vit_gain,
    w_pair,
    w_act,
    pair_frames,
    hidden_out,
    actions_out,
    tokens,
    normed,
    wq,
    wo,
    wp,
    mixed,
    part_send,
    part_recv,
    part_own,
    head_send,
    head_recv,
    hidden,
    vit,
    pair,
    scored,
    local_sem,
    a_send,
    a_recv,
    b_send,
    b_recv,
    c_send,
    c_recv,
    d_send,
    d_recv,
    e_send,
    e_recv,
    v_send,
    v_recv,
    o_send,
    o_recv,
    q_send,
    q_recv,
):
    S, H, U, heads, head_dim = sizes
    N = S * H * U
    rows, width = tokens.shape
    cols = rows // N
    unit = rows // U
    chunk = H * cols
    actions_n, rolls, picks = actions_out.shape
    out_width = wp.shape[2]
    s, h, u = lax.axis_index("seq"), lax.axis_index("head"), lax.axis_index("sub")
    me = (s * H + h) * U + u

    def at(value, size=cols):
        return pl.ds(pl.multiple_of(value, size), size)

    def slab(u_, s_, h_):
        return at(((u_ * S + s_) * H + h_) * cols)

    def piece(s_):
        return at(s_ * chunk, chunk)

    def remote(source, target, send, recv, where):
        return pltpu.make_async_remote_copy(
            src_ref=source,
            dst_ref=target,
            send_sem=send,
            recv_sem=recv,
            device_id=where,
            device_id_type=pl.DeviceIdType.MESH,
        )

    sent = []

    def send(*args):
        copy = remote(*args)
        copy.start()
        sent.append(copy)

    load_q = pltpu.make_async_copy(w_qkv, wq, local_sem.at[0])
    load_o = pltpu.make_async_copy(w_out, wo, local_sem.at[1])
    load_p = pltpu.make_async_copy(w_pair, wp, local_sem.at[2])
    load_own = pltpu.make_async_copy(
        frames.at[at(s * cols)], tokens.at[slab(u, s, h)], local_sem.at[3]
    )
    load_own.start()
    load_q.start()
    load_o.start()
    load_p.start()

    barrier = pltpu.get_barrier_semaphore()

    def greet(step, carry):
        other = lax.rem(me + step, N)
        where = {"seq": other // (H * U), "head": other // U % H, "sub": other % U}
        pl.semaphore_signal(
            barrier, inc=1, device_id=where, device_id_type=pl.DeviceIdType.MESH
        )
        return carry

    lax.fori_loop(1, N, greet, 0)
    pl.semaphore_wait(barrier, N - 1)

    steps = sorted(range(S), key=lambda d: min(d, S - d))

    for dz in reversed(steps[1:]):
        t = lax.rem(s + dz, S)
        send(
            frames.at[at(t * cols)],
            tokens.at[slab(u, s, h)],
            a_send.at[dz - 1],
            a_recv.at[dz - 1],
            {"seq": t},
        )

    def to_heads(dz):
        s_ = lax.rem(s + S - dz, S)
        place = tokens.at[slab(u, s_, h)]
        for dh in range(1, H):
            send(
                place,
                place,
                b_send.at[dh - 1, dz],
                b_recv.at[dh - 1, dz],
                {"head": lax.rem(h + dh, H)},
            )
        to_subs(0, dz)

    def to_subs(dh, dz):
        place = tokens.at[slab(u, lax.rem(s + S - dz, S), lax.rem(h + H - dh, H))]
        for du in range(1, U):
            send(
                place,
                place,
                c_send.at[du - 1, dh, dz],
                c_recv.at[du - 1, dh, dz],
                {"sub": lax.rem(u + du, U)},
            )

    def from_heads(dz):
        s_ = lax.rem(s + S - dz, S)
        for dh in range(1, H):
            place = tokens.at[slab(u, s_, lax.rem(h + H - dh, H))]
            remote(
                place, place, b_send.at[dh - 1, dz], b_recv.at[dh - 1, dz], {"head": h}
            ).wait_recv()
            to_subs(dh, dz)

    def scale(values, gain):
        floats = values.astype(jnp.float32)
        mean_sq = jnp.mean(floats * floats, axis=-1, keepdims=True)
        return (floats * lax.rsqrt(mean_sq + 1e-06) * gain[...]).astype(jnp.bfloat16)

    def normalize_piece(u_, s_):
        place = at((u_ * S + s_) * chunk, chunk)
        normed[place, :] = scale(tokens[place, :], attn_gain)

    load_own.wait()
    to_heads(0)
    for index, dz in enumerate(steps):
        if index + 1 < S:
            ahead = steps[index + 1]
            place = tokens.at[slab(u, lax.rem(s + S - ahead, S), h)]
            remote(
                place, place, a_send.at[ahead - 1], a_recv.at[ahead - 1], {"seq": s}
            ).wait_recv()
            to_heads(ahead)
        from_heads(dz)
        normalize_piece(u, lax.rem(s + S - dz, S))
    for dz in steps:
        s_ = lax.rem(s + S - dz, S)
        for du in range(1, U):
            u_ = lax.rem(u + U - du, U)
            for dh in range(H):
                place = tokens.at[slab(u_, s_, lax.rem(h + H - dh, H))]
                remote(
                    place,
                    place,
                    c_send.at[du - 1, dh, dz],
                    c_recv.at[du - 1, dh, dz],
                    {"sub": u},
                ).wait_recv()
            normalize_piece(u_, s_)

    load_q.wait()
    first = lax.broadcasted_iota(jnp.int32, (rows, rows), 0)
    second = lax.broadcasted_iota(jnp.int32, (rows, rows), 1)
    together = lax.rem(first, cols) == lax.rem(second, cols)
    for head in range(heads):
        base = head * 3 * head_dim
        triple = nt_dot(wq[base : base + 3 * head_dim, :], normed[...]).astype(jnp.bfloat16)
        queries = triple[:head_dim]
        keys = triple[head_dim : 2 * head_dim]
        values = triple[2 * head_dim :]
        scores = jnp.where(together, tn_dot(keys, queries) * head_dim ** (-0.5), -1e30)
        weights = jnp.exp(scores - jnp.max(scores, axis=0, keepdims=True))
        total = jnp.sum(weights, axis=0, keepdims=True)
        out = jnp.dot(values, weights.astype(jnp.bfloat16), preferred_element_type=jnp.float32)
        mixed[head * head_dim : (head + 1) * head_dim, :] = (out / total).astype(jnp.bfloat16)

    load_o.wait()
    for du in range(1, U):
        u_ = lax.rem(u + du, U)
        block = mixed[:, at(u_ * unit, unit)]
        part_send[du - 1] = tn_dot(block, wo[...]).astype(jnp.bfloat16)
        for s_ in range(S):
            send(
                part_send.at[du - 1, piece(s_)],
                part_recv.at[du - 1, piece(s_)],
                d_send.at[du - 1, s_],
                d_recv.at[du - 1, s_],
                {"sub": u_},
            )
    part_own[...] = tn_dot(mixed[:, at(u * unit, unit)], wo[...])

    for s_ in range(S):
        place = piece(s_)
        value = part_own[place, :]
        for du in range(1, U):
            landed = part_recv.at[du - 1, place]
            remote(
                landed, landed, d_send.at[du - 1, s_], d_recv.at[du - 1, s_], {"sub": u}
            ).wait_recv()
            value = value + part_recv[du - 1, place, :].astype(jnp.float32)
        part_own[place, :] = value
        head_send[place, :] = value.astype(jnp.bfloat16)
        for dh in range(1, H):
            send(
                head_send.at[place],
                head_recv.at[dh - 1, place],
                e_send.at[dh - 1, s_],
                e_recv.at[dh - 1, s_],
                {"head": lax.rem(h + dh, H)},
            )

    for s_ in range(S):
        place = piece(s_)
        whole = at(u * unit + s_ * chunk, chunk)
        value = part_own[place, :]
        for dh in range(1, H):
            landed = head_recv.at[dh - 1, place]
            remote(
                landed, landed, e_send.at[dh - 1, s_], e_recv.at[dh - 1, s_], {"head": h}
            ).wait_recv()
            value = value + head_recv[dh - 1, place, :].astype(jnp.float32)
        value = (tokens[whole, :].astype(jnp.float32) + value).astype(jnp.bfloat16)
        hidden[place, :] = value
        vit[whole, :] = scale(value, vit_gain)
        for du in range(1, U):
            send(
                vit.at[whole],
                vit.at[whole],
                v_send.at[du - 1, s_],
                v_recv.at[du - 1, s_],
                {"sub": lax.rem(u + du, U)},
            )
        own = hidden.at[at((s_ * H + h) * cols)]

        @pl.when(s_ != s)
        def _():
            slot = lax.rem(s_ - s + S, S) - 1
            remote(
                own, hidden_out.at[at(s * cols)], o_send.at[slot], o_recv.at[slot], {"seq": s_}
            ).start()

        @pl.when(s_ == s)
        def _():
            pltpu.make_async_copy(own, hidden_out.at[at(s * cols)], local_sem.at[4]).start()

    load_p.wait()
    for du in range(U):
        u_ = lax.rem(u + U - du, U)
        if du:
            for s_ in range(S):
                whole = vit.at[at(u_ * unit + s_ * chunk, chunk)]
                remote(
                    whole, whole, v_send.at[du - 1, s_], v_recv.at[du - 1, s_], {"sub": u}
                ).wait_recv()
        block = vit[at(u_ * unit, unit), :]
        for side in range(2):
            pair[side, u_] = jnp.dot(block, wp[side], preferred_element_type=jnp.float32)

    def gelu(x):
        return 0.5 * x * (1.0 + lax.erf(x * 0.5**0.5))

    pooled = []
    for u_ in range(U):
        if u_ + 1 < U:
            active = gelu(pair[0, u_] + pair[1, u_ + 1])
        else:
            active = gelu(pair[0, u_, : unit - cols] + pair[1, 0, cols:])
            active = jnp.concatenate([active, jnp.zeros((cols, out_width), jnp.float32)], axis=0)
        pooled.append(jnp.sum(active.reshape(unit // cols, cols, out_width), axis=1))
    pooled = jnp.concatenate(pooled, axis=0) * (rolls / (cols * S))
    scored[me, :actions_n, :N] = nt_dot(w_act[...], pooled, precision=lax.Precision.HIGHEST)

    for step in range(1, N):
        other = lax.rem(me + step, N)
        where = {"seq": other // (H * U), "head": other // U % H, "sub": other % U}
        send(scored.at[me], scored.at[me], q_send.at[step - 1], q_recv.at[step - 1], where)

    for dz in range(1, S):
        s_ = lax.rem(s + dz, S)
        remote(
            hidden.at[at((s_ * H + h) * cols)],
            hidden_out.at[at(s_ * cols)],
            o_send.at[dz - 1],
            o_recv.at[dz - 1],
            {"seq": s},
        ).wait_send()
        from_ = lax.rem(s + S - dz, S)
        remote(
            hidden.at[at((s_ * H + h) * cols)],
            hidden_out.at[at(from_ * cols)],
            o_send.at[dz - 1],
            o_recv.at[dz - 1],
            {"seq": s},
        ).wait_recv()
    pltpu.make_async_copy(
        hidden.at[at((s * H + h) * cols)], hidden_out.at[at(s * cols)], local_sem.at[4]
    ).wait()

    for step in range(1, N):
        other = lax.rem(me + N - step, N)
        place = scored.at[other]
        remote(
            place, place, q_send.at[step - 1], q_recv.at[step - 1], {"seq": s}
        ).wait_recv()

    order = lax.broadcasted_iota(jnp.int32, (N, picks), 0)
    frame = lax.rem(order, S * H) * U + order // (S * H)
    share = N // rolls
    for roll in range(rolls):
        total = scored[roll * share, :actions_n, :N]
        for index in range(1, share):
            total = total + scored[roll * share + index, :actions_n, :N]
        chosen = (frame == pair_frames[roll : roll + 1, :]).astype(jnp.float32)
        actions_out[:, roll, :] = jnp.dot(
            total, chosen, preferred_element_type=jnp.float32, precision=lax.Precision.HIGHEST
        )

    for copy in sent:
        copy.wait_send()


def shards(frames_in, attn_gain, w_qkv, w_out, vit_gain, w_pair, w_act, pair_frames):
    S, H, U = lax.axis_size("seq"), lax.axis_size("head"), lax.axis_size("sub")
    N = S * H * U
    rows_own, width = frames_in.shape
    heads = w_qkv.shape[1]
    head_dim = w_qkv.shape[2] // 3
    out_width = w_pair.shape[2]
    actions_n = w_act.shape[1]
    rolls, picks = pair_frames.shape
    cols = rows_own // S
    if N != F or rows_own % S or cols % 16 or S % rolls or (H * rows_own) % 128:
        return shards_by_frame(
            frames_in, attn_gain, w_qkv, w_out, vit_gain, w_pair, w_act, pair_frames
        )
    rows = N * cols
    unit = rows // U
    bf16, f32 = jnp.bfloat16, jnp.float32
    vmem = pl.BlockSpec(memory_space=pltpu.VMEM)
    anywhere = pl.BlockSpec(memory_space=pl.ANY)
    dma = pltpu.SemaphoreType.DMA
    hidden, actions = pl.pallas_call(
        functools.partial(fused_kernel, (S, H, U, heads, head_dim)),
        out_shape=(
            jax.ShapeDtypeStruct((rows_own, width), bf16),
            jax.ShapeDtypeStruct((actions_n, rolls, picks), f32),
        ),
        in_specs=[anywhere, vmem, anywhere, anywhere, vmem, anywhere, vmem, vmem],
        out_specs=(anywhere, vmem),
        scratch_shapes=[
            pltpu.VMEM((rows, width), bf16),
            pltpu.VMEM((rows, width), bf16),
            pltpu.VMEM((heads * 3 * head_dim, width), bf16),
            pltpu.VMEM(w_out.shape, bf16),
            pltpu.VMEM(w_pair.shape, bf16),
            pltpu.VMEM((heads * head_dim, rows), bf16),
            pltpu.VMEM((U - 1, unit, width), bf16),
            pltpu.VMEM((U - 1, unit, width), bf16),
            pltpu.VMEM((unit, width), f32),
            pltpu.VMEM((unit, width), bf16),
            pltpu.VMEM((H - 1, unit, width), bf16),
            pltpu.VMEM((unit, width), bf16),
            pltpu.VMEM((rows, width), bf16),
            pltpu.VMEM((2, U, unit, out_width), f32),
            pltpu.VMEM((N, -(-actions_n // 8) * 8, -(-N // 128) * 128), f32),
            dma((5,)),
            dma((S - 1,)),
            dma((S - 1,)),
            dma((H - 1, S)),
            dma((H - 1, S)),
            dma((U - 1, H, S)),
            dma((U - 1, H, S)),
            dma((U - 1, S)),
            dma((U - 1, S)),
            dma((H - 1, S)),
            dma((H - 1, S)),
            dma((U - 1, S)),
            dma((U - 1, S)),
            dma((S - 1,)),
            dma((S - 1,)),
            dma((N - 1,)),
            dma((N - 1,)),
        ],
        compiler_params=pltpu.CompilerParams(
            collective_id=0, has_side_effects=True, vmem_limit_bytes=48 * 1024 * 1024
        ),
    )(
        frames_in,
        attn_gain.reshape(1, width),
        jnp.transpose(w_qkv, (1, 2, 0)).reshape(heads * 3 * head_dim, width),
        w_out,
        vit_gain.reshape(1, width),
        w_pair,
        jnp.transpose(w_act, (1, 0)),
        pair_frames,
    )
    return (hidden, jnp.transpose(actions, (1, 2, 0)))


def solution(mesh):
    in_specs = (
        P(("groups", "seq", "head", "sub"), None),
        P(),
        P(None, ("head", "sub"), None),
        P(("head", "sub"), None),
        P(),
        P(None, None, ("head", "sub")),
        P(("head", "sub"), None),
        P("groups", None),
    )
    out_specs = (P(("groups", "seq", "head", "sub"), None), P("groups", None, None))
    return jax.shard_map(shards, mesh=mesh, in_specs=in_specs, out_specs=out_specs, check_vma=False)
```

```python
import functools
import jax
import jax.numpy as jnp
from jax import lax
from jax.experimental import pallas as pl
from jax.experimental.pallas import tpu as pltpu
from jax.sharding import PartitionSpec as P

F = 16
ROLLS = 2


def from_behind(value, axis, steps):
    count = lax.axis_size(axis)
    leading, last = (max(0, -steps), min(count, count - steps))
    return lax.ppermute(value, axis, [(source, source + steps) for source in range(leading, last)])


def normalize(values_in, gain_vec):
    floats = values_in.astype(jnp.float32)
    mean_sq = jnp.mean(floats * floats, axis=-1, keepdims=True)
    return (floats * lax.rsqrt(mean_sq + 1e-06) * gain_vec).astype(jnp.bfloat16)


def shards_by_frame(frames_in, attn_gain, w_qkv, w_out, vit_gain, w_pair, w_act, pair_frames):
    rows_own = frames_in.shape[0]
    model_width = frames_in.shape[1]
    seq_count = lax.axis_size("seq")
    split_count = lax.axis_size(("head", "sub"))
    block_rows = rows_own * split_count
    total_cols = block_rows * seq_count // F
    frames_local = max(1, F // seq_count)
    cols_local = block_rows // frames_local
    frame_step = max(1, seq_count // F)
    heads_local = w_qkv.shape[1]
    triple_dim = w_qkv.shape[2]
    head_dim = triple_dim // 3
    qkv_matrix = w_qkv.reshape(model_width, heads_local * triple_dim)
    normed = lax.all_gather(normalize(frames_in, attn_gain), ("head", "sub"), axis=0, tiled=True)
    qkv_rows = jnp.dot(normed, qkv_matrix, preferred_element_type=jnp.float32).astype(jnp.bfloat16)
    qkv_rows = qkv_rows.reshape(
        frames_local, seq_count, cols_local // seq_count, heads_local, triple_dim
    )
    columns = lax.all_to_all(qkv_rows, "seq", split_axis=1, concat_axis=0, tiled=True)
    item_count = columns.shape[2]
    by_frame = columns.reshape(F, -1, heads_local, triple_dim)
    queries = by_frame[..., :head_dim]
    key_part = by_frame[..., head_dim : 2 * head_dim]
    value_part = by_frame[..., 2 * head_dim :]
    scores = jnp.einsum(
        "fchd,gchd->chfg", queries, key_part, preferred_element_type=jnp.float32
    ) * head_dim ** (-0.5)
    row_peak = jnp.max(scores, axis=-1, keepdims=True)
    weights = jnp.exp(scores - row_peak)
    weights = (weights / jnp.sum(weights, axis=-1, keepdims=True)).astype(jnp.bfloat16)
    mixed_out = jnp.einsum(
        "chfg,gchd->fchd", weights, value_part, preferred_element_type=jnp.float32
    ).astype(jnp.bfloat16)
    mixed_out = mixed_out.reshape(seq_count * frames_local, 1, item_count, heads_local * head_dim)
    attended = lax.all_to_all(mixed_out, "seq", split_axis=0, concat_axis=1, tiled=True)
    attended = attended.reshape(block_rows, heads_local * head_dim)
    branch_sum = lax.psum_scatter(
        jnp.dot(attended, w_out, preferred_element_type=jnp.float32).astype(jnp.bfloat16),
        ("head", "sub"),
        scatter_dimension=0,
        tiled=True,
    ).astype(jnp.float32)
    hidden = (frames_in.astype(jnp.float32) + branch_sum).astype(jnp.bfloat16)
    vit_own = normalize(hidden, vit_gain)
    vit_rows = lax.all_gather(vit_own, ("head", "sub"), axis=0, tiled=True)
    current = jnp.dot(vit_rows, w_pair[0], preferred_element_type=jnp.float32)
    ahead_proj = jnp.dot(vit_rows, w_pair[1], preferred_element_type=jnp.float32)
    ahead_proj = ahead_proj.reshape(frames_local, cols_local, -1)
    arrived = from_behind(ahead_proj[:1].astype(jnp.bfloat16), "seq", -frame_step).astype(
        jnp.float32
    )
    following = jnp.concatenate([ahead_proj[1:], arrived], axis=0).reshape(block_rows, -1)
    embedded = current + following
    activated = jax.nn.gelu(embedded, approximate=False).reshape(frames_local, cols_local, -1)
    seq_index = lax.axis_index("seq")
    first_token = seq_index * block_rows
    frame_first = first_token // total_cols
    col_first = first_token % total_cols
    patches = total_cols // ROLLS
    roll_ids = (col_first + jnp.arange(cols_local, dtype=jnp.int32)) // patches
    member = (roll_ids[None, :] == jnp.arange(ROLLS, dtype=jnp.int32)[:, None]).astype(
        jnp.float32
    ) / patches
    pooled = jnp.einsum("rp,fpe->fre", member, activated, precision=lax.Precision.HIGHEST)
    scored = jnp.einsum("fre,ea->fra", pooled, w_act, precision=lax.Precision.HIGHEST)
    frame_ids = frame_first + jnp.arange(frames_local, dtype=jnp.int32)
    selector = (pair_frames[:, :, None] == frame_ids[None, None, :]).astype(jnp.float32)
    partial_value = jnp.einsum("rjf,fra->rja", selector, scored, precision=lax.Precision.HIGHEST)
    actions = lax.psum(partial_value, ("seq", "head", "sub"))
    return (hidden, actions)


def nt_dot(lhs, rhs, **kw):
    return lax.dot_general(
        lhs, rhs, (((1,), (1,)), ((), ())), preferred_element_type=jnp.float32, **kw
    )


def tn_dot(lhs, rhs):
    return lax.dot_general(
        lhs, rhs, (((0,), (0,)), ((), ())), preferred_element_type=jnp.float32
    )


def fused_kernel(
    sizes,
    frames,
    attn_gain_in,
    w_qkv,
    w_out,
    vit_gain_in,
    w_pair,
    w_act_in,
    pair_frames_in,
    hidden_out,
    actions_out,
    attn_gain,
    vit_gain,
    w_act,
    pair_frames,
    tokens,
    normed,
    wq,
    wo,
    wp,
    mixed,
    part_send,
    part_recv,
    part_own,
    head_send,
    head_recv,
    hidden,
    vit,
    pair,
    scored,
    local_sem,
    a_send,
    a_recv,
    b_send,
    b_recv,
    c_send,
    c_recv,
    d_send,
    d_recv,
    e_send,
    e_recv,
    v_send,
    v_recv,
    o_send,
    o_recv,
    q_send,
    q_recv,
):
    S, H, U, heads, head_dim = sizes
    N = S * H * U
    rows, width = tokens.shape
    cols = rows // N
    unit = rows // U
    chunk = H * cols
    actions_n, rolls, picks = actions_out.shape
    out_width = wp.shape[2]
    s, h, u = lax.axis_index("seq"), lax.axis_index("head"), lax.axis_index("sub")
    me = (s * H + h) * U + u

    def at(value, size=cols):
        return pl.ds(pl.multiple_of(value, size), size)

    def slab(u_, s_, h_):
        return at(((u_ * S + s_) * H + h_) * cols)

    def piece(s_):
        return at(s_ * chunk, chunk)

    def remote(source, target, send, recv, where):
        return pltpu.make_async_remote_copy(
            src_ref=source,
            dst_ref=target,
            send_sem=send,
            recv_sem=recv,
            device_id=where,
            device_id_type=pl.DeviceIdType.MESH,
        )

    sent = []

    def send(*args):
        copy = remote(*args)
        copy.start()
        sent.append(copy)

    load_q = pltpu.make_async_copy(w_qkv, wq, local_sem.at[0])
    load_o = pltpu.make_async_copy(w_out, wo, local_sem.at[1])
    load_p = pltpu.make_async_copy(w_pair, wp, local_sem.at[2])
    load_own = pltpu.make_async_copy(
        frames.at[at(s * cols)], tokens.at[slab(u, s, h)], local_sem.at[3]
    )
    small = [
        pltpu.make_async_copy(source, target, local_sem.at[5 + index])
        for index, (source, target) in enumerate(
            (
                (attn_gain_in, attn_gain),
                (vit_gain_in, vit_gain),
                (w_act_in, w_act),
                (pair_frames_in, pair_frames),
            )
        )
    ]
    load_own.start()
    for load in small:
        load.start()
    load_q.start()
    load_o.start()
    load_p.start()

    barrier = pltpu.get_barrier_semaphore()

    def greet(step, carry):
        other = lax.rem(me + step, N)
        where = {"seq": other // (H * U), "head": other // U % H, "sub": other % U}
        pl.semaphore_signal(
            barrier, inc=1, device_id=where, device_id_type=pl.DeviceIdType.MESH
        )
        return carry

    lax.fori_loop(1, N, greet, 0)
    pl.semaphore_wait(barrier, N - 1)

    steps = sorted(range(S), key=lambda d: min(d, S - d))

    for dz in reversed(steps[1:]):
        t = lax.rem(s + dz, S)
        send(
            frames.at[at(t * cols)],
            tokens.at[slab(u, s, h)],
            a_send.at[dz - 1],
            a_recv.at[dz - 1],
            {"seq": t},
        )

    def to_heads(dz):
        s_ = lax.rem(s + S - dz, S)
        place = tokens.at[slab(u, s_, h)]
        for dh in range(1, H):
            send(
                place,
                place,
                b_send.at[dh - 1, dz],
                b_recv.at[dh - 1, dz],
                {"head": lax.rem(h + dh, H)},
            )
        to_subs(0, dz)

    def to_subs(dh, dz):
        place = tokens.at[slab(u, lax.rem(s + S - dz, S), lax.rem(h + H - dh, H))]
        for du in range(1, U):
            send(
                place,
                place,
                c_send.at[du - 1, dh, dz],
                c_recv.at[du - 1, dh, dz],
                {"sub": lax.rem(u + du, U)},
            )

    def from_heads(dz):
        s_ = lax.rem(s + S - dz, S)
        for dh in range(1, H):
            place = tokens.at[slab(u, s_, lax.rem(h + H - dh, H))]
            remote(
                place, place, b_send.at[dh - 1, dz], b_recv.at[dh - 1, dz], {"head": h}
            ).wait_recv()
            to_subs(dh, dz)

    def scale(values, gain):
        floats = values.astype(jnp.float32)
        mean_sq = jnp.mean(floats * floats, axis=-1, keepdims=True)
        return (floats * lax.rsqrt(mean_sq + 1e-06) * gain[...][None, :]).astype(jnp.bfloat16)

    def normalize_piece(u_, s_):
        place = at((u_ * S + s_) * chunk, chunk)
        normed[place, :] = scale(tokens[place, :], attn_gain)

    load_own.wait()
    to_heads(0)
    for load in small:
        load.wait()
    for index, dz in enumerate(steps):
        if index + 1 < S:
            ahead = steps[index + 1]
            place = tokens.at[slab(u, lax.rem(s + S - ahead, S), h)]
            remote(
                place, place, a_send.at[ahead - 1], a_recv.at[ahead - 1], {"seq": s}
            ).wait_recv()
            to_heads(ahead)
        from_heads(dz)
        normalize_piece(u, lax.rem(s + S - dz, S))
    for dz in steps:
        s_ = lax.rem(s + S - dz, S)
        for du in range(1, U):
            u_ = lax.rem(u + U - du, U)
            for dh in range(H):
                place = tokens.at[slab(u_, s_, lax.rem(h + H - dh, H))]
                remote(
                    place,
                    place,
                    c_send.at[du - 1, dh, dz],
                    c_recv.at[du - 1, dh, dz],
                    {"sub": u},
                ).wait_recv()
            normalize_piece(u_, s_)

    load_q.wait()
    first = lax.broadcasted_iota(jnp.int32, (rows, rows), 0)
    second = lax.broadcasted_iota(jnp.int32, (rows, rows), 1)
    together = lax.rem(first, cols) == lax.rem(second, cols)
    for head in range(heads):
        base = head * 3 * head_dim
        triple = nt_dot(wq[base : base + 3 * head_dim, :], normed[...]).astype(jnp.bfloat16)
        queries = triple[:head_dim]
        keys = triple[head_dim : 2 * head_dim]
        values = triple[2 * head_dim :]
        scores = jnp.where(together, tn_dot(keys, queries) * head_dim ** (-0.5), -1e30)
        weights = jnp.exp(scores - jnp.max(scores, axis=0, keepdims=True))
        total = jnp.sum(weights, axis=0, keepdims=True)
        out = jnp.dot(values, weights.astype(jnp.bfloat16), preferred_element_type=jnp.float32)
        mixed[head * head_dim : (head + 1) * head_dim, :] = (out / total).astype(jnp.bfloat16)

    load_o.wait()
    for du in range(1, U):
        u_ = lax.rem(u + du, U)
        block = mixed[:, at(u_ * unit, unit)]
        part_send[du - 1] = tn_dot(block, wo[...]).astype(jnp.bfloat16)
        for s_ in range(S):
            send(
                part_send.at[du - 1, piece(s_)],
                part_recv.at[du - 1, piece(s_)],
                d_send.at[du - 1, s_],
                d_recv.at[du - 1, s_],
                {"sub": u_},
            )
    part_own[...] = tn_dot(mixed[:, at(u * unit, unit)], wo[...])

    for s_ in range(S):
        place = piece(s_)
        value = part_own[place, :]
        for du in range(1, U):
            landed = part_recv.at[du - 1, place]
            remote(
                landed, landed, d_send.at[du - 1, s_], d_recv.at[du - 1, s_], {"sub": u}
            ).wait_recv()
            value = value + part_recv[du - 1, place, :].astype(jnp.float32)
        part_own[place, :] = value
        head_send[place, :] = value.astype(jnp.bfloat16)
        for dh in range(1, H):
            send(
                head_send.at[place],
                head_recv.at[dh - 1, place],
                e_send.at[dh - 1, s_],
                e_recv.at[dh - 1, s_],
                {"head": lax.rem(h + dh, H)},
            )

    for s_ in range(S):
        place = piece(s_)
        whole = at(u * unit + s_ * chunk, chunk)
        value = part_own[place, :]
        for dh in range(1, H):
            landed = head_recv.at[dh - 1, place]
            remote(
                landed, landed, e_send.at[dh - 1, s_], e_recv.at[dh - 1, s_], {"head": h}
            ).wait_recv()
            value = value + head_recv[dh - 1, place, :].astype(jnp.float32)
        value = (tokens[whole, :].astype(jnp.float32) + value).astype(jnp.bfloat16)
        hidden[place, :] = value
        vit[whole, :] = scale(value, vit_gain)
        for du in range(1, U):
            send(
                vit.at[whole],
                vit.at[whole],
                v_send.at[du - 1, s_],
                v_recv.at[du - 1, s_],
                {"sub": lax.rem(u + du, U)},
            )
        own = hidden.at[at((s_ * H + h) * cols)]

        @pl.when(s_ != s)
        def _():
            slot = lax.rem(s_ - s + S, S) - 1
            remote(
                own, hidden_out.at[at(s * cols)], o_send.at[slot], o_recv.at[slot], {"seq": s_}
            ).start()

        @pl.when(s_ == s)
        def _():
            pltpu.make_async_copy(own, hidden_out.at[at(s * cols)], local_sem.at[4]).start()

    load_p.wait()
    for du in range(U):
        u_ = lax.rem(u + U - du, U)
        if du:
            for s_ in range(S):
                whole = vit.at[at(u_ * unit + s_ * chunk, chunk)]
                remote(
                    whole, whole, v_send.at[du - 1, s_], v_recv.at[du - 1, s_], {"sub": u}
                ).wait_recv()
        block = vit[at(u_ * unit, unit), :]
        for side in range(2):
            pair[side, u_] = jnp.dot(block, wp[side], preferred_element_type=jnp.float32)

    def gelu(x):
        return 0.5 * x * (1.0 + lax.erf(x * 0.5**0.5))

    pooled = []
    for u_ in range(U):
        if u_ + 1 < U:
            active = gelu(pair[0, u_] + pair[1, u_ + 1])
        else:
            active = gelu(pair[0, u_, : unit - cols] + pair[1, 0, cols:])
            active = jnp.concatenate([active, jnp.zeros((cols, out_width), jnp.float32)], axis=0)
        pooled.append(jnp.sum(active.reshape(unit // cols, cols, out_width), axis=1))
    pooled = jnp.concatenate(pooled, axis=0) * (rolls / (cols * S))
    scored[me, :actions_n, :N] = nt_dot(w_act[...], pooled, precision=lax.Precision.HIGHEST)

    for step in range(1, N):
        other = lax.rem(me + step, N)
        where = {"seq": other // (H * U), "head": other // U % H, "sub": other % U}
        send(scored.at[me], scored.at[me], q_send.at[step - 1], q_recv.at[step - 1], where)

    for dz in range(1, S):
        s_ = lax.rem(s + dz, S)
        remote(
            hidden.at[at((s_ * H + h) * cols)],
            hidden_out.at[at(s_ * cols)],
            o_send.at[dz - 1],
            o_recv.at[dz - 1],
            {"seq": s},
        ).wait_send()
        from_ = lax.rem(s + S - dz, S)
        remote(
            hidden.at[at((s_ * H + h) * cols)],
            hidden_out.at[at(from_ * cols)],
            o_send.at[dz - 1],
            o_recv.at[dz - 1],
            {"seq": s},
        ).wait_recv()
    pltpu.make_async_copy(
        hidden.at[at((s * H + h) * cols)], hidden_out.at[at(s * cols)], local_sem.at[4]
    ).wait()

    for step in range(1, N):
        other = lax.rem(me + N - step, N)
        place = scored.at[other]
        remote(
            place, place, q_send.at[step - 1], q_recv.at[step - 1], {"seq": s}
        ).wait_recv()

    order = lax.broadcasted_iota(jnp.int32, (N, picks), 0)
    frame = lax.rem(order, S * H) * U + order // (S * H)
    share = N // rolls
    for roll in range(rolls):
        total = scored[roll * share, :actions_n, :N]
        for index in range(1, share):
            total = total + scored[roll * share + index, :actions_n, :N]
        chosen = (frame == pair_frames[roll : roll + 1, :]).astype(jnp.float32)
        actions_out[:, roll, :] = jnp.dot(
            total, chosen, preferred_element_type=jnp.float32, precision=lax.Precision.HIGHEST
        )

    for copy in sent:
        copy.wait_send()


def shards(frames_in, attn_gain, w_qkv, w_out, vit_gain, w_pair, w_act, pair_frames):
    S, H, U = lax.axis_size("seq"), lax.axis_size("head"), lax.axis_size("sub")
    N = S * H * U
    rows_own, width = frames_in.shape
    heads = w_qkv.shape[1]
    head_dim = w_qkv.shape[2] // 3
    out_width = w_pair.shape[2]
    actions_n = w_act.shape[1]
    rolls, picks = pair_frames.shape
    cols = rows_own // S
    if N != F or rows_own % S or cols % 16 or S % rolls or (H * rows_own) % 128:
        return shards_by_frame(
            frames_in, attn_gain, w_qkv, w_out, vit_gain, w_pair, w_act, pair_frames
        )
    rows = N * cols
    unit = rows // U
    bf16, f32 = jnp.bfloat16, jnp.float32
    vmem = pl.BlockSpec(memory_space=pltpu.VMEM)
    anywhere = pl.BlockSpec(memory_space=pl.ANY)
    dma = pltpu.SemaphoreType.DMA
    hidden, actions = pl.pallas_call(
        functools.partial(fused_kernel, (S, H, U, heads, head_dim)),
        out_shape=(
            jax.ShapeDtypeStruct((rows_own, width), bf16),
            jax.ShapeDtypeStruct((actions_n, rolls, picks), f32),
        ),
        in_specs=[anywhere] * 8,
        out_specs=(anywhere, vmem),
        scratch_shapes=[
            pltpu.VMEM((width,), f32),
            pltpu.VMEM((width,), f32),
            pltpu.VMEM((actions_n, out_width), f32),
            pltpu.VMEM((rolls, picks), jnp.int32),
            pltpu.VMEM((rows, width), bf16),
            pltpu.VMEM((rows, width), bf16),
            pltpu.VMEM((heads * 3 * head_dim, width), bf16),
            pltpu.VMEM(w_out.shape, bf16),
            pltpu.VMEM(w_pair.shape, bf16),
            pltpu.VMEM((heads * head_dim, rows), bf16),
            pltpu.VMEM((U - 1, unit, width), bf16),
            pltpu.VMEM((U - 1, unit, width), bf16),
            pltpu.VMEM((unit, width), f32),
            pltpu.VMEM((unit, width), bf16),
            pltpu.VMEM((H - 1, unit, width), bf16),
            pltpu.VMEM((unit, width), bf16),
            pltpu.VMEM((rows, width), bf16),
            pltpu.VMEM((2, U, unit, out_width), f32),
            pltpu.VMEM((N, -(-actions_n // 8) * 8, -(-N // 128) * 128), f32),
            dma((9,)),
            dma((S - 1,)),
            dma((S - 1,)),
            dma((H - 1, S)),
            dma((H - 1, S)),
            dma((U - 1, H, S)),
            dma((U - 1, H, S)),
            dma((U - 1, S)),
            dma((U - 1, S)),
            dma((H - 1, S)),
            dma((H - 1, S)),
            dma((U - 1, S)),
            dma((U - 1, S)),
            dma((S - 1,)),
            dma((S - 1,)),
            dma((N - 1,)),
            dma((N - 1,)),
        ],
        compiler_params=pltpu.CompilerParams(
            collective_id=0, has_side_effects=True, vmem_limit_bytes=60 * 1024 * 1024
        ),
    )(
        frames_in,
        attn_gain,
        jnp.transpose(w_qkv, (1, 2, 0)).reshape(heads * 3 * head_dim, width),
        w_out,
        vit_gain,
        w_pair,
        jnp.transpose(w_act, (1, 0)),
        pair_frames,
    )
    return (hidden, jnp.transpose(actions, (1, 2, 0)))


def solution(mesh):
    in_specs = (
        P(("groups", "seq", "head", "sub"), None),
        P(),
        P(None, ("head", "sub"), None),
        P(("head", "sub"), None),
        P(),
        P(None, None, ("head", "sub")),
        P(("head", "sub"), None),
        P("groups", None),
    )
    out_specs = (P(("groups", "seq", "head", "sub"), None), P("groups", None, None))
    return jax.shard_map(shards, mesh=mesh, in_specs=in_specs, out_specs=out_specs, check_vma=False)
```

```python
import functools
import jax
import jax.numpy as jnp
from jax import lax
from jax.experimental import pallas as pl
from jax.experimental.pallas import tpu as pltpu
from jax.sharding import PartitionSpec as P

F = 16
ROLLS = 2


def from_behind(value, axis, steps):
    count = lax.axis_size(axis)
    leading, last = (max(0, -steps), min(count, count - steps))
    return lax.ppermute(value, axis, [(source, source + steps) for source in range(leading, last)])


def normalize(values_in, gain_vec):
    floats = values_in.astype(jnp.float32)
    mean_sq = jnp.mean(floats * floats, axis=-1, keepdims=True)
    return (floats * lax.rsqrt(mean_sq + 1e-06) * gain_vec).astype(jnp.bfloat16)


def shards_by_frame(frames_in, attn_gain, w_qkv, w_out, vit_gain, w_pair, w_act, pair_frames):
    rows_own = frames_in.shape[0]
    model_width = frames_in.shape[1]
    seq_count = lax.axis_size("seq")
    split_count = lax.axis_size(("head", "sub"))
    block_rows = rows_own * split_count
    total_cols = block_rows * seq_count // F
    frames_local = max(1, F // seq_count)
    cols_local = block_rows // frames_local
    frame_step = max(1, seq_count // F)
    heads_local = w_qkv.shape[1]
    triple_dim = w_qkv.shape[2]
    head_dim = triple_dim // 3
    qkv_matrix = w_qkv.reshape(model_width, heads_local * triple_dim)
    normed = lax.all_gather(normalize(frames_in, attn_gain), ("head", "sub"), axis=0, tiled=True)
    qkv_rows = jnp.dot(normed, qkv_matrix, preferred_element_type=jnp.float32).astype(jnp.bfloat16)
    qkv_rows = qkv_rows.reshape(
        frames_local, seq_count, cols_local // seq_count, heads_local, triple_dim
    )
    columns = lax.all_to_all(qkv_rows, "seq", split_axis=1, concat_axis=0, tiled=True)
    item_count = columns.shape[2]
    by_frame = columns.reshape(F, -1, heads_local, triple_dim)
    queries = by_frame[..., :head_dim]
    key_part = by_frame[..., head_dim : 2 * head_dim]
    value_part = by_frame[..., 2 * head_dim :]
    scores = jnp.einsum(
        "fchd,gchd->chfg", queries, key_part, preferred_element_type=jnp.float32
    ) * head_dim ** (-0.5)
    row_peak = jnp.max(scores, axis=-1, keepdims=True)
    weights = jnp.exp(scores - row_peak)
    weights = (weights / jnp.sum(weights, axis=-1, keepdims=True)).astype(jnp.bfloat16)
    mixed_out = jnp.einsum(
        "chfg,gchd->fchd", weights, value_part, preferred_element_type=jnp.float32
    ).astype(jnp.bfloat16)
    mixed_out = mixed_out.reshape(seq_count * frames_local, 1, item_count, heads_local * head_dim)
    attended = lax.all_to_all(mixed_out, "seq", split_axis=0, concat_axis=1, tiled=True)
    attended = attended.reshape(block_rows, heads_local * head_dim)
    branch_sum = lax.psum_scatter(
        jnp.dot(attended, w_out, preferred_element_type=jnp.float32).astype(jnp.bfloat16),
        ("head", "sub"),
        scatter_dimension=0,
        tiled=True,
    ).astype(jnp.float32)
    hidden = (frames_in.astype(jnp.float32) + branch_sum).astype(jnp.bfloat16)
    vit_own = normalize(hidden, vit_gain)
    vit_rows = lax.all_gather(vit_own, ("head", "sub"), axis=0, tiled=True)
    current = jnp.dot(vit_rows, w_pair[0], preferred_element_type=jnp.float32)
    ahead_proj = jnp.dot(vit_rows, w_pair[1], preferred_element_type=jnp.float32)
    ahead_proj = ahead_proj.reshape(frames_local, cols_local, -1)
    arrived = from_behind(ahead_proj[:1].astype(jnp.bfloat16), "seq", -frame_step).astype(
        jnp.float32
    )
    following = jnp.concatenate([ahead_proj[1:], arrived], axis=0).reshape(block_rows, -1)
    embedded = current + following
    activated = jax.nn.gelu(embedded, approximate=False).reshape(frames_local, cols_local, -1)
    seq_index = lax.axis_index("seq")
    first_token = seq_index * block_rows
    frame_first = first_token // total_cols
    col_first = first_token % total_cols
    patches = total_cols // ROLLS
    roll_ids = (col_first + jnp.arange(cols_local, dtype=jnp.int32)) // patches
    member = (roll_ids[None, :] == jnp.arange(ROLLS, dtype=jnp.int32)[:, None]).astype(
        jnp.float32
    ) / patches
    pooled = jnp.einsum("rp,fpe->fre", member, activated, precision=lax.Precision.HIGHEST)
    scored = jnp.einsum("fre,ea->fra", pooled, w_act, precision=lax.Precision.HIGHEST)
    frame_ids = frame_first + jnp.arange(frames_local, dtype=jnp.int32)
    selector = (pair_frames[:, :, None] == frame_ids[None, None, :]).astype(jnp.float32)
    partial_value = jnp.einsum("rjf,fra->rja", selector, scored, precision=lax.Precision.HIGHEST)
    actions = lax.psum(partial_value, ("seq", "head", "sub"))
    return (hidden, actions)


HALVES = 2
PIECES = 2


def nt_dot(lhs, rhs, **kw):
    return lax.dot_general(
        lhs, rhs, (((1,), (1,)), ((), ())), preferred_element_type=jnp.float32, **kw
    )


def tn_dot(lhs, rhs):
    return lax.dot_general(
        lhs, rhs, (((0,), (0,)), ((), ())), preferred_element_type=jnp.float32
    )


def fused_kernel(
    sizes,
    frames,
    attn_gain_in,
    w_qkv,
    w_out,
    vit_gain_in,
    w_pair,
    w_act_in,
    pair_frames_in,
    hidden_out,
    actions_out,
    attn_gain,
    vit_gain,
    w_act,
    pair_frames,
    tokens,
    normed,
    wq,
    wo,
    wp,
    qkv,
    mixed,
    branch,
    part_send,
    part_recv,
    part_own,
    head_send,
    head_recv,
    hidden_wide,
    hidden,
    vit,
    scored,
    local_sem,
    a_send,
    a_recv,
    b_send,
    b_recv,
    c_send,
    c_recv,
    d_send,
    d_recv,
    e_send,
    e_recv,
    v_send,
    v_recv,
    o_send,
    o_recv,
    q_send,
    q_recv,
):
    S, H, U, heads, head_dim = sizes
    N = S * H * U
    rows, width = tokens.shape
    cols = rows // N
    unit = rows // U
    chunk = H * cols
    part = cols // HALVES
    half_rows = rows // HALVES
    half_unit = unit // HALVES
    pieces = HALVES * PIECES
    piece_rows = half_unit // PIECES
    piece_seq = S // PIECES
    actions_n, rolls, picks = actions_out.shape
    out_width = wp.shape[2]
    s, h, u = lax.axis_index("seq"), lax.axis_index("head"), lax.axis_index("sub")
    me = (s * H + h) * U + u

    def at(value, size=cols):
        return pl.ds(pl.multiple_of(value, size), size)

    def slab(u_, s_, h_):
        return at(((u_ * S + s_) * H + h_) * cols)

    def piece(p):
        return at(p * piece_rows, piece_rows)

    def vit_piece(u_, p):
        half, index = divmod(p, PIECES)
        start = half * half_rows + u_ * half_unit + index * piece_rows
        return at(start, piece_rows)

    def halved(values, half):
        return values.reshape(-1, HALVES, part, width)[:, half].reshape(-1, width)

    def remote(source, target, send, recv, where):
        return pltpu.make_async_remote_copy(
            src_ref=source,
            dst_ref=target,
            send_sem=send,
            recv_sem=recv,
            device_id=where,
            device_id_type=pl.DeviceIdType.MESH,
        )

    sent = []

    def send(*args):
        copy = remote(*args)
        copy.start()
        sent.append(copy)

    load_q = pltpu.make_async_copy(w_qkv, wq, local_sem.at[0])
    load_o = pltpu.make_async_copy(w_out, wo, local_sem.at[1])
    load_p = pltpu.make_async_copy(w_pair, wp, local_sem.at[2])
    load_own = pltpu.make_async_copy(
        frames.at[at(s * cols)], tokens.at[slab(u, s, h)], local_sem.at[3]
    )
    small = [
        pltpu.make_async_copy(source, target, local_sem.at[5 + index])
        for index, (source, target) in enumerate(
            (
                (attn_gain_in, attn_gain),
                (vit_gain_in, vit_gain),
                (w_act_in, w_act),
                (pair_frames_in, pair_frames),
            )
        )
    ]
    load_own.start()
    for load in small:
        load.start()
    load_q.start()
    load_o.start()
    load_p.start()

    barrier = pltpu.get_barrier_semaphore()

    def greet(step, carry):
        other = lax.rem(me + step, N)
        where = {"seq": other // (H * U), "head": other // U % H, "sub": other % U}
        pl.semaphore_signal(
            barrier, inc=1, device_id=where, device_id_type=pl.DeviceIdType.MESH
        )
        return carry

    lax.fori_loop(1, N, greet, 0)
    pl.semaphore_wait(barrier, N - 1)

    steps = sorted(range(S), key=lambda d: min(d, S - d))

    for dz in reversed(steps[1:]):
        t = lax.rem(s + dz, S)
        send(
            frames.at[at(t * cols)],
            tokens.at[slab(u, s, h)],
            a_send.at[dz - 1],
            a_recv.at[dz - 1],
            {"seq": t},
        )

    def to_heads(dz):
        s_ = lax.rem(s + S - dz, S)
        place = tokens.at[slab(u, s_, h)]
        for dh in range(1, H):
            send(
                place,
                place,
                b_send.at[dh - 1, dz],
                b_recv.at[dh - 1, dz],
                {"head": lax.rem(h + dh, H)},
            )
        to_subs(0, dz)

    def to_subs(dh, dz):
        place = tokens.at[slab(u, lax.rem(s + S - dz, S), lax.rem(h + H - dh, H))]
        for du in range(1, U):
            send(
                place,
                place,
                c_send.at[du - 1, dh, dz],
                c_recv.at[du - 1, dh, dz],
                {"sub": lax.rem(u + du, U)},
            )

    def from_heads(dz):
        s_ = lax.rem(s + S - dz, S)
        for dh in range(1, H):
            place = tokens.at[slab(u, s_, lax.rem(h + H - dh, H))]
            remote(
                place, place, b_send.at[dh - 1, dz], b_recv.at[dh - 1, dz], {"head": h}
            ).wait_recv()
            to_subs(dh, dz)

    def scale(values, gain):
        floats = values.astype(jnp.float32)
        mean_sq = jnp.mean(floats * floats, axis=-1, keepdims=True)
        return floats * lax.rsqrt(mean_sq + 1e-06) * gain[...][None, :]

    def normalize_piece(u_, s_):
        place = at((u_ * S + s_) * chunk, chunk)
        scaled = scale(tokens[place, :], attn_gain)
        for half in range(HALVES):
            target = at(half * half_rows + (u_ * S + s_) * H * part, H * part)
            normed[target, :] = halved(scaled, half).astype(jnp.bfloat16)

    load_own.wait()
    to_heads(0)
    for load in small:
        load.wait()
    for index, dz in enumerate(steps):
        if index + 1 < S:
            ahead = steps[index + 1]
            place = tokens.at[slab(u, lax.rem(s + S - ahead, S), h)]
            remote(
                place, place, a_send.at[ahead - 1], a_recv.at[ahead - 1], {"seq": s}
            ).wait_recv()
            to_heads(ahead)
        from_heads(dz)
        normalize_piece(u, lax.rem(s + S - dz, S))
    for dz in steps:
        s_ = lax.rem(s + S - dz, S)
        for du in range(1, U):
            u_ = lax.rem(u + U - du, U)
            for dh in range(H):
                place = tokens.at[slab(u_, s_, lax.rem(h + H - dh, H))]
                remote(
                    place,
                    place,
                    c_send.at[du - 1, dh, dz],
                    c_recv.at[du - 1, dh, dz],
                    {"sub": u},
                ).wait_recv()
            normalize_piece(u_, s_)

    load_q.wait()
    first = lax.broadcasted_iota(jnp.int32, (half_rows, half_rows), 0)
    second = lax.broadcasted_iota(jnp.int32, (half_rows, half_rows), 1)
    together = lax.rem(first, part) == lax.rem(second, part)

    def project(head):
        base = head * 3 * head_dim
        qkv[base : base + 3 * head_dim, :] = nt_dot(
            wq[base : base + 3 * head_dim, :], normed[...]
        ).astype(jnp.bfloat16)

    def attend(head, half):
        base = head * 3 * head_dim
        lanes = slice(half * half_rows, (half + 1) * half_rows)
        queries = qkv[base : base + head_dim, lanes]
        keys = qkv[base + head_dim : base + 2 * head_dim, lanes]
        values = qkv[base + 2 * head_dim : base + 3 * head_dim, lanes]
        scores = jnp.where(together, tn_dot(keys, queries) * head_dim ** (-0.5), -1e30)
        weights = jnp.exp(scores - jnp.max(scores, axis=0, keepdims=True))
        total = jnp.sum(weights, axis=0, keepdims=True)
        out = jnp.dot(values, weights.astype(jnp.bfloat16), preferred_element_type=jnp.float32)
        mixed[head * head_dim : (head + 1) * head_dim, lanes] = (out / total).astype(jnp.bfloat16)

    def output(half):
        lanes = slice(half * half_rows, (half + 1) * half_rows)
        branch[half] = tn_dot(mixed[:, lanes], wo[...])
        for du in range(1, U):
            u_ = lax.rem(u + du, U)
            for p in range(half * PIECES, (half + 1) * PIECES):
                start = u_ * half_unit + (p % PIECES) * piece_rows
                part_send[du - 1, piece(p), :] = branch[half, at(start, piece_rows), :].astype(
                    jnp.bfloat16
                )
                send(
                    part_send.at[du - 1, piece(p)],
                    part_recv.at[du - 1, piece(p)],
                    d_send.at[du - 1, p],
                    d_recv.at[du - 1, p],
                    {"sub": u_},
                )

    def exchange(half):
        for p in range(half * PIECES, (half + 1) * PIECES):
            place = piece(p)
            start = u * half_unit + (p % PIECES) * piece_rows
            value = branch[half, at(start, piece_rows), :]
            for du in range(1, U):
                landed = part_recv.at[du - 1, place]
                remote(
                    landed, landed, d_send.at[du - 1, p], d_recv.at[du - 1, p], {"sub": u}
                ).wait_recv()
                value = value + part_recv[du - 1, place, :].astype(jnp.float32)
            part_own[place, :] = value
            head_send[place, :] = value.astype(jnp.bfloat16)
            for dh in range(1, H):
                send(
                    head_send.at[place],
                    head_recv.at[dh - 1, place],
                    e_send.at[dh - 1, p],
                    e_recv.at[dh - 1, p],
                    {"head": lax.rem(h + dh, H)},
                )

    for head in range(heads):
        project(head)
        attend(head, 0)
    load_o.wait()
    output(0)
    for half in range(1, HALVES):
        for head in range(heads // 2):
            attend(head, half)
        exchange(half - 1)
        for head in range(heads // 2, heads):
            attend(head, half)
        output(half)
    exchange(HALVES - 1)

    def finish(p):
        half, index = divmod(p, PIECES)
        place = piece(p)
        value = part_own[place, :]
        for dh in range(1, H):
            landed = head_recv.at[dh - 1, place]
            remote(
                landed, landed, e_send.at[dh - 1, p], e_recv.at[dh - 1, p], {"head": h}
            ).wait_recv()
            value = value + head_recv[dh - 1, place, :].astype(jnp.float32)
        block = piece_rows * HALVES
        source = at(u * unit + index * block, block)
        value = value + halved(tokens[source, :].astype(jnp.float32), half)
        value = value.astype(jnp.bfloat16)
        wide = value.astype(jnp.float32)
        hidden_wide[half, index * piece_seq : (index + 1) * piece_seq] = wide.reshape(
            piece_seq, H, part, width
        )
        mine = vit_piece(u, p)
        vit[mine, :] = scale(value, vit_gain).astype(jnp.bfloat16)
        for du in range(1, U):
            send(
                vit.at[mine],
                vit.at[mine],
                v_send.at[du - 1, p],
                v_recv.at[du - 1, p],
                {"sub": lax.rem(u + du, U)},
            )

    def send_hidden(s_):
        rows_ = [hidden_wide[half, s_, h] for half in range(HALVES)]
        hidden[s_] = jnp.concatenate(rows_, axis=0).astype(jnp.bfloat16)
        own = hidden.at[s_]

        @pl.when(s_ != s)
        def _():
            slot = lax.rem(s_ - s + S, S) - 1
            remote(
                own, hidden_out.at[at(s * cols)], o_send.at[slot], o_recv.at[slot], {"seq": s_}
            ).start()

        @pl.when(s_ == s)
        def _():
            pltpu.make_async_copy(own, hidden_out.at[at(s * cols)], local_sem.at[4]).start()

    def gelu(x):
        return 0.5 * x * (1.0 + lax.erf(x * 0.5**0.5))

    def embed(half):
        for du in range(1, U):
            for p in range(half * PIECES, (half + 1) * PIECES):
                theirs = vit.at[vit_piece(lax.rem(u + U - du, U), p)]
                remote(
                    theirs, theirs, v_send.at[du - 1, p], v_recv.at[du - 1, p], {"sub": u}
                ).wait_recv()
        block = vit[half * half_rows : (half + 1) * half_rows, :]
        now = jnp.dot(block, wp[0], preferred_element_type=jnp.float32)
        then = jnp.dot(block, wp[1], preferred_element_type=jnp.float32)
        pooled = []
        for u_ in range(U):
            start, stop = u_ * half_unit, (u_ + 1) * half_unit
            if u_ + 1 < U:
                active = gelu(now[start:stop] + then[stop : stop + half_unit])
            else:
                active = gelu(now[start : stop - part] + then[part:half_unit])
                active = jnp.concatenate([active, jnp.zeros((part, out_width), jnp.float32)], axis=0)
            pooled.append(jnp.sum(active.reshape(-1, part, out_width), axis=1))
        return jnp.concatenate(pooled, axis=0)

    load_p.wait()
    pooled = jnp.zeros((N, out_width), jnp.float32)
    for half in range(HALVES):
        for p in range(half * PIECES, (half + 1) * PIECES):
            finish(p)
            if half == HALVES - 1:
                index = p % PIECES
                for s_ in range(index * piece_seq, (index + 1) * piece_seq):
                    send_hidden(s_)
        pooled = pooled + embed(half)
    pooled = pooled * (rolls / (cols * S))
    scored[me, :actions_n, :N] = nt_dot(w_act[...], pooled, precision=lax.Precision.HIGHEST)

    for step in range(1, N):
        other = lax.rem(me + step, N)
        where = {"seq": other // (H * U), "head": other // U % H, "sub": other % U}
        send(scored.at[me], scored.at[me], q_send.at[step - 1], q_recv.at[step - 1], where)

    for dz in range(1, S):
        s_ = lax.rem(s + dz, S)
        remote(
            hidden.at[s_],
            hidden_out.at[at(s_ * cols)],
            o_send.at[dz - 1],
            o_recv.at[dz - 1],
            {"seq": s},
        ).wait_send()
        from_ = lax.rem(s + S - dz, S)
        remote(
            hidden.at[s_],
            hidden_out.at[at(from_ * cols)],
            o_send.at[dz - 1],
            o_recv.at[dz - 1],
            {"seq": s},
        ).wait_recv()
    pltpu.make_async_copy(
        hidden.at[s], hidden_out.at[at(s * cols)], local_sem.at[4]
    ).wait()

    for step in range(1, N):
        other = lax.rem(me + N - step, N)
        place = scored.at[other]
        remote(
            place, place, q_send.at[step - 1], q_recv.at[step - 1], {"seq": s}
        ).wait_recv()

    order = lax.broadcasted_iota(jnp.int32, (N, picks), 0)
    frame = lax.rem(order, S * H) * U + order // (S * H)
    share = N // rolls
    for roll in range(rolls):
        total = scored[roll * share, :actions_n, :N]
        for index in range(1, share):
            total = total + scored[roll * share + index, :actions_n, :N]
        chosen = (frame == pair_frames[roll : roll + 1, :]).astype(jnp.float32)
        actions_out[:, roll, :] = jnp.dot(
            total, chosen, preferred_element_type=jnp.float32, precision=lax.Precision.HIGHEST
        )

    for copy in sent:
        copy.wait_send()


def shards(frames_in, attn_gain, w_qkv, w_out, vit_gain, w_pair, w_act, pair_frames):
    S, H, U = lax.axis_size("seq"), lax.axis_size("head"), lax.axis_size("sub")
    N = S * H * U
    rows_own, width = frames_in.shape
    heads = w_qkv.shape[1]
    head_dim = w_qkv.shape[2] // 3
    out_width = w_pair.shape[2]
    actions_n = w_act.shape[1]
    rolls, picks = pair_frames.shape
    cols = rows_own // S
    whole = rows_own % S == 0 and cols % 16 == 0 and S % rolls == 0 and S % PIECES == 0
    if N != F or not whole or (H * rows_own) % 128 or (H * U * rows_own) % (128 * HALVES):
        return shards_by_frame(
            frames_in, attn_gain, w_qkv, w_out, vit_gain, w_pair, w_act, pair_frames
        )
    rows = N * cols
    unit = rows // U
    bf16, f32 = jnp.bfloat16, jnp.float32
    vmem = pl.BlockSpec(memory_space=pltpu.VMEM)
    anywhere = pl.BlockSpec(memory_space=pl.ANY)
    dma = pltpu.SemaphoreType.DMA
    hidden, actions = pl.pallas_call(
        functools.partial(fused_kernel, (S, H, U, heads, head_dim)),
        out_shape=(
            jax.ShapeDtypeStruct((rows_own, width), bf16),
            jax.ShapeDtypeStruct((actions_n, rolls, picks), f32),
        ),
        in_specs=[anywhere] * 8,
        out_specs=(anywhere, vmem),
        scratch_shapes=[
            pltpu.VMEM((width,), f32),
            pltpu.VMEM((width,), f32),
            pltpu.VMEM((actions_n, out_width), f32),
            pltpu.VMEM((rolls, picks), jnp.int32),
            pltpu.VMEM((rows, width), bf16),
            pltpu.VMEM((rows, width), bf16),
            pltpu.VMEM((heads * 3 * head_dim, width), bf16),
            pltpu.VMEM(w_out.shape, bf16),
            pltpu.VMEM(w_pair.shape, bf16),
            pltpu.VMEM((heads * 3 * head_dim, rows), bf16),
            pltpu.VMEM((heads * head_dim, rows), bf16),
            pltpu.VMEM((HALVES, rows // HALVES, width), f32),
            pltpu.VMEM((U - 1, unit, width), bf16),
            pltpu.VMEM((U - 1, unit, width), bf16),
            pltpu.VMEM((unit, width), f32),
            pltpu.VMEM((unit, width), bf16),
            pltpu.VMEM((H - 1, unit, width), bf16),
            pltpu.VMEM((HALVES, S, H, cols // HALVES, width), f32),
            pltpu.VMEM((S, cols, width), bf16),
            pltpu.VMEM((rows, width), bf16),
            pltpu.VMEM((N, -(-actions_n // 8) * 8, -(-N // 128) * 128), f32),
            dma((9,)),
            dma((S - 1,)),
            dma((S - 1,)),
            dma((H - 1, S)),
            dma((H - 1, S)),
            dma((U - 1, H, S)),
            dma((U - 1, H, S)),
            dma((U - 1, HALVES * PIECES)),
            dma((U - 1, HALVES * PIECES)),
            dma((H - 1, HALVES * PIECES)),
            dma((H - 1, HALVES * PIECES)),
            dma((U - 1, HALVES * PIECES)),
            dma((U - 1, HALVES * PIECES)),
            dma((S - 1,)),
            dma((S - 1,)),
            dma((N - 1,)),
            dma((N - 1,)),
        ],
        compiler_params=pltpu.CompilerParams(
            collective_id=0, has_side_effects=True, vmem_limit_bytes=60 * 1024 * 1024
        ),
    )(
        frames_in,
        attn_gain,
        jnp.transpose(w_qkv, (1, 2, 0)).reshape(heads * 3 * head_dim, width),
        w_out,
        vit_gain,
        w_pair,
        jnp.transpose(w_act, (1, 0)),
        pair_frames,
    )
    return (hidden, jnp.transpose(actions, (1, 2, 0)))


def solution(mesh):
    in_specs = (
        P(("groups", "seq", "head", "sub"), None),
        P(),
        P(None, ("head", "sub"), None),
        P(("head", "sub"), None),
        P(),
        P(None, None, ("head", "sub")),
        P(("head", "sub"), None),
        P("groups", None),
    )
    out_specs = (P(("groups", "seq", "head", "sub"), None), P("groups", None, None))
    return jax.shard_map(shards, mesh=mesh, in_specs=in_specs, out_specs=out_specs, check_vma=False)
```

```python
import functools
import jax
import jax.numpy as jnp
from jax import lax
from jax.experimental import pallas as pl
from jax.experimental.pallas import tpu as pltpu
from jax.sharding import PartitionSpec as P

F = 16
ROLLS = 2


def from_behind(value, axis, steps):
    count = lax.axis_size(axis)
    leading, last = (max(0, -steps), min(count, count - steps))
    return lax.ppermute(value, axis, [(source, source + steps) for source in range(leading, last)])


def normalize(values_in, gain_vec):
    floats = values_in.astype(jnp.float32)
    mean_sq = jnp.mean(floats * floats, axis=-1, keepdims=True)
    return (floats * lax.rsqrt(mean_sq + 1e-06) * gain_vec).astype(jnp.bfloat16)


def shards_by_frame(frames_in, attn_gain, w_qkv, w_out, vit_gain, w_pair, w_act, pair_frames):
    rows_own = frames_in.shape[0]
    model_width = frames_in.shape[1]
    seq_count = lax.axis_size("seq")
    split_count = lax.axis_size(("head", "sub"))
    block_rows = rows_own * split_count
    total_cols = block_rows * seq_count // F
    frames_local = max(1, F // seq_count)
    cols_local = block_rows // frames_local
    frame_step = max(1, seq_count // F)
    heads_local = w_qkv.shape[1]
    triple_dim = w_qkv.shape[2]
    head_dim = triple_dim // 3
    qkv_matrix = w_qkv.reshape(model_width, heads_local * triple_dim)
    normed = lax.all_gather(normalize(frames_in, attn_gain), ("head", "sub"), axis=0, tiled=True)
    qkv_rows = jnp.dot(normed, qkv_matrix, preferred_element_type=jnp.float32).astype(jnp.bfloat16)
    qkv_rows = qkv_rows.reshape(
        frames_local, seq_count, cols_local // seq_count, heads_local, triple_dim
    )
    columns = lax.all_to_all(qkv_rows, "seq", split_axis=1, concat_axis=0, tiled=True)
    item_count = columns.shape[2]
    by_frame = columns.reshape(F, -1, heads_local, triple_dim)
    queries = by_frame[..., :head_dim]
    key_part = by_frame[..., head_dim : 2 * head_dim]
    value_part = by_frame[..., 2 * head_dim :]
    scores = jnp.einsum(
        "fchd,gchd->chfg", queries, key_part, preferred_element_type=jnp.float32
    ) * head_dim ** (-0.5)
    row_peak = jnp.max(scores, axis=-1, keepdims=True)
    weights = jnp.exp(scores - row_peak)
    weights = (weights / jnp.sum(weights, axis=-1, keepdims=True)).astype(jnp.bfloat16)
    mixed_out = jnp.einsum(
        "chfg,gchd->fchd", weights, value_part, preferred_element_type=jnp.float32
    ).astype(jnp.bfloat16)
    mixed_out = mixed_out.reshape(seq_count * frames_local, 1, item_count, heads_local * head_dim)
    attended = lax.all_to_all(mixed_out, "seq", split_axis=0, concat_axis=1, tiled=True)
    attended = attended.reshape(block_rows, heads_local * head_dim)
    branch_sum = lax.psum_scatter(
        jnp.dot(attended, w_out, preferred_element_type=jnp.float32).astype(jnp.bfloat16),
        ("head", "sub"),
        scatter_dimension=0,
        tiled=True,
    ).astype(jnp.float32)
    hidden = (frames_in.astype(jnp.float32) + branch_sum).astype(jnp.bfloat16)
    vit_own = normalize(hidden, vit_gain)
    vit_rows = lax.all_gather(vit_own, ("head", "sub"), axis=0, tiled=True)
    current = jnp.dot(vit_rows, w_pair[0], preferred_element_type=jnp.float32)
    ahead_proj = jnp.dot(vit_rows, w_pair[1], preferred_element_type=jnp.float32)
    ahead_proj = ahead_proj.reshape(frames_local, cols_local, -1)
    arrived = from_behind(ahead_proj[:1].astype(jnp.bfloat16), "seq", -frame_step).astype(
        jnp.float32
    )
    following = jnp.concatenate([ahead_proj[1:], arrived], axis=0).reshape(block_rows, -1)
    embedded = current + following
    activated = jax.nn.gelu(embedded, approximate=False).reshape(frames_local, cols_local, -1)
    seq_index = lax.axis_index("seq")
    first_token = seq_index * block_rows
    frame_first = first_token // total_cols
    col_first = first_token % total_cols
    patches = total_cols // ROLLS
    roll_ids = (col_first + jnp.arange(cols_local, dtype=jnp.int32)) // patches
    member = (roll_ids[None, :] == jnp.arange(ROLLS, dtype=jnp.int32)[:, None]).astype(
        jnp.float32
    ) / patches
    pooled = jnp.einsum("rp,fpe->fre", member, activated, precision=lax.Precision.HIGHEST)
    scored = jnp.einsum("fre,ea->fra", pooled, w_act, precision=lax.Precision.HIGHEST)
    frame_ids = frame_first + jnp.arange(frames_local, dtype=jnp.int32)
    selector = (pair_frames[:, :, None] == frame_ids[None, None, :]).astype(jnp.float32)
    partial_value = jnp.einsum("rjf,fra->rja", selector, scored, precision=lax.Precision.HIGHEST)
    actions = lax.psum(partial_value, ("seq", "head", "sub"))
    return (hidden, actions)


HALVES = 2
PIECES = 2


def nt_dot(lhs, rhs, **kw):
    return lax.dot_general(
        lhs, rhs, (((1,), (1,)), ((), ())), preferred_element_type=jnp.float32, **kw
    )


def tn_dot(lhs, rhs):
    return lax.dot_general(
        lhs, rhs, (((0,), (0,)), ((), ())), preferred_element_type=jnp.float32
    )


def fused_kernel(
    sizes,
    frames,
    attn_gain_in,
    w_qkv,
    w_out,
    vit_gain_in,
    w_pair,
    w_act_in,
    pair_frames_in,
    hidden_out,
    actions_out,
    attn_gain,
    vit_gain,
    w_act,
    pair_frames,
    own_frames,
    outgoing,
    tokens,
    normed,
    wq,
    wo,
    wp,
    qkv,
    mixed,
    branch,
    part_send,
    part_recv,
    part_own,
    head_send,
    head_recv,
    hidden_wide,
    hidden,
    vit,
    scored,
    local_sem,
    a_send,
    a_recv,
    b_send,
    b_recv,
    c_send,
    c_recv,
    d_send,
    d_recv,
    e_send,
    e_recv,
    v_send,
    v_recv,
    o_send,
    o_recv,
    q_send,
    q_recv,
):
    S, H, U, heads, head_dim = sizes
    N = S * H * U
    width = wq.shape[1]
    rows = mixed.shape[1]
    cols = rows // N
    unit = rows // U
    part = cols // HALVES
    half_rows = rows // HALVES
    half_unit = unit // HALVES
    pieces = HALVES * PIECES
    piece_rows = half_unit // PIECES
    piece_seq = S // PIECES
    actions_n, rolls, picks = actions_out.shape
    out_width = wp.shape[2]
    s, h, u = lax.axis_index("seq"), lax.axis_index("head"), lax.axis_index("sub")
    me = (s * H + h) * U + u

    def at(value, size=cols):
        return pl.ds(pl.multiple_of(value, size), size)

    def order(u_, s_, h_):
        return (u_ * S + s_) * H + h_

    def behind(d):
        return lax.rem(s + S - d, S)

    def piece(p):
        return at(p * piece_rows, piece_rows)

    def vit_piece(u_, p):
        half, index = divmod(p, PIECES)
        start = half * half_rows + u_ * half_unit + index * piece_rows
        return at(start, piece_rows)

    def unpack(half, start, count):
        packed = tokens[half, pl.ds(start, count)].astype(jnp.float32)
        packed = packed.reshape(count, HALVES, part, width // HALVES)
        wide = jnp.concatenate([packed[:, index] for index in range(HALVES)], axis=-1)
        return wide.reshape(count * part, width)

    def remote(source, target, send, recv, where):
        return pltpu.make_async_remote_copy(
            src_ref=source,
            dst_ref=target,
            send_sem=send,
            recv_sem=recv,
            device_id=where,
            device_id_type=pl.DeviceIdType.MESH,
        )

    sent = []

    def send(*args):
        copy = remote(*args)
        copy.start()
        sent.append(copy)

    load_q = pltpu.make_async_copy(w_qkv, wq, local_sem.at[0])
    load_o = pltpu.make_async_copy(w_out, wo, local_sem.at[1])
    load_p = pltpu.make_async_copy(w_pair, wp, local_sem.at[2])
    load_own = pltpu.make_async_copy(
        frames, own_frames, local_sem.at[3]
    )
    small = [
        pltpu.make_async_copy(source, target, local_sem.at[5 + index])
        for index, (source, target) in enumerate(
            (
                (attn_gain_in, attn_gain),
                (vit_gain_in, vit_gain),
                (w_act_in, w_act),
                (pair_frames_in, pair_frames),
            )
        )
    ]
    load_own.start()
    for load in small:
        load.start()
    load_q.start()
    load_o.start()
    load_p.start()

    load_own.wait()
    for t in range(S):
        for half in range(HALVES):
            start = t * cols
            slab = own_frames[start : start + cols, :].astype(jnp.float32)
            slab = slab[half * part : (half + 1) * part]
            span = width // HALVES
            packed = [slab[:, k * span : (k + 1) * span] for k in range(HALVES)]
            outgoing[half, t] = jnp.concatenate(packed, axis=0).astype(jnp.bfloat16)
    for half in range(HALVES):
        tokens[half, order(u, s, h)] = outgoing[half, s]

    barrier = pltpu.get_barrier_semaphore()

    def greet(step, carry):
        other = lax.rem(me + step, N)
        where = {"seq": other // (H * U), "head": other // U % H, "sub": other % U}
        pl.semaphore_signal(
            barrier, inc=1, device_id=where, device_id_type=pl.DeviceIdType.MESH
        )
        return carry

    lax.fori_loop(1, N, greet, 0)
    pl.semaphore_wait(barrier, N - 1)

    steps = sorted(range(S), key=lambda d: min(d, S - d))

    def to_seq(half):
        for dz in reversed(steps[1:]):
            t = lax.rem(s + dz, S)
            send(
                outgoing.at[half, t],
                tokens.at[half, order(u, s, h)],
                a_send.at[half, dz - 1],
                a_recv.at[half, dz - 1],
                {"seq": t},
            )

    def to_heads(half, dz):
        place = tokens.at[half, order(u, behind(dz), h)]
        if dz:
            remote(
                place, place, a_send.at[half, dz - 1], a_recv.at[half, dz - 1], {"seq": s}
            ).wait_recv()
        for dh in range(1, H):
            send(
                place,
                place,
                b_send.at[half, dh - 1, dz],
                b_recv.at[half, dh - 1, dz],
                {"head": lax.rem(h + dh, H)},
            )

    def to_subs(half, dz):
        s_ = behind(dz)
        for dh in range(1, H):
            place = tokens.at[half, order(u, s_, lax.rem(h + H - dh, H))]
            remote(
                place, place, b_send.at[half, dh - 1, dz], b_recv.at[half, dh - 1, dz], {"head": h}
            ).wait_recv()
        place = tokens.at[half, pl.ds(order(u, s_, 0), H)]
        for du in range(1, U):
            send(
                place,
                place,
                c_send.at[half, du - 1, dz],
                c_recv.at[half, du - 1, dz],
                {"sub": lax.rem(u + du, U)},
            )

    def scale(values, gain):
        floats = values.astype(jnp.float32)
        mean_sq = jnp.mean(floats * floats, axis=-1, keepdims=True)
        return floats * lax.rsqrt(mean_sq + 1e-06) * gain[...][None, :]

    def normalize_piece(half, u_, s_):
        scaled = scale(unpack(half, order(u_, s_, 0), H), attn_gain)
        target = at(half * half_rows + (u_ * S + s_) * H * part, H * part)
        normed[target, :] = scaled.astype(jnp.bfloat16)

    def normalize_half(half):
        for dz in steps:
            normalize_piece(half, u, behind(dz))
        for dz in steps:
            s_ = behind(dz)
            for du in range(1, U):
                u_ = lax.rem(u + U - du, U)
                place = tokens.at[half, pl.ds(order(u_, s_, 0), H)]
                remote(
                    place,
                    place,
                    c_send.at[half, du - 1, dz],
                    c_recv.at[half, du - 1, dz],
                    {"sub": u},
                ).wait_recv()
                normalize_piece(half, u_, s_)

    to_seq(0)
    to_heads(0, 0)
    for half in range(1, HALVES):
        to_seq(half)
    for load in small:
        load.wait()
    for dz in steps[1:]:
        to_heads(0, dz)
    for dz in steps:
        to_subs(0, dz)
        for half in range(1, HALVES):
            to_heads(half, dz)
    normalize_half(0)
    load_q.wait()
    first = lax.broadcasted_iota(jnp.int32, (half_rows, half_rows), 0)
    second = lax.broadcasted_iota(jnp.int32, (half_rows, half_rows), 1)
    together = lax.rem(first, part) == lax.rem(second, part)

    def project(half):
        lanes = slice(half * half_rows, (half + 1) * half_rows)
        qkv[:, lanes] = nt_dot(wq[...], normed[lanes, :]).astype(jnp.bfloat16)

    def attend(head, half):
        base = head * 3 * head_dim
        lanes = slice(half * half_rows, (half + 1) * half_rows)
        queries = qkv[base : base + head_dim, lanes]
        keys = qkv[base + head_dim : base + 2 * head_dim, lanes]
        values = qkv[base + 2 * head_dim : base + 3 * head_dim, lanes]
        scores = jnp.where(together, tn_dot(keys, queries) * head_dim ** (-0.5), -1e30)
        weights = jnp.exp(scores - jnp.max(scores, axis=0, keepdims=True))
        total = jnp.sum(weights, axis=0, keepdims=True)
        out = jnp.dot(values, weights.astype(jnp.bfloat16), preferred_element_type=jnp.float32)
        mixed[head * head_dim : (head + 1) * head_dim, lanes] = (out / total).astype(jnp.bfloat16)

    def output(half):
        lanes = slice(half * half_rows, (half + 1) * half_rows)
        branch[half] = tn_dot(mixed[:, lanes], wo[...])
        for du in range(1, U):
            u_ = lax.rem(u + du, U)
            for p in range(half * PIECES, (half + 1) * PIECES):
                start = u_ * half_unit + (p % PIECES) * piece_rows
                part_send[du - 1, piece(p), :] = branch[half, at(start, piece_rows), :].astype(
                    jnp.bfloat16
                )
                send(
                    part_send.at[du - 1, piece(p)],
                    part_recv.at[du - 1, piece(p)],
                    d_send.at[du - 1, p],
                    d_recv.at[du - 1, p],
                    {"sub": u_},
                )

    def exchange(half):
        for p in range(half * PIECES, (half + 1) * PIECES):
            place = piece(p)
            start = u * half_unit + (p % PIECES) * piece_rows
            value = branch[half, at(start, piece_rows), :]
            for du in range(1, U):
                landed = part_recv.at[du - 1, place]
                remote(
                    landed, landed, d_send.at[du - 1, p], d_recv.at[du - 1, p], {"sub": u}
                ).wait_recv()
                value = value + part_recv[du - 1, place, :].astype(jnp.float32)
            part_own[place, :] = value
            head_send[place, :] = value.astype(jnp.bfloat16)
            for dh in range(1, H):
                send(
                    head_send.at[place],
                    head_recv.at[dh - 1, place],
                    e_send.at[dh - 1, p],
                    e_recv.at[dh - 1, p],
                    {"head": lax.rem(h + dh, H)},
                )

    for half in range(HALVES):
        project(half)
        if half + 1 < HALVES:
            for dz in steps:
                to_subs(half + 1, dz)
        for head in range(heads):
            attend(head, half)
        if half == 0:
            load_o.wait()
        output(half)
        if half + 1 < HALVES:
            normalize_half(half + 1)
        exchange(half)

    def finish(p):
        half, index = divmod(p, PIECES)
        place = piece(p)
        value = part_own[place, :]
        for dh in range(1, H):
            landed = head_recv.at[dh - 1, place]
            remote(
                landed, landed, e_send.at[dh - 1, p], e_recv.at[dh - 1, p], {"head": h}
            ).wait_recv()
            value = value + head_recv[dh - 1, place, :].astype(jnp.float32)
        value = value + unpack(half, order(u, index * piece_seq, 0), piece_seq * H)
        value = value.astype(jnp.bfloat16)
        wide = value.astype(jnp.float32)
        hidden_wide[half, index * piece_seq : (index + 1) * piece_seq] = wide.reshape(
            piece_seq, H, part, width
        )
        mine = vit_piece(u, p)
        vit[mine, :] = scale(value, vit_gain).astype(jnp.bfloat16)
        for du in range(1, U):
            send(
                vit.at[mine],
                vit.at[mine],
                v_send.at[du - 1, p],
                v_recv.at[du - 1, p],
                {"sub": lax.rem(u + du, U)},
            )

    def send_hidden(s_):
        rows_ = [hidden_wide[half, s_, h] for half in range(HALVES)]
        hidden[s_] = jnp.concatenate(rows_, axis=0).astype(jnp.bfloat16)
        own = hidden.at[s_]

        @pl.when(s_ != s)
        def _():
            slot = lax.rem(s_ - s + S, S) - 1
            remote(
                own, hidden_out.at[at(s * cols)], o_send.at[slot], o_recv.at[slot], {"seq": s_}
            ).start()

        @pl.when(s_ == s)
        def _():
            pltpu.make_async_copy(own, hidden_out.at[at(s * cols)], local_sem.at[4]).start()

    def gelu(x):
        return 0.5 * x * (1.0 + lax.erf(x * 0.5**0.5))

    def embed(half):
        for du in range(1, U):
            for p in range(half * PIECES, (half + 1) * PIECES):
                theirs = vit.at[vit_piece(lax.rem(u + U - du, U), p)]
                remote(
                    theirs, theirs, v_send.at[du - 1, p], v_recv.at[du - 1, p], {"sub": u}
                ).wait_recv()
        block = vit[half * half_rows : (half + 1) * half_rows, :]
        now = jnp.dot(block, wp[0], preferred_element_type=jnp.float32)
        then = jnp.dot(block, wp[1], preferred_element_type=jnp.float32)
        pooled = []
        for u_ in range(U):
            start, stop = u_ * half_unit, (u_ + 1) * half_unit
            if u_ + 1 < U:
                active = gelu(now[start:stop] + then[stop : stop + half_unit])
            else:
                active = gelu(now[start : stop - part] + then[part:half_unit])
                active = jnp.concatenate([active, jnp.zeros((part, out_width), jnp.float32)], axis=0)
            pooled.append(jnp.sum(active.reshape(-1, part, out_width), axis=1))
        return jnp.concatenate(pooled, axis=0)

    load_p.wait()
    pooled = jnp.zeros((N, out_width), jnp.float32)
    for half in range(HALVES):
        for p in range(half * PIECES, (half + 1) * PIECES):
            finish(p)
            if half == HALVES - 1:
                index = p % PIECES
                for s_ in range(index * piece_seq, (index + 1) * piece_seq):
                    send_hidden(s_)
        pooled = pooled + embed(half)
    pooled = pooled * (rolls / (cols * S))
    scored[me, :actions_n, :N] = nt_dot(w_act[...], pooled, precision=lax.Precision.HIGHEST)

    for step in range(1, N):
        other = lax.rem(me + step, N)
        where = {"seq": other // (H * U), "head": other // U % H, "sub": other % U}
        send(scored.at[me], scored.at[me], q_send.at[step - 1], q_recv.at[step - 1], where)

    for dz in range(1, S):
        s_ = lax.rem(s + dz, S)
        remote(
            hidden.at[s_],
            hidden_out.at[at(s_ * cols)],
            o_send.at[dz - 1],
            o_recv.at[dz - 1],
            {"seq": s},
        ).wait_send()
        from_ = lax.rem(s + S - dz, S)
        remote(
            hidden.at[s_],
            hidden_out.at[at(from_ * cols)],
            o_send.at[dz - 1],
            o_recv.at[dz - 1],
            {"seq": s},
        ).wait_recv()
    pltpu.make_async_copy(
        hidden.at[s], hidden_out.at[at(s * cols)], local_sem.at[4]
    ).wait()

    for step in range(1, N):
        other = lax.rem(me + N - step, N)
        place = scored.at[other]
        remote(
            place, place, q_send.at[step - 1], q_recv.at[step - 1], {"seq": s}
        ).wait_recv()

    row = lax.broadcasted_iota(jnp.int32, (N, picks), 0)
    frame = lax.rem(row, S * H) * U + row // (S * H)
    share = N // rolls
    for roll in range(rolls):
        total = scored[roll * share, :actions_n, :N]
        for index in range(1, share):
            total = total + scored[roll * share + index, :actions_n, :N]
        chosen = (frame == pair_frames[roll : roll + 1, :]).astype(jnp.float32)
        actions_out[:, roll, :] = jnp.dot(
            total, chosen, preferred_element_type=jnp.float32, precision=lax.Precision.HIGHEST
        )

    for copy in sent:
        copy.wait_send()


def shards(frames_in, attn_gain, w_qkv, w_out, vit_gain, w_pair, w_act, pair_frames):
    S, H, U = lax.axis_size("seq"), lax.axis_size("head"), lax.axis_size("sub")
    N = S * H * U
    rows_own, width = frames_in.shape
    heads = w_qkv.shape[1]
    head_dim = w_qkv.shape[2] // 3
    out_width = w_pair.shape[2]
    actions_n = w_act.shape[1]
    rolls, picks = pair_frames.shape
    cols = rows_own // S
    whole = rows_own % S == 0 and cols % 16 == 0 and S % rolls == 0 and S % PIECES == 0
    if N != F or not whole or (H * rows_own) % 128 or (H * U * rows_own) % (128 * HALVES):
        return shards_by_frame(
            frames_in, attn_gain, w_qkv, w_out, vit_gain, w_pair, w_act, pair_frames
        )
    rows = N * cols
    unit = rows // U
    bf16, f32 = jnp.bfloat16, jnp.float32
    vmem = pl.BlockSpec(memory_space=pltpu.VMEM)
    anywhere = pl.BlockSpec(memory_space=pl.ANY)
    dma = pltpu.SemaphoreType.DMA
    hidden, actions = pl.pallas_call(
        functools.partial(fused_kernel, (S, H, U, heads, head_dim)),
        out_shape=(
            jax.ShapeDtypeStruct((rows_own, width), bf16),
            jax.ShapeDtypeStruct((actions_n, rolls, picks), f32),
        ),
        in_specs=[anywhere] * 8,
        out_specs=(anywhere, vmem),
        scratch_shapes=[
            pltpu.VMEM((width,), f32),
            pltpu.VMEM((width,), f32),
            pltpu.VMEM((actions_n, out_width), f32),
            pltpu.VMEM((rolls, picks), jnp.int32),
            pltpu.VMEM((rows_own, width), bf16),
            pltpu.VMEM((HALVES, S, cols, width // HALVES), bf16),
            pltpu.VMEM((HALVES, N, cols, width // HALVES), bf16),
            pltpu.VMEM((rows, width), bf16),
            pltpu.VMEM((heads * 3 * head_dim, width), bf16),
            pltpu.VMEM(w_out.shape, bf16),
            pltpu.VMEM(w_pair.shape, bf16),
            pltpu.VMEM((heads * 3 * head_dim, rows), bf16),
            pltpu.VMEM((heads * head_dim, rows), bf16),
            pltpu.VMEM((HALVES, rows // HALVES, width), f32),
            pltpu.VMEM((U - 1, unit, width), bf16),
            pltpu.VMEM((U - 1, unit, width), bf16),
            pltpu.VMEM((unit, width), f32),
            pltpu.VMEM((unit, width), bf16),
            pltpu.VMEM((H - 1, unit, width), bf16),
            pltpu.VMEM((HALVES, S, H, cols // HALVES, width), f32),
            pltpu.VMEM((S, cols, width), bf16),
            pltpu.VMEM((rows, width), bf16),
            pltpu.VMEM((N, -(-actions_n // 8) * 8, -(-N // 128) * 128), f32),
            dma((9,)),
            dma((HALVES, S - 1)),
            dma((HALVES, S - 1)),
            dma((HALVES, H - 1, S)),
            dma((HALVES, H - 1, S)),
            dma((HALVES, U - 1, S)),
            dma((HALVES, U - 1, S)),
            dma((U - 1, HALVES * PIECES)),
            dma((U - 1, HALVES * PIECES)),
            dma((H - 1, HALVES * PIECES)),
            dma((H - 1, HALVES * PIECES)),
            dma((U - 1, HALVES * PIECES)),
            dma((U - 1, HALVES * PIECES)),
            dma((S - 1,)),
            dma((S - 1,)),
            dma((N - 1,)),
            dma((N - 1,)),
        ],
        compiler_params=pltpu.CompilerParams(
            collective_id=0, has_side_effects=True, vmem_limit_bytes=60 * 1024 * 1024
        ),
    )(
        frames_in,
        attn_gain,
        jnp.transpose(w_qkv, (1, 2, 0)).reshape(heads * 3 * head_dim, width),
        w_out,
        vit_gain,
        w_pair,
        jnp.transpose(w_act, (1, 0)),
        pair_frames,
    )
    return (hidden, jnp.transpose(actions, (1, 2, 0)))


def solution(mesh):
    in_specs = (
        P(("groups", "seq", "head", "sub"), None),
        P(),
        P(None, ("head", "sub"), None),
        P(("head", "sub"), None),
        P(),
        P(None, None, ("head", "sub")),
        P(("head", "sub"), None),
        P("groups", None),
    )
    out_specs = (P(("groups", "seq", "head", "sub"), None), P("groups", None, None))
    return jax.shard_map(shards, mesh=mesh, in_specs=in_specs, out_specs=out_specs, check_vma=False)
```

```python
import functools
import jax
import jax.numpy as jnp
from jax import lax
from jax.experimental import pallas as pl
from jax.experimental.pallas import tpu as pltpu
from jax.sharding import PartitionSpec as P

F = 16
ROLLS = 2


def from_behind(value, axis, steps):
    count = lax.axis_size(axis)
    leading, last = (max(0, -steps), min(count, count - steps))
    return lax.ppermute(value, axis, [(source, source + steps) for source in range(leading, last)])


def normalize(values_in, gain_vec):
    floats = values_in.astype(jnp.float32)
    mean_sq = jnp.mean(floats * floats, axis=-1, keepdims=True)
    return (floats * lax.rsqrt(mean_sq + 1e-06) * gain_vec).astype(jnp.bfloat16)


def shards_by_frame(frames_in, attn_gain, w_qkv, w_out, vit_gain, w_pair, w_act, pair_frames):
    rows_own = frames_in.shape[0]
    model_width = frames_in.shape[1]
    seq_count = lax.axis_size("seq")
    split_count = lax.axis_size(("head", "sub"))
    block_rows = rows_own * split_count
    total_cols = block_rows * seq_count // F
    frames_local = max(1, F // seq_count)
    cols_local = block_rows // frames_local
    frame_step = max(1, seq_count // F)
    heads_local = w_qkv.shape[1]
    triple_dim = w_qkv.shape[2]
    head_dim = triple_dim // 3
    qkv_matrix = w_qkv.reshape(model_width, heads_local * triple_dim)
    normed = lax.all_gather(normalize(frames_in, attn_gain), ("head", "sub"), axis=0, tiled=True)
    qkv_rows = jnp.dot(normed, qkv_matrix, preferred_element_type=jnp.float32).astype(jnp.bfloat16)
    qkv_rows = qkv_rows.reshape(
        frames_local, seq_count, cols_local // seq_count, heads_local, triple_dim
    )
    columns = lax.all_to_all(qkv_rows, "seq", split_axis=1, concat_axis=0, tiled=True)
    item_count = columns.shape[2]
    by_frame = columns.reshape(F, -1, heads_local, triple_dim)
    queries = by_frame[..., :head_dim]
    key_part = by_frame[..., head_dim : 2 * head_dim]
    value_part = by_frame[..., 2 * head_dim :]
    scores = jnp.einsum(
        "fchd,gchd->chfg", queries, key_part, preferred_element_type=jnp.float32
    ) * head_dim ** (-0.5)
    row_peak = jnp.max(scores, axis=-1, keepdims=True)
    weights = jnp.exp(scores - row_peak)
    weights = (weights / jnp.sum(weights, axis=-1, keepdims=True)).astype(jnp.bfloat16)
    mixed_out = jnp.einsum(
        "chfg,gchd->fchd", weights, value_part, preferred_element_type=jnp.float32
    ).astype(jnp.bfloat16)
    mixed_out = mixed_out.reshape(seq_count * frames_local, 1, item_count, heads_local * head_dim)
    attended = lax.all_to_all(mixed_out, "seq", split_axis=0, concat_axis=1, tiled=True)
    attended = attended.reshape(block_rows, heads_local * head_dim)
    branch_sum = lax.psum_scatter(
        jnp.dot(attended, w_out, preferred_element_type=jnp.float32).astype(jnp.bfloat16),
        ("head", "sub"),
        scatter_dimension=0,
        tiled=True,
    ).astype(jnp.float32)
    hidden = (frames_in.astype(jnp.float32) + branch_sum).astype(jnp.bfloat16)
    vit_own = normalize(hidden, vit_gain)
    vit_rows = lax.all_gather(vit_own, ("head", "sub"), axis=0, tiled=True)
    current = jnp.dot(vit_rows, w_pair[0], preferred_element_type=jnp.float32)
    ahead_proj = jnp.dot(vit_rows, w_pair[1], preferred_element_type=jnp.float32)
    ahead_proj = ahead_proj.reshape(frames_local, cols_local, -1)
    arrived = from_behind(ahead_proj[:1].astype(jnp.bfloat16), "seq", -frame_step).astype(
        jnp.float32
    )
    following = jnp.concatenate([ahead_proj[1:], arrived], axis=0).reshape(block_rows, -1)
    embedded = current + following
    activated = jax.nn.gelu(embedded, approximate=False).reshape(frames_local, cols_local, -1)
    seq_index = lax.axis_index("seq")
    first_token = seq_index * block_rows
    frame_first = first_token // total_cols
    col_first = first_token % total_cols
    patches = total_cols // ROLLS
    roll_ids = (col_first + jnp.arange(cols_local, dtype=jnp.int32)) // patches
    member = (roll_ids[None, :] == jnp.arange(ROLLS, dtype=jnp.int32)[:, None]).astype(
        jnp.float32
    ) / patches
    pooled = jnp.einsum("rp,fpe->fre", member, activated, precision=lax.Precision.HIGHEST)
    scored = jnp.einsum("fre,ea->fra", pooled, w_act, precision=lax.Precision.HIGHEST)
    frame_ids = frame_first + jnp.arange(frames_local, dtype=jnp.int32)
    selector = (pair_frames[:, :, None] == frame_ids[None, None, :]).astype(jnp.float32)
    partial_value = jnp.einsum("rjf,fra->rja", selector, scored, precision=lax.Precision.HIGHEST)
    actions = lax.psum(partial_value, ("seq", "head", "sub"))
    return (hidden, actions)


HALVES = 2
PIECES = 2


def nt_dot(lhs, rhs, **kw):
    return lax.dot_general(
        lhs, rhs, (((1,), (1,)), ((), ())), preferred_element_type=jnp.float32, **kw
    )


def tn_dot(lhs, rhs):
    return lax.dot_general(
        lhs, rhs, (((0,), (0,)), ((), ())), preferred_element_type=jnp.float32
    )


def fused_kernel(
    sizes,
    frames,
    attn_gain_in,
    w_qkv,
    w_out,
    vit_gain_in,
    w_pair,
    w_act_in,
    pair_frames_in,
    hidden_out,
    actions_out,
    attn_gain,
    vit_gain,
    w_act,
    pair_frames,
    own_frames,
    outgoing,
    tokens,
    normed,
    wq,
    wo,
    wp,
    qkv,
    mixed,
    branch,
    part_send,
    part_recv,
    part_own,
    head_send,
    head_recv,
    hidden_wide,
    hidden,
    vit,
    scored,
    local_sem,
    a_send,
    a_recv,
    b_send,
    b_recv,
    c_send,
    c_recv,
    d_send,
    d_recv,
    e_send,
    e_recv,
    v_send,
    v_recv,
    o_send,
    o_recv,
    q_send,
    q_recv,
):
    S, H, U, heads, head_dim = sizes
    N = S * H * U
    width = wq.shape[1]
    rows = mixed.shape[1]
    cols = rows // N
    unit = rows // U
    part = cols // HALVES
    half_rows = rows // HALVES
    half_unit = unit // HALVES
    pieces = HALVES * PIECES
    piece_rows = half_unit // PIECES
    piece_seq = S // PIECES
    actions_n, rolls, picks = actions_out.shape
    out_width = wp.shape[2]
    s, h, u = lax.axis_index("seq"), lax.axis_index("head"), lax.axis_index("sub")
    me = (s * H + h) * U + u

    def at(value, size=cols):
        return pl.ds(pl.multiple_of(value, size), size)

    def order(u_, s_, h_):
        return (u_ * S + s_) * H + h_

    def behind(d):
        return lax.rem(s + S - d, S)

    def piece(p):
        return at(p * piece_rows, piece_rows)

    def vit_piece(u_, p):
        half, index = divmod(p, PIECES)
        start = half * half_rows + u_ * half_unit + index * piece_rows
        return at(start, piece_rows)

    def unpack(half, start, count):
        packed = tokens[half, pl.ds(start, count)].astype(jnp.float32)
        packed = packed.reshape(count, HALVES, part, width // HALVES)
        wide = jnp.concatenate([packed[:, index] for index in range(HALVES)], axis=-1)
        return wide.reshape(count * part, width)

    def remote(source, target, send, recv, where):
        return pltpu.make_async_remote_copy(
            src_ref=source,
            dst_ref=target,
            send_sem=send,
            recv_sem=recv,
            device_id=where,
            device_id_type=pl.DeviceIdType.MESH,
        )

    sent = []

    def send(*args):
        copy = remote(*args)
        copy.start()
        sent.append(copy)

    load_q = pltpu.make_async_copy(w_qkv, wq, local_sem.at[0])
    load_o = pltpu.make_async_copy(w_out, wo, local_sem.at[1])
    load_p = pltpu.make_async_copy(w_pair, wp, local_sem.at[2])
    load_own = pltpu.make_async_copy(
        frames, own_frames, local_sem.at[3]
    )
    small = [
        pltpu.make_async_copy(source, target, local_sem.at[5 + index])
        for index, (source, target) in enumerate(
            (
                (attn_gain_in, attn_gain),
                (vit_gain_in, vit_gain),
                (w_act_in, w_act),
                (pair_frames_in, pair_frames),
            )
        )
    ]
    load_own.start()
    for load in small:
        load.start()
    load_q.start()
    load_o.start()
    load_p.start()

    load_own.wait()
    for t in range(S):
        for half in range(HALVES):
            start = t * cols
            slab = own_frames[start : start + cols, :].astype(jnp.float32)
            slab = slab[half * part : (half + 1) * part]
            span = width // HALVES
            packed = [slab[:, k * span : (k + 1) * span] for k in range(HALVES)]
            outgoing[half, t] = jnp.concatenate(packed, axis=0).astype(jnp.bfloat16)
    for half in range(HALVES):
        tokens[half, order(u, s, h)] = outgoing[half, s]

    barrier = pltpu.get_barrier_semaphore()

    def greet(step, carry):
        other = lax.rem(me + step, N)
        where = {"seq": other // (H * U), "head": other // U % H, "sub": other % U}
        pl.semaphore_signal(
            barrier, inc=1, device_id=where, device_id_type=pl.DeviceIdType.MESH
        )
        return carry

    lax.fori_loop(1, N, greet, 0)
    pl.semaphore_wait(barrier, N - 1)

    steps = sorted(range(S), key=lambda d: min(d, S - d))

    def to_seq(half):
        for dz in reversed(steps[1:]):
            t = lax.rem(s + dz, S)
            send(
                outgoing.at[half, t],
                tokens.at[half, order(u, s, h)],
                a_send.at[half, dz - 1],
                a_recv.at[half, dz - 1],
                {"seq": t},
            )

    def to_heads(half, dz):
        place = tokens.at[half, order(u, behind(dz), h)]
        if dz:
            remote(
                place, place, a_send.at[half, dz - 1], a_recv.at[half, dz - 1], {"seq": s}
            ).wait_recv()
        for dh in range(1, H):
            send(
                place,
                place,
                b_send.at[half, dh - 1, dz],
                b_recv.at[half, dh - 1, dz],
                {"head": lax.rem(h + dh, H)},
            )

    def to_subs(half, dz):
        s_ = behind(dz)
        for dh in range(1, H):
            place = tokens.at[half, order(u, s_, lax.rem(h + H - dh, H))]
            remote(
                place, place, b_send.at[half, dh - 1, dz], b_recv.at[half, dh - 1, dz], {"head": h}
            ).wait_recv()
        place = tokens.at[half, pl.ds(order(u, s_, 0), H)]
        for du in range(1, U):
            send(
                place,
                place,
                c_send.at[half, du - 1, dz],
                c_recv.at[half, du - 1, dz],
                {"sub": lax.rem(u + du, U)},
            )

    def scale(values, gain):
        floats = values.astype(jnp.float32)
        mean_sq = jnp.mean(floats * floats, axis=-1, keepdims=True)
        return floats * lax.rsqrt(mean_sq + 1e-06) * gain[...][None, :]

    def normalize_piece(half, u_, s_):
        scaled = scale(unpack(half, order(u_, s_, 0), H), attn_gain)
        target = at(half * half_rows + (u_ * S + s_) * H * part, H * part)
        normed[target, :] = scaled.astype(jnp.bfloat16)

    def normalize_half(half):
        for dz in steps:
            normalize_piece(half, u, behind(dz))
        for dz in steps:
            s_ = behind(dz)
            for du in range(1, U):
                u_ = lax.rem(u + U - du, U)
                place = tokens.at[half, pl.ds(order(u_, s_, 0), H)]
                remote(
                    place,
                    place,
                    c_send.at[half, du - 1, dz],
                    c_recv.at[half, du - 1, dz],
                    {"sub": u},
                ).wait_recv()
                normalize_piece(half, u_, s_)

    to_seq(0)
    to_heads(0, 0)
    for half in range(1, HALVES):
        to_seq(half)
    for load in small:
        load.wait()
    for dz in steps[1:]:
        to_heads(0, dz)
    for dz in steps:
        to_subs(0, dz)
        for half in range(1, HALVES):
            to_heads(half, dz)
    normalize_half(0)
    load_q.wait()
    first = lax.broadcasted_iota(jnp.int32, (half_rows, half_rows), 0)
    second = lax.broadcasted_iota(jnp.int32, (half_rows, half_rows), 1)
    together = lax.rem(first, part) == lax.rem(second, part)

    def project(half):
        lanes = slice(half * half_rows, (half + 1) * half_rows)
        qkv[:, lanes] = nt_dot(wq[...], normed[lanes, :]).astype(jnp.bfloat16)

    def attend(half):
        lanes = slice(half * half_rows, (half + 1) * half_rows)

        def cut(head, index):
            base = (head * 3 + index) * head_dim
            return qkv[base : base + head_dim, lanes]

        scores = jnp.stack([tn_dot(cut(head, 1), cut(head, 0)) for head in range(heads)])
        scores = jnp.where(together[None], scores * head_dim ** (-0.5), -1e30)
        weights = jnp.exp(scores - jnp.max(scores, axis=1, keepdims=True))
        total = 1.0 / jnp.sum(weights, axis=1, keepdims=True)
        weights = (weights * total).astype(jnp.bfloat16)
        outs = [
            jnp.dot(cut(head, 2), weights[head], preferred_element_type=jnp.float32)
            for head in range(heads)
        ]
        mixed[:, lanes] = jnp.concatenate(outs, axis=0).astype(jnp.bfloat16)

    def output(half):
        lanes = slice(half * half_rows, (half + 1) * half_rows)
        branch[half] = tn_dot(mixed[:, lanes], wo[...])
        for du in range(1, U):
            u_ = lax.rem(u + du, U)
            for p in range(half * PIECES, (half + 1) * PIECES):
                start = u_ * half_unit + (p % PIECES) * piece_rows
                part_send[du - 1, piece(p), :] = branch[half, at(start, piece_rows), :].astype(
                    jnp.bfloat16
                )
                send(
                    part_send.at[du - 1, piece(p)],
                    part_recv.at[du - 1, piece(p)],
                    d_send.at[du - 1, p],
                    d_recv.at[du - 1, p],
                    {"sub": u_},
                )

    def exchange(half):
        for p in range(half * PIECES, (half + 1) * PIECES):
            place = piece(p)
            start = u * half_unit + (p % PIECES) * piece_rows
            value = branch[half, at(start, piece_rows), :]
            for du in range(1, U):
                landed = part_recv.at[du - 1, place]
                remote(
                    landed, landed, d_send.at[du - 1, p], d_recv.at[du - 1, p], {"sub": u}
                ).wait_recv()
                value = value + part_recv[du - 1, place, :].astype(jnp.float32)
            part_own[place, :] = value
            head_send[place, :] = value.astype(jnp.bfloat16)
            for dh in range(1, H):
                send(
                    head_send.at[place],
                    head_recv.at[dh - 1, place],
                    e_send.at[dh - 1, p],
                    e_recv.at[dh - 1, p],
                    {"head": lax.rem(h + dh, H)},
                )

    for half in range(HALVES):
        project(half)
        if half + 1 < HALVES:
            for dz in steps:
                to_subs(half + 1, dz)
        attend(half)
        if half == 0:
            load_o.wait()
        output(half)
        if half + 1 < HALVES:
            normalize_half(half + 1)
        exchange(half)

    def finish(p):
        half, index = divmod(p, PIECES)
        place = piece(p)
        value = part_own[place, :]
        for dh in range(1, H):
            landed = head_recv.at[dh - 1, place]
            remote(
                landed, landed, e_send.at[dh - 1, p], e_recv.at[dh - 1, p], {"head": h}
            ).wait_recv()
            value = value + head_recv[dh - 1, place, :].astype(jnp.float32)
        value = value + unpack(half, order(u, index * piece_seq, 0), piece_seq * H)
        value = value.astype(jnp.bfloat16)
        wide = value.astype(jnp.float32)
        hidden_wide[half, index * piece_seq : (index + 1) * piece_seq] = wide.reshape(
            piece_seq, H, part, width
        )
        mine = vit_piece(u, p)
        vit[mine, :] = scale(value, vit_gain).astype(jnp.bfloat16)
        for du in range(1, U):
            send(
                vit.at[mine],
                vit.at[mine],
                v_send.at[du - 1, p],
                v_recv.at[du - 1, p],
                {"sub": lax.rem(u + du, U)},
            )

    def send_hidden(s_):
        rows_ = [hidden_wide[half, s_, h] for half in range(HALVES)]
        hidden[s_] = jnp.concatenate(rows_, axis=0).astype(jnp.bfloat16)
        own = hidden.at[s_]

        @pl.when(s_ != s)
        def _():
            slot = lax.rem(s_ - s + S, S) - 1
            remote(
                own, hidden_out.at[at(s * cols)], o_send.at[slot], o_recv.at[slot], {"seq": s_}
            ).start()

        @pl.when(s_ == s)
        def _():
            pltpu.make_async_copy(own, hidden_out.at[at(s * cols)], local_sem.at[4]).start()

    def gelu(x):
        return 0.5 * x * (1.0 + lax.erf(x * 0.5**0.5))

    def embed(half):
        for du in range(1, U):
            for p in range(half * PIECES, (half + 1) * PIECES):
                theirs = vit.at[vit_piece(lax.rem(u + U - du, U), p)]
                remote(
                    theirs, theirs, v_send.at[du - 1, p], v_recv.at[du - 1, p], {"sub": u}
                ).wait_recv()
        block = vit[half * half_rows : (half + 1) * half_rows, :]
        now = jnp.dot(block, wp[0], preferred_element_type=jnp.float32)
        then = jnp.dot(block, wp[1], preferred_element_type=jnp.float32)
        pooled = []
        for u_ in range(U):
            start, stop = u_ * half_unit, (u_ + 1) * half_unit
            if u_ + 1 < U:
                active = gelu(now[start:stop] + then[stop : stop + half_unit])
            else:
                active = gelu(now[start : stop - part] + then[part:half_unit])
                active = jnp.concatenate([active, jnp.zeros((part, out_width), jnp.float32)], axis=0)
            pooled.append(jnp.sum(active.reshape(-1, part, out_width), axis=1))
        return jnp.concatenate(pooled, axis=0)

    load_p.wait()
    pooled = jnp.zeros((N, out_width), jnp.float32)
    for half in range(HALVES):
        for p in range(half * PIECES, (half + 1) * PIECES):
            finish(p)
            if half == HALVES - 1:
                index = p % PIECES
                for s_ in range(index * piece_seq, (index + 1) * piece_seq):
                    send_hidden(s_)
        pooled = pooled + embed(half)
    pooled = pooled * (rolls / (cols * S))
    scored[me, :actions_n, :N] = nt_dot(w_act[...], pooled, precision=lax.Precision.HIGHEST)

    for step in range(1, N):
        other = lax.rem(me + step, N)
        where = {"seq": other // (H * U), "head": other // U % H, "sub": other % U}
        send(scored.at[me], scored.at[me], q_send.at[step - 1], q_recv.at[step - 1], where)

    for dz in range(1, S):
        s_ = lax.rem(s + dz, S)
        remote(
            hidden.at[s_],
            hidden_out.at[at(s_ * cols)],
            o_send.at[dz - 1],
            o_recv.at[dz - 1],
            {"seq": s},
        ).wait_send()
        from_ = lax.rem(s + S - dz, S)
        remote(
            hidden.at[s_],
            hidden_out.at[at(from_ * cols)],
            o_send.at[dz - 1],
            o_recv.at[dz - 1],
            {"seq": s},
        ).wait_recv()
    pltpu.make_async_copy(
        hidden.at[s], hidden_out.at[at(s * cols)], local_sem.at[4]
    ).wait()

    for step in range(1, N):
        other = lax.rem(me + N - step, N)
        place = scored.at[other]
        remote(
            place, place, q_send.at[step - 1], q_recv.at[step - 1], {"seq": s}
        ).wait_recv()

    row = lax.broadcasted_iota(jnp.int32, (N, picks), 0)
    frame = lax.rem(row, S * H) * U + row // (S * H)
    share = N // rolls
    for roll in range(rolls):
        total = scored[roll * share, :actions_n, :N]
        for index in range(1, share):
            total = total + scored[roll * share + index, :actions_n, :N]
        chosen = (frame == pair_frames[roll : roll + 1, :]).astype(jnp.float32)
        actions_out[:, roll, :] = jnp.dot(
            total, chosen, preferred_element_type=jnp.float32, precision=lax.Precision.HIGHEST
        )

    for copy in sent:
        copy.wait_send()


def write_kernel(hidden_in, actions_in, hidden_out, actions_out, sem):
    copies = [
        pltpu.make_async_copy(hidden_in, hidden_out, sem.at[0]),
        pltpu.make_async_copy(actions_in, actions_out, sem.at[1]),
    ]
    for copy in copies:
        copy.start()
    for copy in copies:
        copy.wait()


def shards(frames_in, attn_gain, w_qkv, w_out, vit_gain, w_pair, w_act, pair_frames):
    S, H, U = lax.axis_size("seq"), lax.axis_size("head"), lax.axis_size("sub")
    N = S * H * U
    rows_own, width = frames_in.shape
    heads = w_qkv.shape[1]
    head_dim = w_qkv.shape[2] // 3
    out_width = w_pair.shape[2]
    actions_n = w_act.shape[1]
    rolls, picks = pair_frames.shape
    cols = rows_own // S
    whole = rows_own % S == 0 and cols % 16 == 0 and S % rolls == 0 and S % PIECES == 0
    if N != F or not whole or (H * rows_own) % 128 or (H * U * rows_own) % (128 * HALVES):
        return shards_by_frame(
            frames_in, attn_gain, w_qkv, w_out, vit_gain, w_pair, w_act, pair_frames
        )
    rows = N * cols
    unit = rows // U
    bf16, f32 = jnp.bfloat16, jnp.float32
    vmem = pl.BlockSpec(memory_space=pltpu.VMEM)
    anywhere = pl.BlockSpec(memory_space=pl.ANY)
    dma = pltpu.SemaphoreType.DMA
    hidden, actions = pl.pallas_call(
        functools.partial(fused_kernel, (S, H, U, heads, head_dim)),
        out_shape=(
            jax.ShapeDtypeStruct((rows_own, width), bf16),
            jax.ShapeDtypeStruct((actions_n, rolls, picks), f32),
        ),
        in_specs=[anywhere] * 8,
        out_specs=(anywhere, vmem),
        scratch_shapes=[
            pltpu.VMEM((width,), f32),
            pltpu.VMEM((width,), f32),
            pltpu.VMEM((actions_n, out_width), f32),
            pltpu.VMEM((rolls, picks), jnp.int32),
            pltpu.VMEM((rows_own, width), bf16),
            pltpu.VMEM((HALVES, S, cols, width // HALVES), bf16),
            pltpu.VMEM((HALVES, N, cols, width // HALVES), bf16),
            pltpu.VMEM((rows, width), bf16),
            pltpu.VMEM((heads * 3 * head_dim, width), bf16),
            pltpu.VMEM(w_out.shape, bf16),
            pltpu.VMEM(w_pair.shape, bf16),
            pltpu.VMEM((heads * 3 * head_dim, rows), bf16),
            pltpu.VMEM((heads * head_dim, rows), bf16),
            pltpu.VMEM((HALVES, rows // HALVES, width), f32),
            pltpu.VMEM((U - 1, unit, width), bf16),
            pltpu.VMEM((U - 1, unit, width), bf16),
            pltpu.VMEM((unit, width), f32),
            pltpu.VMEM((unit, width), bf16),
            pltpu.VMEM((H - 1, unit, width), bf16),
            pltpu.VMEM((HALVES, S, H, cols // HALVES, width), f32),
            pltpu.VMEM((S, cols, width), bf16),
            pltpu.VMEM((rows, width), bf16),
            pltpu.VMEM((N, -(-actions_n // 8) * 8, -(-N // 128) * 128), f32),
            dma((9,)),
            dma((HALVES, S - 1)),
            dma((HALVES, S - 1)),
            dma((HALVES, H - 1, S)),
            dma((HALVES, H - 1, S)),
            dma((HALVES, U - 1, S)),
            dma((HALVES, U - 1, S)),
            dma((U - 1, HALVES * PIECES)),
            dma((U - 1, HALVES * PIECES)),
            dma((H - 1, HALVES * PIECES)),
            dma((H - 1, HALVES * PIECES)),
            dma((U - 1, HALVES * PIECES)),
            dma((U - 1, HALVES * PIECES)),
            dma((S - 1,)),
            dma((S - 1,)),
            dma((N - 1,)),
            dma((N - 1,)),
        ],
        compiler_params=pltpu.CompilerParams(
            collective_id=0, has_side_effects=True, vmem_limit_bytes=60 * 1024 * 1024
        ),
    )(
        frames_in,
        attn_gain,
        jnp.transpose(w_qkv, (1, 2, 0)).reshape(heads * 3 * head_dim, width),
        w_out,
        vit_gain,
        w_pair,
        jnp.transpose(w_act, (1, 0)),
        pair_frames,
    )
    hidden, actions = pl.pallas_call(
        write_kernel,
        out_shape=(
            jax.ShapeDtypeStruct(hidden.shape, bf16),
            jax.ShapeDtypeStruct(actions.shape, f32),
        ),
        in_specs=[anywhere] * 2,
        out_specs=(anywhere, anywhere),
        scratch_shapes=[dma((2,))],
        compiler_params=pltpu.CompilerParams(vmem_limit_bytes=60 * 1024 * 1024),
    )(hidden, actions)
    return (hidden, jnp.transpose(actions, (1, 2, 0)))


def solution(mesh):
    in_specs = (
        P(("groups", "seq", "head", "sub"), None),
        P(),
        P(None, ("head", "sub"), None),
        P(("head", "sub"), None),
        P(),
        P(None, None, ("head", "sub")),
        P(("head", "sub"), None),
        P("groups", None),
    )
    out_specs = (P(("groups", "seq", "head", "sub"), None), P("groups", None, None))
    return jax.shard_map(shards, mesh=mesh, in_specs=in_specs, out_specs=out_specs, check_vma=False)
```

```python
import functools
import jax
import jax.numpy as jnp
from jax import lax
from jax.experimental import pallas as pl
from jax.experimental.pallas import tpu as pltpu
from jax.sharding import PartitionSpec as P

F = 16
ROLLS = 2


def from_behind(value, axis, steps):
    count = lax.axis_size(axis)
    leading, last = (max(0, -steps), min(count, count - steps))
    return lax.ppermute(value, axis, [(source, source + steps) for source in range(leading, last)])


def normalize(values_in, gain_vec):
    floats = values_in.astype(jnp.float32)
    mean_sq = jnp.mean(floats * floats, axis=-1, keepdims=True)
    return (floats * lax.rsqrt(mean_sq + 1e-06) * gain_vec).astype(jnp.bfloat16)


def shards_by_frame(frames_in, attn_gain, w_qkv, w_out, vit_gain, w_pair, w_act, pair_frames):
    rows_own = frames_in.shape[0]
    model_width = frames_in.shape[1]
    seq_count = lax.axis_size("seq")
    split_count = lax.axis_size(("head", "sub"))
    block_rows = rows_own * split_count
    total_cols = block_rows * seq_count // F
    frames_local = max(1, F // seq_count)
    cols_local = block_rows // frames_local
    frame_step = max(1, seq_count // F)
    heads_local = w_qkv.shape[1]
    triple_dim = w_qkv.shape[2]
    head_dim = triple_dim // 3
    qkv_matrix = w_qkv.reshape(model_width, heads_local * triple_dim)
    normed = lax.all_gather(normalize(frames_in, attn_gain), ("head", "sub"), axis=0, tiled=True)
    qkv_rows = jnp.dot(normed, qkv_matrix, preferred_element_type=jnp.float32).astype(jnp.bfloat16)
    qkv_rows = qkv_rows.reshape(
        frames_local, seq_count, cols_local // seq_count, heads_local, triple_dim
    )
    columns = lax.all_to_all(qkv_rows, "seq", split_axis=1, concat_axis=0, tiled=True)
    item_count = columns.shape[2]
    by_frame = columns.reshape(F, -1, heads_local, triple_dim)
    queries = by_frame[..., :head_dim]
    key_part = by_frame[..., head_dim : 2 * head_dim]
    value_part = by_frame[..., 2 * head_dim :]
    scores = jnp.einsum(
        "fchd,gchd->chfg", queries, key_part, preferred_element_type=jnp.float32
    ) * head_dim ** (-0.5)
    row_peak = jnp.max(scores, axis=-1, keepdims=True)
    weights = jnp.exp(scores - row_peak)
    weights = (weights / jnp.sum(weights, axis=-1, keepdims=True)).astype(jnp.bfloat16)
    mixed_out = jnp.einsum(
        "chfg,gchd->fchd", weights, value_part, preferred_element_type=jnp.float32
    ).astype(jnp.bfloat16)
    mixed_out = mixed_out.reshape(seq_count * frames_local, 1, item_count, heads_local * head_dim)
    attended = lax.all_to_all(mixed_out, "seq", split_axis=0, concat_axis=1, tiled=True)
    attended = attended.reshape(block_rows, heads_local * head_dim)
    branch_sum = lax.psum_scatter(
        jnp.dot(attended, w_out, preferred_element_type=jnp.float32).astype(jnp.bfloat16),
        ("head", "sub"),
        scatter_dimension=0,
        tiled=True,
    ).astype(jnp.float32)
    hidden = (frames_in.astype(jnp.float32) + branch_sum).astype(jnp.bfloat16)
    vit_own = normalize(hidden, vit_gain)
    vit_rows = lax.all_gather(vit_own, ("head", "sub"), axis=0, tiled=True)
    current = jnp.dot(vit_rows, w_pair[0], preferred_element_type=jnp.float32)
    ahead_proj = jnp.dot(vit_rows, w_pair[1], preferred_element_type=jnp.float32)
    ahead_proj = ahead_proj.reshape(frames_local, cols_local, -1)
    arrived = from_behind(ahead_proj[:1].astype(jnp.bfloat16), "seq", -frame_step).astype(
        jnp.float32
    )
    following = jnp.concatenate([ahead_proj[1:], arrived], axis=0).reshape(block_rows, -1)
    embedded = current + following
    activated = jax.nn.gelu(embedded, approximate=False).reshape(frames_local, cols_local, -1)
    seq_index = lax.axis_index("seq")
    first_token = seq_index * block_rows
    frame_first = first_token // total_cols
    col_first = first_token % total_cols
    patches = total_cols // ROLLS
    roll_ids = (col_first + jnp.arange(cols_local, dtype=jnp.int32)) // patches
    member = (roll_ids[None, :] == jnp.arange(ROLLS, dtype=jnp.int32)[:, None]).astype(
        jnp.float32
    ) / patches
    pooled = jnp.einsum("rp,fpe->fre", member, activated, precision=lax.Precision.HIGHEST)
    scored = jnp.einsum("fre,ea->fra", pooled, w_act, precision=lax.Precision.HIGHEST)
    frame_ids = frame_first + jnp.arange(frames_local, dtype=jnp.int32)
    selector = (pair_frames[:, :, None] == frame_ids[None, None, :]).astype(jnp.float32)
    partial_value = jnp.einsum("rjf,fra->rja", selector, scored, precision=lax.Precision.HIGHEST)
    actions = lax.psum(partial_value, ("seq", "head", "sub"))
    return (hidden, actions)


HALVES = 2
PIECES = 2


def nt_dot(lhs, rhs, **kw):
    return lax.dot_general(
        lhs, rhs, (((1,), (1,)), ((), ())), preferred_element_type=jnp.float32, **kw
    )


def tn_dot(lhs, rhs):
    return lax.dot_general(
        lhs, rhs, (((0,), (0,)), ((), ())), preferred_element_type=jnp.float32
    )


def fused_kernel(
    sizes,
    frames,
    attn_gain_in,
    w_qkv,
    w_out,
    vit_gain_in,
    w_pair,
    w_act_in,
    pair_frames_in,
    hidden_out,
    actions_out,
    attn_gain,
    vit_gain,
    w_act,
    pair_frames,
    own_frames,
    outgoing,
    tokens,
    normed,
    wq,
    wo,
    wp,
    qkv,
    mixed,
    branch,
    part_send,
    part_recv,
    part_own,
    head_send,
    head_recv,
    hidden_wide,
    hidden,
    vit,
    scored,
    local_sem,
    a_send,
    a_recv,
    b_send,
    b_recv,
    c_send,
    c_recv,
    d_send,
    d_recv,
    e_send,
    e_recv,
    v_send,
    v_recv,
    o_send,
    o_recv,
    q_send,
    q_recv,
):
    S, H, U, heads, head_dim = sizes
    N = S * H * U
    width = wq.shape[1]
    rows = mixed.shape[1]
    cols = rows // N
    unit = rows // U
    part = cols // HALVES
    half_rows = rows // HALVES
    half_unit = unit // HALVES
    pieces = HALVES * PIECES
    piece_rows = half_unit // PIECES
    piece_seq = S // PIECES
    actions_n, rolls, picks = actions_out.shape
    out_width = wp.shape[2]
    s, h, u = lax.axis_index("seq"), lax.axis_index("head"), lax.axis_index("sub")
    me = (s * H + h) * U + u

    def at(value, size=cols):
        return pl.ds(pl.multiple_of(value, size), size)

    def order(u_, s_, h_):
        return (u_ * S + s_) * H + h_

    def behind(d):
        return lax.rem(s + S - d, S)

    def piece(p):
        return at(p * piece_rows, piece_rows)

    def vit_piece(u_, p):
        half, index = divmod(p, PIECES)
        start = half * half_rows + u_ * half_unit + index * piece_rows
        return at(start, piece_rows)

    def unpack(half, start, count):
        packed = tokens[half, pl.ds(start, count)].astype(jnp.float32)
        packed = packed.reshape(count, HALVES, part, width // HALVES)
        wide = jnp.concatenate([packed[:, index] for index in range(HALVES)], axis=-1)
        return wide.reshape(count * part, width)

    def remote(source, target, send, recv, where):
        return pltpu.make_async_remote_copy(
            src_ref=source,
            dst_ref=target,
            send_sem=send,
            recv_sem=recv,
            device_id=where,
            device_id_type=pl.DeviceIdType.MESH,
        )

    sent = []

    def send(*args):
        copy = remote(*args)
        copy.start()
        sent.append(copy)

    load_q = pltpu.make_async_copy(w_qkv, wq, local_sem.at[0])
    load_o = pltpu.make_async_copy(w_out, wo, local_sem.at[1])
    load_p = pltpu.make_async_copy(w_pair, wp, local_sem.at[2])
    load_own = pltpu.make_async_copy(
        frames, own_frames, local_sem.at[3]
    )
    small = [
        pltpu.make_async_copy(source, target, local_sem.at[5 + index])
        for index, (source, target) in enumerate(
            (
                (attn_gain_in, attn_gain),
                (vit_gain_in, vit_gain),
                (w_act_in, w_act),
                (pair_frames_in, pair_frames),
            )
        )
    ]
    load_own.start()
    for load in small:
        load.start()
    load_q.start()
    load_o.start()
    load_p.start()

    barrier = pltpu.get_barrier_semaphore()

    def greet(step, carry):
        other = lax.rem(me + step, N)
        where = {"seq": other // (H * U), "head": other // U % H, "sub": other % U}
        pl.semaphore_signal(
            barrier, inc=1, device_id=where, device_id_type=pl.DeviceIdType.MESH
        )
        return carry

    lax.fori_loop(1, N, greet, 0)
    load_own.wait()
    for t in range(S):
        for half in range(HALVES):
            start = t * cols
            slab = own_frames[start : start + cols, :].astype(jnp.float32)
            slab = slab[half * part : (half + 1) * part]
            span = width // HALVES
            packed = [slab[:, k * span : (k + 1) * span] for k in range(HALVES)]
            outgoing[half, t] = jnp.concatenate(packed, axis=0).astype(jnp.bfloat16)
    for half in range(HALVES):
        tokens[half, order(u, s, h)] = outgoing[half, s]

    pl.semaphore_wait(barrier, N - 1)

    steps = sorted(range(S), key=lambda d: min(d, S - d))

    def to_seq(half):
        for dz in reversed(steps[1:]):
            t = lax.rem(s + dz, S)
            send(
                outgoing.at[half, t],
                tokens.at[half, order(u, s, h)],
                a_send.at[half, dz - 1],
                a_recv.at[half, dz - 1],
                {"seq": t},
            )

    def to_heads(half, dz):
        place = tokens.at[half, order(u, behind(dz), h)]
        if dz:
            remote(
                place, place, a_send.at[half, dz - 1], a_recv.at[half, dz - 1], {"seq": s}
            ).wait_recv()
        for dh in range(1, H):
            send(
                place,
                place,
                b_send.at[half, dh - 1, dz],
                b_recv.at[half, dh - 1, dz],
                {"head": lax.rem(h + dh, H)},
            )

    def to_subs(half, dz):
        s_ = behind(dz)
        for dh in range(1, H):
            place = tokens.at[half, order(u, s_, lax.rem(h + H - dh, H))]
            remote(
                place, place, b_send.at[half, dh - 1, dz], b_recv.at[half, dh - 1, dz], {"head": h}
            ).wait_recv()
        place = tokens.at[half, pl.ds(order(u, s_, 0), H)]
        for du in range(1, U):
            send(
                place,
                place,
                c_send.at[half, du - 1, dz],
                c_recv.at[half, du - 1, dz],
                {"sub": lax.rem(u + du, U)},
            )

    def scale(values, gain):
        floats = values.astype(jnp.float32)
        mean_sq = jnp.mean(floats * floats, axis=-1, keepdims=True)
        return floats * lax.rsqrt(mean_sq + 1e-06) * gain[...][None, :]

    def normalize_piece(half, u_, s_):
        scaled = scale(unpack(half, order(u_, s_, 0), H), attn_gain)
        target = at(half * half_rows + (u_ * S + s_) * H * part, H * part)
        normed[target, :] = scaled.astype(jnp.bfloat16)

    def normalize_half(half):
        for dz in steps:
            normalize_piece(half, u, behind(dz))
        for dz in steps:
            s_ = behind(dz)
            for du in range(1, U):
                u_ = lax.rem(u + U - du, U)
                place = tokens.at[half, pl.ds(order(u_, s_, 0), H)]
                remote(
                    place,
                    place,
                    c_send.at[half, du - 1, dz],
                    c_recv.at[half, du - 1, dz],
                    {"sub": u},
                ).wait_recv()
                normalize_piece(half, u_, s_)

    to_seq(0)
    to_heads(0, 0)
    for load in small:
        load.wait()
    for dz in steps[1:]:
        to_heads(0, dz)
    for half in range(1, HALVES):
        to_seq(half)
        to_heads(half, 0)
    for dz in steps:
        to_subs(0, dz)
    normalize_half(0)
    load_q.wait()
    first = lax.broadcasted_iota(jnp.int32, (half_rows, half_rows), 0)
    second = lax.broadcasted_iota(jnp.int32, (half_rows, half_rows), 1)
    together = lax.rem(first, part) == lax.rem(second, part)

    def project(half):
        lanes = slice(half * half_rows, (half + 1) * half_rows)
        qkv[:, lanes] = nt_dot(wq[...], normed[lanes, :]).astype(jnp.bfloat16)

    def attend(half):
        lanes = slice(half * half_rows, (half + 1) * half_rows)

        def cut(head, index):
            base = (head * 3 + index) * head_dim
            return qkv[base : base + head_dim, lanes]

        scores = jnp.stack([tn_dot(cut(head, 1), cut(head, 0)) for head in range(heads)])
        scores = jnp.where(together[None], scores * head_dim ** (-0.5), -1e30)
        weights = jnp.exp(scores - jnp.max(scores, axis=1, keepdims=True))
        total = 1.0 / jnp.sum(weights, axis=1, keepdims=True)
        weights = (weights * total).astype(jnp.bfloat16)
        outs = [
            jnp.dot(cut(head, 2), weights[head], preferred_element_type=jnp.float32)
            for head in range(heads)
        ]
        mixed[:, lanes] = jnp.concatenate(outs, axis=0).astype(jnp.bfloat16)

    def output(half):
        lanes = slice(half * half_rows, (half + 1) * half_rows)
        branch[half] = tn_dot(mixed[:, lanes], wo[...])
        for du in range(1, U):
            u_ = lax.rem(u + du, U)
            for p in range(half * PIECES, (half + 1) * PIECES):
                start = u_ * half_unit + (p % PIECES) * piece_rows
                part_send[du - 1, piece(p), :] = branch[half, at(start, piece_rows), :].astype(
                    jnp.bfloat16
                )
                send(
                    part_send.at[du - 1, piece(p)],
                    part_recv.at[du - 1, piece(p)],
                    d_send.at[du - 1, p],
                    d_recv.at[du - 1, p],
                    {"sub": u_},
                )

    def exchange(half):
        for p in range(half * PIECES, (half + 1) * PIECES):
            place = piece(p)
            start = u * half_unit + (p % PIECES) * piece_rows
            value = branch[half, at(start, piece_rows), :]
            for du in range(1, U):
                landed = part_recv.at[du - 1, place]
                remote(
                    landed, landed, d_send.at[du - 1, p], d_recv.at[du - 1, p], {"sub": u}
                ).wait_recv()
                value = value + part_recv[du - 1, place, :].astype(jnp.float32)
            part_own[place, :] = value
            head_send[place, :] = value.astype(jnp.bfloat16)
            for dh in range(1, H):
                send(
                    head_send.at[place],
                    head_recv.at[dh - 1, place],
                    e_send.at[dh - 1, p],
                    e_recv.at[dh - 1, p],
                    {"head": lax.rem(h + dh, H)},
                )

    for half in range(HALVES):
        following = steps[1:] if half + 1 < HALVES else []
        project(half)
        for dz in following[:1]:
            to_heads(half + 1, dz)
        attend(half)
        for dz in following[1:]:
            to_heads(half + 1, dz)
        if half == 0:
            load_o.wait()
        output(half)
        exchange(half)
        if half + 1 < HALVES:
            for dz in steps:
                to_subs(half + 1, dz)
            normalize_half(half + 1)

    def finish(p):
        half, index = divmod(p, PIECES)
        place = piece(p)
        value = part_own[place, :]
        for dh in range(1, H):
            landed = head_recv.at[dh - 1, place]
            remote(
                landed, landed, e_send.at[dh - 1, p], e_recv.at[dh - 1, p], {"head": h}
            ).wait_recv()
            value = value + head_recv[dh - 1, place, :].astype(jnp.float32)
        value = value + unpack(half, order(u, index * piece_seq, 0), piece_seq * H)
        value = value.astype(jnp.bfloat16)
        wide = value.astype(jnp.float32)
        hidden_wide[half, index * piece_seq : (index + 1) * piece_seq] = wide.reshape(
            piece_seq, H, part, width
        )
        mine = vit_piece(u, p)
        vit[mine, :] = scale(value, vit_gain).astype(jnp.bfloat16)
        for du in range(1, U):
            send(
                vit.at[mine],
                vit.at[mine],
                v_send.at[du - 1, p],
                v_recv.at[du - 1, p],
                {"sub": lax.rem(u + du, U)},
            )

    def send_hidden(s_):
        rows_ = [hidden_wide[half, s_, h] for half in range(HALVES)]
        hidden[s_] = jnp.concatenate(rows_, axis=0).astype(jnp.bfloat16)
        own = hidden.at[s_]

        @pl.when(s_ != s)
        def _():
            slot = lax.rem(s_ - s + S, S) - 1
            remote(
                own, hidden_out.at[at(s * cols)], o_send.at[slot], o_recv.at[slot], {"seq": s_}
            ).start()

        @pl.when(s_ == s)
        def _():
            pltpu.make_async_copy(own, hidden_out.at[at(s * cols)], local_sem.at[4]).start()

    def gelu(x):
        return 0.5 * x * (1.0 + lax.erf(x * 0.5**0.5))

    def embed(half):
        for du in range(1, U):
            for p in range(half * PIECES, (half + 1) * PIECES):
                theirs = vit.at[vit_piece(lax.rem(u + U - du, U), p)]
                remote(
                    theirs, theirs, v_send.at[du - 1, p], v_recv.at[du - 1, p], {"sub": u}
                ).wait_recv()
        block = vit[half * half_rows : (half + 1) * half_rows, :]
        now = jnp.dot(block, wp[0], preferred_element_type=jnp.float32)
        then = jnp.dot(block, wp[1], preferred_element_type=jnp.float32)
        pooled = []
        for u_ in range(U):
            start, stop = u_ * half_unit, (u_ + 1) * half_unit
            if u_ + 1 < U:
                active = gelu(now[start:stop] + then[stop : stop + half_unit])
            else:
                active = gelu(now[start : stop - part] + then[part:half_unit])
                active = jnp.concatenate([active, jnp.zeros((part, out_width), jnp.float32)], axis=0)
            pooled.append(jnp.sum(active.reshape(-1, part, out_width), axis=1))
        return jnp.concatenate(pooled, axis=0)

    load_p.wait()
    pooled = jnp.zeros((N, out_width), jnp.float32)
    for half in range(HALVES):
        for p in range(half * PIECES, (half + 1) * PIECES):
            finish(p)
            if half == HALVES - 1:
                index = p % PIECES
                for s_ in range(index * piece_seq, (index + 1) * piece_seq):
                    send_hidden(s_)
        pooled = pooled + embed(half)
    pooled = pooled * (rolls / (cols * S))
    scored[me, :actions_n, :N] = nt_dot(w_act[...], pooled, precision=lax.Precision.HIGHEST)

    for step in range(1, N):
        other = lax.rem(me + step, N)
        where = {"seq": other // (H * U), "head": other // U % H, "sub": other % U}
        send(scored.at[me], scored.at[me], q_send.at[step - 1], q_recv.at[step - 1], where)

    for dz in range(1, S):
        s_ = lax.rem(s + dz, S)
        remote(
            hidden.at[s_],
            hidden_out.at[at(s_ * cols)],
            o_send.at[dz - 1],
            o_recv.at[dz - 1],
            {"seq": s},
        ).wait_send()
        from_ = lax.rem(s + S - dz, S)
        remote(
            hidden.at[s_],
            hidden_out.at[at(from_ * cols)],
            o_send.at[dz - 1],
            o_recv.at[dz - 1],
            {"seq": s},
        ).wait_recv()
    pltpu.make_async_copy(
        hidden.at[s], hidden_out.at[at(s * cols)], local_sem.at[4]
    ).wait()

    for step in range(1, N):
        other = lax.rem(me + N - step, N)
        place = scored.at[other]
        remote(
            place, place, q_send.at[step - 1], q_recv.at[step - 1], {"seq": s}
        ).wait_recv()

    row = lax.broadcasted_iota(jnp.int32, (N, picks), 0)
    frame = lax.rem(row, S * H) * U + row // (S * H)
    share = N // rolls
    for roll in range(rolls):
        total = scored[roll * share, :actions_n, :N]
        for index in range(1, share):
            total = total + scored[roll * share + index, :actions_n, :N]
        chosen = (frame == pair_frames[roll : roll + 1, :]).astype(jnp.float32)
        actions_out[:, roll, :] = jnp.dot(
            total, chosen, preferred_element_type=jnp.float32, precision=lax.Precision.HIGHEST
        )

    for copy in sent:
        copy.wait_send()


def write_kernel(hidden_in, actions_in, hidden_out, actions_out):
    hidden_out[...] = hidden_in[...]
    actions_out[...] = actions_in[...]


def shards(frames_in, attn_gain, w_qkv, w_out, vit_gain, w_pair, w_act, pair_frames):
    S, H, U = lax.axis_size("seq"), lax.axis_size("head"), lax.axis_size("sub")
    N = S * H * U
    rows_own, width = frames_in.shape
    heads = w_qkv.shape[1]
    head_dim = w_qkv.shape[2] // 3
    out_width = w_pair.shape[2]
    actions_n = w_act.shape[1]
    rolls, picks = pair_frames.shape
    cols = rows_own // S
    whole = rows_own % S == 0 and cols % 16 == 0 and S % rolls == 0 and S % PIECES == 0
    if N != F or not whole or (H * rows_own) % 128 or (H * U * rows_own) % (128 * HALVES):
        return shards_by_frame(
            frames_in, attn_gain, w_qkv, w_out, vit_gain, w_pair, w_act, pair_frames
        )
    rows = N * cols
    unit = rows // U
    bf16, f32 = jnp.bfloat16, jnp.float32
    vmem = pl.BlockSpec(memory_space=pltpu.VMEM)
    anywhere = pl.BlockSpec(memory_space=pl.ANY)
    dma = pltpu.SemaphoreType.DMA
    hidden, actions = pl.pallas_call(
        functools.partial(fused_kernel, (S, H, U, heads, head_dim)),
        out_shape=(
            jax.ShapeDtypeStruct((rows_own, width), bf16),
            jax.ShapeDtypeStruct((actions_n, rolls, picks), f32),
        ),
        in_specs=[anywhere] * 8,
        out_specs=(anywhere, vmem),
        scratch_shapes=[
            pltpu.VMEM((width,), f32),
            pltpu.VMEM((width,), f32),
            pltpu.VMEM((actions_n, out_width), f32),
            pltpu.VMEM((rolls, picks), jnp.int32),
            pltpu.VMEM((rows_own, width), bf16),
            pltpu.VMEM((HALVES, S, cols, width // HALVES), bf16),
            pltpu.VMEM((HALVES, N, cols, width // HALVES), bf16),
            pltpu.VMEM((rows, width), bf16),
            pltpu.VMEM((heads * 3 * head_dim, width), bf16),
            pltpu.VMEM(w_out.shape, bf16),
            pltpu.VMEM(w_pair.shape, bf16),
            pltpu.VMEM((heads * 3 * head_dim, rows), bf16),
            pltpu.VMEM((heads * head_dim, rows), bf16),
            pltpu.VMEM((HALVES, rows // HALVES, width), f32),
            pltpu.VMEM((U - 1, unit, width), bf16),
            pltpu.VMEM((U - 1, unit, width), bf16),
            pltpu.VMEM((unit, width), f32),
            pltpu.VMEM((unit, width), bf16),
            pltpu.VMEM((H - 1, unit, width), bf16),
            pltpu.VMEM((HALVES, S, H, cols // HALVES, width), f32),
            pltpu.VMEM((S, cols, width), bf16),
            pltpu.VMEM((rows, width), bf16),
            pltpu.VMEM((N, -(-actions_n // 8) * 8, -(-N // 128) * 128), f32),
            dma((9,)),
            dma((HALVES, S - 1)),
            dma((HALVES, S - 1)),
            dma((HALVES, H - 1, S)),
            dma((HALVES, H - 1, S)),
            dma((HALVES, U - 1, S)),
            dma((HALVES, U - 1, S)),
            dma((U - 1, HALVES * PIECES)),
            dma((U - 1, HALVES * PIECES)),
            dma((H - 1, HALVES * PIECES)),
            dma((H - 1, HALVES * PIECES)),
            dma((U - 1, HALVES * PIECES)),
            dma((U - 1, HALVES * PIECES)),
            dma((S - 1,)),
            dma((S - 1,)),
            dma((N - 1,)),
            dma((N - 1,)),
        ],
        compiler_params=pltpu.CompilerParams(
            collective_id=0, has_side_effects=True, vmem_limit_bytes=60 * 1024 * 1024
        ),
    )(
        frames_in,
        attn_gain,
        jnp.transpose(w_qkv, (1, 2, 0)).reshape(heads * 3 * head_dim, width),
        w_out,
        vit_gain,
        w_pair,
        jnp.transpose(w_act, (1, 0)),
        pair_frames,
    )
    hidden, actions = pl.pallas_call(
        write_kernel,
        out_shape=(
            jax.ShapeDtypeStruct(hidden.shape, bf16),
            jax.ShapeDtypeStruct(actions.shape, f32),
        ),
        in_specs=[vmem] * 2,
        out_specs=(vmem, vmem),
    )(hidden, actions)
    return (hidden, jnp.transpose(actions, (1, 2, 0)))


def solution(mesh):
    in_specs = (
        P(("groups", "seq", "head", "sub"), None),
        P(),
        P(None, ("head", "sub"), None),
        P(("head", "sub"), None),
        P(),
        P(None, None, ("head", "sub")),
        P(("head", "sub"), None),
        P("groups", None),
    )
    out_specs = (P(("groups", "seq", "head", "sub"), None), P("groups", None, None))
    return jax.shard_map(shards, mesh=mesh, in_specs=in_specs, out_specs=out_specs, check_vma=False)
```

```python
import functools
import jax
import jax.numpy as jnp
from jax import lax
from jax.experimental import pallas as pl
from jax.experimental.pallas import tpu as pltpu
from jax.sharding import PartitionSpec as P

F = 16
ROLLS = 2


def from_behind(value, axis, steps):
    count = lax.axis_size(axis)
    leading, last = (max(0, -steps), min(count, count - steps))
    return lax.ppermute(value, axis, [(source, source + steps) for source in range(leading, last)])


def normalize(values_in, gain_vec):
    floats = values_in.astype(jnp.float32)
    mean_sq = jnp.mean(floats * floats, axis=-1, keepdims=True)
    return (floats * lax.rsqrt(mean_sq + 1e-06) * gain_vec).astype(jnp.bfloat16)


def shards_by_frame(frames_in, attn_gain, w_qkv, w_out, vit_gain, w_pair, w_act, pair_frames):
    rows_own = frames_in.shape[0]
    model_width = frames_in.shape[1]
    seq_count = lax.axis_size("seq")
    split_count = lax.axis_size(("head", "sub"))
    block_rows = rows_own * split_count
    total_cols = block_rows * seq_count // F
    frames_local = max(1, F // seq_count)
    cols_local = block_rows // frames_local
    frame_step = max(1, seq_count // F)
    heads_local = w_qkv.shape[1]
    triple_dim = w_qkv.shape[2]
    head_dim = triple_dim // 3
    qkv_matrix = w_qkv.reshape(model_width, heads_local * triple_dim)
    normed = lax.all_gather(normalize(frames_in, attn_gain), ("head", "sub"), axis=0, tiled=True)
    qkv_rows = jnp.dot(normed, qkv_matrix, preferred_element_type=jnp.float32).astype(jnp.bfloat16)
    qkv_rows = qkv_rows.reshape(
        frames_local, seq_count, cols_local // seq_count, heads_local, triple_dim
    )
    columns = lax.all_to_all(qkv_rows, "seq", split_axis=1, concat_axis=0, tiled=True)
    item_count = columns.shape[2]
    by_frame = columns.reshape(F, -1, heads_local, triple_dim)
    queries = by_frame[..., :head_dim]
    key_part = by_frame[..., head_dim : 2 * head_dim]
    value_part = by_frame[..., 2 * head_dim :]
    scores = jnp.einsum(
        "fchd,gchd->chfg", queries, key_part, preferred_element_type=jnp.float32
    ) * head_dim ** (-0.5)
    row_peak = jnp.max(scores, axis=-1, keepdims=True)
    weights = jnp.exp(scores - row_peak)
    weights = (weights / jnp.sum(weights, axis=-1, keepdims=True)).astype(jnp.bfloat16)
    mixed_out = jnp.einsum(
        "chfg,gchd->fchd", weights, value_part, preferred_element_type=jnp.float32
    ).astype(jnp.bfloat16)
    mixed_out = mixed_out.reshape(seq_count * frames_local, 1, item_count, heads_local * head_dim)
    attended = lax.all_to_all(mixed_out, "seq", split_axis=0, concat_axis=1, tiled=True)
    attended = attended.reshape(block_rows, heads_local * head_dim)
    branch_sum = lax.psum_scatter(
        jnp.dot(attended, w_out, preferred_element_type=jnp.float32).astype(jnp.bfloat16),
        ("head", "sub"),
        scatter_dimension=0,
        tiled=True,
    ).astype(jnp.float32)
    hidden = (frames_in.astype(jnp.float32) + branch_sum).astype(jnp.bfloat16)
    vit_own = normalize(hidden, vit_gain)
    vit_rows = lax.all_gather(vit_own, ("head", "sub"), axis=0, tiled=True)
    current = jnp.dot(vit_rows, w_pair[0], preferred_element_type=jnp.float32)
    ahead_proj = jnp.dot(vit_rows, w_pair[1], preferred_element_type=jnp.float32)
    ahead_proj = ahead_proj.reshape(frames_local, cols_local, -1)
    arrived = from_behind(ahead_proj[:1].astype(jnp.bfloat16), "seq", -frame_step).astype(
        jnp.float32
    )
    following = jnp.concatenate([ahead_proj[1:], arrived], axis=0).reshape(block_rows, -1)
    embedded = current + following
    activated = jax.nn.gelu(embedded, approximate=False).reshape(frames_local, cols_local, -1)
    seq_index = lax.axis_index("seq")
    first_token = seq_index * block_rows
    frame_first = first_token // total_cols
    col_first = first_token % total_cols
    patches = total_cols // ROLLS
    roll_ids = (col_first + jnp.arange(cols_local, dtype=jnp.int32)) // patches
    member = (roll_ids[None, :] == jnp.arange(ROLLS, dtype=jnp.int32)[:, None]).astype(
        jnp.float32
    ) / patches
    pooled = jnp.einsum("rp,fpe->fre", member, activated, precision=lax.Precision.HIGHEST)
    scored = jnp.einsum("fre,ea->fra", pooled, w_act, precision=lax.Precision.HIGHEST)
    frame_ids = frame_first + jnp.arange(frames_local, dtype=jnp.int32)
    selector = (pair_frames[:, :, None] == frame_ids[None, None, :]).astype(jnp.float32)
    partial_value = jnp.einsum("rjf,fra->rja", selector, scored, precision=lax.Precision.HIGHEST)
    actions = lax.psum(partial_value, ("seq", "head", "sub"))
    return (hidden, actions)


HALVES = 2
PIECES = 2


def nt_dot(lhs, rhs, **kw):
    return lax.dot_general(
        lhs, rhs, (((1,), (1,)), ((), ())), preferred_element_type=jnp.float32, **kw
    )


def tn_dot(lhs, rhs):
    return lax.dot_general(
        lhs, rhs, (((0,), (0,)), ((), ())), preferred_element_type=jnp.float32
    )


def fused_kernel(
    sizes,
    frames,
    attn_gain_in,
    w_qkv,
    w_out,
    vit_gain_in,
    w_pair,
    w_act_in,
    pair_frames_in,
    hidden_out,
    actions_out,
    attn_gain,
    vit_gain,
    w_act,
    pair_frames,
    own_frames,
    outgoing,
    tokens,
    normed,
    wq,
    wo,
    wp,
    qkv,
    mixed,
    branch,
    part_send,
    part_recv,
    part_own,
    head_send,
    head_recv,
    hidden_wide,
    hidden,
    vit,
    grouped,
    scored,
    local_sem,
    a_send,
    a_recv,
    b_send,
    b_recv,
    c_send,
    c_recv,
    d_send,
    d_recv,
    e_send,
    e_recv,
    v_send,
    v_recv,
    o_send,
    o_recv,
    p_send,
    p_recv,
    q_send,
    q_recv,
):
    S, H, U, heads, head_dim = sizes
    N = S * H * U
    width = wq.shape[1]
    rows = mixed.shape[1]
    cols = rows // N
    unit = rows // U
    part = cols // HALVES
    half_rows = rows // HALVES
    half_unit = unit // HALVES
    pieces = HALVES * PIECES
    piece_rows = half_unit // PIECES
    piece_seq = S // PIECES
    actions_n, rolls, picks = actions_out.shape
    out_width = wp.shape[2]
    s, h, u = lax.axis_index("seq"), lax.axis_index("head"), lax.axis_index("sub")

    def at(value, size=cols):
        return pl.ds(pl.multiple_of(value, size), size)

    def order(u_, s_, h_):
        return (u_ * S + s_) * H + h_

    def behind(d):
        return lax.rem(s + S - d, S)

    def piece(p):
        return at(p * piece_rows, piece_rows)

    def vit_piece(u_, p):
        half, index = divmod(p, PIECES)
        start = half * half_rows + u_ * half_unit + index * piece_rows
        return at(start, piece_rows)

    def unpack(half, start, count):
        packed = tokens[half, pl.ds(start, count)].astype(jnp.float32)
        packed = packed.reshape(count, HALVES, part, width // HALVES)
        wide = jnp.concatenate([packed[:, index] for index in range(HALVES)], axis=-1)
        return wide.reshape(count * part, width)

    def remote(source, target, send, recv, where):
        return pltpu.make_async_remote_copy(
            src_ref=source,
            dst_ref=target,
            send_sem=send,
            recv_sem=recv,
            device_id=where,
            device_id_type=pl.DeviceIdType.MESH,
        )

    sent = []

    def send(*args):
        copy = remote(*args)
        copy.start()
        sent.append(copy)

    load_q = pltpu.make_async_copy(w_qkv, wq, local_sem.at[0])
    load_o = pltpu.make_async_copy(w_out, wo, local_sem.at[1])
    load_p = pltpu.make_async_copy(w_pair, wp, local_sem.at[2])
    load_own = pltpu.make_async_copy(
        frames, own_frames, local_sem.at[3]
    )
    small = [
        pltpu.make_async_copy(source, target, local_sem.at[5 + index])
        for index, (source, target) in enumerate(
            (
                (attn_gain_in, attn_gain),
                (vit_gain_in, vit_gain),
                (w_act_in, w_act),
                (pair_frames_in, pair_frames),
            )
        )
    ]
    load_own.start()
    for load in small:
        load.start()
    load_q.start()
    load_o.start()
    load_p.start()

    barrier = pltpu.get_barrier_semaphore()

    G = H * U
    mine = h * U + u

    def group_peer(step):
        other = lax.rem(mine + step, G)
        return {"head": other // U, "sub": lax.rem(other, U)}

    def seq_peer(step):
        return {"seq": lax.rem(s + step, S)}

    peers = [group_peer(step) for step in range(1, G)] + [seq_peer(step) for step in range(1, S)]
    for where in peers:
        pl.semaphore_signal(
            barrier, inc=1, device_id=where, device_id_type=pl.DeviceIdType.MESH
        )
    load_own.wait()
    for t in range(S):
        for half in range(HALVES):
            start = t * cols
            slab = own_frames[start : start + cols, :].astype(jnp.float32)
            slab = slab[half * part : (half + 1) * part]
            span = width // HALVES
            packed = [slab[:, k * span : (k + 1) * span] for k in range(HALVES)]
            outgoing[half, t] = jnp.concatenate(packed, axis=0).astype(jnp.bfloat16)
    for half in range(HALVES):
        tokens[half, order(u, s, h)] = outgoing[half, s]

    pl.semaphore_wait(barrier, len(peers))

    steps = sorted(range(S), key=lambda d: min(d, S - d))

    def to_seq(half):
        for dz in reversed(steps[1:]):
            t = lax.rem(s + dz, S)
            send(
                outgoing.at[half, t],
                tokens.at[half, order(u, s, h)],
                a_send.at[half, dz - 1],
                a_recv.at[half, dz - 1],
                {"seq": t},
            )

    def to_heads(half, dz):
        place = tokens.at[half, order(u, behind(dz), h)]
        if dz:
            remote(
                place, place, a_send.at[half, dz - 1], a_recv.at[half, dz - 1], {"seq": s}
            ).wait_recv()
        for dh in range(1, H):
            send(
                place,
                place,
                b_send.at[half, dh - 1, dz],
                b_recv.at[half, dh - 1, dz],
                {"head": lax.rem(h + dh, H)},
            )

    def to_subs(half, dz):
        s_ = behind(dz)
        for dh in range(1, H):
            place = tokens.at[half, order(u, s_, lax.rem(h + H - dh, H))]
            remote(
                place, place, b_send.at[half, dh - 1, dz], b_recv.at[half, dh - 1, dz], {"head": h}
            ).wait_recv()
        place = tokens.at[half, pl.ds(order(u, s_, 0), H)]
        for du in range(1, U):
            send(
                place,
                place,
                c_send.at[half, du - 1, dz],
                c_recv.at[half, du - 1, dz],
                {"sub": lax.rem(u + du, U)},
            )

    def scale(values, gain):
        floats = values.astype(jnp.float32)
        mean_sq = jnp.mean(floats * floats, axis=-1, keepdims=True)
        return floats * lax.rsqrt(mean_sq + 1e-06) * gain[...][None, :]

    def normalize_piece(half, u_, s_):
        scaled = scale(unpack(half, order(u_, s_, 0), H), attn_gain)
        target = at(half * half_rows + (u_ * S + s_) * H * part, H * part)
        normed[target, :] = scaled.astype(jnp.bfloat16)

    def normalize_half(half):
        for dz in steps:
            normalize_piece(half, u, behind(dz))
        for dz in steps:
            s_ = behind(dz)
            for du in range(1, U):
                u_ = lax.rem(u + U - du, U)
                place = tokens.at[half, pl.ds(order(u_, s_, 0), H)]
                remote(
                    place,
                    place,
                    c_send.at[half, du - 1, dz],
                    c_recv.at[half, du - 1, dz],
                    {"sub": u},
                ).wait_recv()
                normalize_piece(half, u_, s_)

    to_seq(0)
    to_heads(0, 0)
    for load in small:
        load.wait()
    for dz in steps[1:]:
        to_heads(0, dz)
    for half in range(1, HALVES):
        to_seq(half)
        to_heads(half, 0)
    for dz in steps:
        to_subs(0, dz)
    normalize_half(0)
    load_q.wait()
    first = lax.broadcasted_iota(jnp.int32, (half_rows, half_rows), 0)
    second = lax.broadcasted_iota(jnp.int32, (half_rows, half_rows), 1)
    together = lax.rem(first, part) == lax.rem(second, part)

    def project(half):
        lanes = slice(half * half_rows, (half + 1) * half_rows)
        qkv[:, lanes] = nt_dot(wq[...], normed[lanes, :]).astype(jnp.bfloat16)

    def attend(half):
        lanes = slice(half * half_rows, (half + 1) * half_rows)

        def cut(head, index):
            base = (head * 3 + index) * head_dim
            return qkv[base : base + head_dim, lanes]

        scores = jnp.stack([tn_dot(cut(head, 1), cut(head, 0)) for head in range(heads)])
        scores = jnp.where(together[None], scores * head_dim ** (-0.5), -1e30)
        weights = jnp.exp(scores - jnp.max(scores, axis=1, keepdims=True))
        total = 1.0 / jnp.sum(weights, axis=1, keepdims=True)
        weights = (weights * total).astype(jnp.bfloat16)
        outs = [
            jnp.dot(cut(head, 2), weights[head], preferred_element_type=jnp.float32)
            for head in range(heads)
        ]
        mixed[:, lanes] = jnp.concatenate(outs, axis=0).astype(jnp.bfloat16)

    def output(half):
        lanes = slice(half * half_rows, (half + 1) * half_rows)
        branch[half] = tn_dot(mixed[:, lanes], wo[...])
        for du in range(1, U):
            u_ = lax.rem(u + du, U)
            for p in range(half * PIECES, (half + 1) * PIECES):
                start = u_ * half_unit + (p % PIECES) * piece_rows
                part_send[du - 1, piece(p), :] = branch[half, at(start, piece_rows), :].astype(
                    jnp.bfloat16
                )
                send(
                    part_send.at[du - 1, piece(p)],
                    part_recv.at[du - 1, piece(p)],
                    d_send.at[du - 1, p],
                    d_recv.at[du - 1, p],
                    {"sub": u_},
                )

    def exchange(half):
        for p in range(half * PIECES, (half + 1) * PIECES):
            place = piece(p)
            start = u * half_unit + (p % PIECES) * piece_rows
            value = branch[half, at(start, piece_rows), :]
            for du in range(1, U):
                landed = part_recv.at[du - 1, place]
                remote(
                    landed, landed, d_send.at[du - 1, p], d_recv.at[du - 1, p], {"sub": u}
                ).wait_recv()
                value = value + part_recv[du - 1, place, :].astype(jnp.float32)
            part_own[place, :] = value
            head_send[place, :] = value.astype(jnp.bfloat16)
            for dh in range(1, H):
                send(
                    head_send.at[place],
                    head_recv.at[dh - 1, place],
                    e_send.at[dh - 1, p],
                    e_recv.at[dh - 1, p],
                    {"head": lax.rem(h + dh, H)},
                )

    for half in range(HALVES):
        following = steps[1:] if half + 1 < HALVES else []
        project(half)
        for dz in following[:1]:
            to_heads(half + 1, dz)
        attend(half)
        for dz in following[1:]:
            to_heads(half + 1, dz)
        if half == 0:
            load_o.wait()
        output(half)
        early = sent[:]
        sent.clear()
        exchange(half)
        if half + 1 == HALVES:
            for copy in early:
                copy.wait_send()
        else:
            sent.extend(early)
        if half + 1 < HALVES:
            for dz in steps:
                to_subs(half + 1, dz)
            normalize_half(half + 1)

    def finish(p):
        half, index = divmod(p, PIECES)
        place = piece(p)
        value = part_own[place, :]
        for dh in range(1, H):
            landed = head_recv.at[dh - 1, place]
            remote(
                landed, landed, e_send.at[dh - 1, p], e_recv.at[dh - 1, p], {"head": h}
            ).wait_recv()
            value = value + head_recv[dh - 1, place, :].astype(jnp.float32)
        value = value + unpack(half, order(u, index * piece_seq, 0), piece_seq * H)
        value = value.astype(jnp.bfloat16)
        wide = value.astype(jnp.float32)
        hidden_wide[half, index * piece_seq : (index + 1) * piece_seq] = wide.reshape(
            piece_seq, H, part, width
        )
        placed = vit_piece(u, p)
        vit[placed, :] = scale(value, vit_gain).astype(jnp.bfloat16)
        for du in range(1, U):
            send(
                vit.at[placed],
                vit.at[placed],
                v_send.at[du - 1, p],
                v_recv.at[du - 1, p],
                {"sub": lax.rem(u + du, U)},
            )

    def send_hidden(s_):
        rows_ = [hidden_wide[half, s_, h] for half in range(HALVES)]
        hidden[s_] = jnp.concatenate(rows_, axis=0).astype(jnp.bfloat16)
        own = hidden.at[s_]

        @pl.when(s_ != s)
        def _():
            slot = lax.rem(s_ - s + S, S) - 1
            remote(
                own, hidden_out.at[at(s * cols)], o_send.at[slot], o_recv.at[slot], {"seq": s_}
            ).start()

        @pl.when(s_ == s)
        def _():
            pltpu.make_async_copy(own, hidden_out.at[at(s * cols)], local_sem.at[4]).start()

    def gelu(x):
        return 0.5 * x * (1.0 + lax.erf(x * 0.5**0.5))

    def embed(half):
        for du in range(1, U):
            for p in range(half * PIECES, (half + 1) * PIECES):
                theirs = vit.at[vit_piece(lax.rem(u + U - du, U), p)]
                remote(
                    theirs, theirs, v_send.at[du - 1, p], v_recv.at[du - 1, p], {"sub": u}
                ).wait_recv()
        block = vit[half * half_rows : (half + 1) * half_rows, :]
        now = jnp.dot(block, wp[0], preferred_element_type=jnp.float32)
        then = jnp.dot(block, wp[1], preferred_element_type=jnp.float32)
        pooled = []
        for u_ in range(U):
            start, stop = u_ * half_unit, (u_ + 1) * half_unit
            if u_ + 1 < U:
                active = gelu(now[start:stop] + then[stop : stop + half_unit])
            else:
                active = gelu(now[start : stop - part] + then[part:half_unit])
                active = jnp.concatenate([active, jnp.zeros((part, out_width), jnp.float32)], axis=0)
            pooled.append(jnp.sum(active.reshape(-1, part, out_width), axis=1))
        return jnp.concatenate(pooled, axis=0)

    load_p.wait()
    pooled = jnp.zeros((N, out_width), jnp.float32)
    for half in range(HALVES):
        for p in range(half * PIECES, (half + 1) * PIECES):
            finish(p)
            if half == HALVES - 1:
                index = p % PIECES
                for s_ in range(index * piece_seq, (index + 1) * piece_seq):
                    send_hidden(s_)
        pooled = pooled + embed(half)
    pooled = pooled * (rolls / (cols * S))
    grouped[mine, :actions_n, :N] = nt_dot(w_act[...], pooled, precision=lax.Precision.HIGHEST)
    early = sent[:]
    sent.clear()
    for step in range(1, G):
        send(
            grouped.at[mine],
            grouped.at[mine],
            p_send.at[step - 1],
            p_recv.at[step - 1],
            group_peer(step),
        )
    for copy in early:
        copy.wait_send()
    for dz in range(1, S):
        s_ = lax.rem(s + dz, S)
        remote(
            hidden.at[s_],
            hidden_out.at[at(s_ * cols)],
            o_send.at[dz - 1],
            o_recv.at[dz - 1],
            {"seq": s},
        ).wait_send()
    for step in range(1, G):
        place = grouped.at[lax.rem(mine + G - step, G)]
        remote(
            place, place, p_send.at[step - 1], p_recv.at[step - 1], {"seq": s}
        ).wait_recv()
    total = grouped[0, :actions_n, :N]
    for index in range(1, G):
        total = total + grouped[index, :actions_n, :N]
    scored[s, :actions_n, :N] = total
    for step in range(1, S):
        send(
            scored.at[s],
            scored.at[s],
            q_send.at[step - 1],
            q_recv.at[step - 1],
            seq_peer(step),
        )
    for dz in range(1, S):
        from_ = behind(dz)
        remote(
            hidden.at[from_],
            hidden_out.at[at(from_ * cols)],
            o_send.at[dz - 1],
            o_recv.at[dz - 1],
            {"seq": s},
        ).wait_recv()
    pltpu.make_async_copy(hidden.at[s], hidden_out.at[at(s * cols)], local_sem.at[4]).wait()
    for copy in sent:
        copy.wait_send()
    for step in range(1, S):
        place = scored.at[behind(step)]
        remote(
            place, place, q_send.at[step - 1], q_recv.at[step - 1], {"seq": s}
        ).wait_recv()

    row = lax.broadcasted_iota(jnp.int32, (N, picks), 0)
    frame = lax.rem(row, S * H) * U + row // (S * H)
    share = S // rolls
    for roll in range(rolls):
        total = scored[roll * share, :actions_n, :N]
        for index in range(1, share):
            total = total + scored[roll * share + index, :actions_n, :N]
        chosen = (frame == pair_frames[roll : roll + 1, :]).astype(jnp.float32)
        actions_out[:, roll, :] = jnp.dot(
            total, chosen, preferred_element_type=jnp.float32, precision=lax.Precision.HIGHEST
        )

def write_kernel(hidden_in, actions_in, hidden_out, actions_out):
    hidden_out[...] = hidden_in[...]
    actions_out[...] = actions_in[...]


def shards(frames_in, attn_gain, w_qkv, w_out, vit_gain, w_pair, w_act, pair_frames):
    S, H, U = lax.axis_size("seq"), lax.axis_size("head"), lax.axis_size("sub")
    N = S * H * U
    rows_own, width = frames_in.shape
    heads = w_qkv.shape[1]
    head_dim = w_qkv.shape[2] // 3
    out_width = w_pair.shape[2]
    actions_n = w_act.shape[1]
    rolls, picks = pair_frames.shape
    cols = rows_own // S
    whole = rows_own % S == 0 and cols % 16 == 0 and S % rolls == 0 and S % PIECES == 0
    if N != F or not whole or (H * rows_own) % 128 or (H * U * rows_own) % (128 * HALVES):
        return shards_by_frame(
            frames_in, attn_gain, w_qkv, w_out, vit_gain, w_pair, w_act, pair_frames
        )
    rows = N * cols
    unit = rows // U
    bf16, f32 = jnp.bfloat16, jnp.float32
    vmem = pl.BlockSpec(memory_space=pltpu.VMEM)
    anywhere = pl.BlockSpec(memory_space=pl.ANY)
    dma = pltpu.SemaphoreType.DMA
    hidden, actions = pl.pallas_call(
        functools.partial(fused_kernel, (S, H, U, heads, head_dim)),
        out_shape=(
            jax.ShapeDtypeStruct((rows_own, width), bf16),
            jax.ShapeDtypeStruct((actions_n, rolls, picks), f32),
        ),
        in_specs=[anywhere] * 8,
        out_specs=(anywhere, vmem),
        scratch_shapes=[
            pltpu.VMEM((width,), f32),
            pltpu.VMEM((width,), f32),
            pltpu.VMEM((actions_n, out_width), f32),
            pltpu.VMEM((rolls, picks), jnp.int32),
            pltpu.VMEM((rows_own, width), bf16),
            pltpu.VMEM((HALVES, S, cols, width // HALVES), bf16),
            pltpu.VMEM((HALVES, N, cols, width // HALVES), bf16),
            pltpu.VMEM((rows, width), bf16),
            pltpu.VMEM((heads * 3 * head_dim, width), bf16),
            pltpu.VMEM(w_out.shape, bf16),
            pltpu.VMEM(w_pair.shape, bf16),
            pltpu.VMEM((heads * 3 * head_dim, rows), bf16),
            pltpu.VMEM((heads * head_dim, rows), bf16),
            pltpu.VMEM((HALVES, rows // HALVES, width), f32),
            pltpu.VMEM((U - 1, unit, width), bf16),
            pltpu.VMEM((U - 1, unit, width), bf16),
            pltpu.VMEM((unit, width), f32),
            pltpu.VMEM((unit, width), bf16),
            pltpu.VMEM((H - 1, unit, width), bf16),
            pltpu.VMEM((HALVES, S, H, cols // HALVES, width), f32),
            pltpu.VMEM((S, cols, width), bf16),
            pltpu.VMEM((rows, width), bf16),
            pltpu.VMEM((H * U, -(-actions_n // 8) * 8, -(-N // 128) * 128), f32),
            pltpu.VMEM((S, -(-actions_n // 8) * 8, -(-N // 128) * 128), f32),
            dma((9,)),
            dma((HALVES, S - 1)),
            dma((HALVES, S - 1)),
            dma((HALVES, H - 1, S)),
            dma((HALVES, H - 1, S)),
            dma((HALVES, U - 1, S)),
            dma((HALVES, U - 1, S)),
            dma((U - 1, HALVES * PIECES)),
            dma((U - 1, HALVES * PIECES)),
            dma((H - 1, HALVES * PIECES)),
            dma((H - 1, HALVES * PIECES)),
            dma((U - 1, HALVES * PIECES)),
            dma((U - 1, HALVES * PIECES)),
            dma((S - 1,)),
            dma((S - 1,)),
            dma((H * U - 1,)),
            dma((H * U - 1,)),
            dma((S - 1,)),
            dma((S - 1,)),
        ],
        compiler_params=pltpu.CompilerParams(
            collective_id=0, has_side_effects=True, vmem_limit_bytes=60 * 1024 * 1024
        ),
    )(
        frames_in,
        attn_gain,
        jnp.transpose(w_qkv, (1, 2, 0)).reshape(heads * 3 * head_dim, width),
        w_out,
        vit_gain,
        w_pair,
        jnp.transpose(w_act, (1, 0)),
        pair_frames,
    )
    hidden, actions = pl.pallas_call(
        write_kernel,
        out_shape=(
            jax.ShapeDtypeStruct(hidden.shape, bf16),
            jax.ShapeDtypeStruct(actions.shape, f32),
        ),
        in_specs=[vmem] * 2,
        out_specs=(vmem, vmem),
    )(hidden, actions)
    return (hidden, jnp.transpose(actions, (1, 2, 0)))


def solution(mesh):
    in_specs = (
        P(("groups", "seq", "head", "sub"), None),
        P(),
        P(None, ("head", "sub"), None),
        P(("head", "sub"), None),
        P(),
        P(None, None, ("head", "sub")),
        P(("head", "sub"), None),
        P("groups", None),
    )
    out_specs = (P(("groups", "seq", "head", "sub"), None), P("groups", None, None))
    return jax.shard_map(shards, mesh=mesh, in_specs=in_specs, out_specs=out_specs, check_vma=False)
```

```python
import functools
import jax
import jax.numpy as jnp
from jax import lax
from jax.experimental import pallas as pl
from jax.experimental.pallas import tpu as pltpu
from jax.sharding import PartitionSpec as P

F = 16
ROLLS = 2


def from_behind(value, axis, steps):
    count = lax.axis_size(axis)
    leading, last = (max(0, -steps), min(count, count - steps))
    return lax.ppermute(value, axis, [(source, source + steps) for source in range(leading, last)])


def normalize(values_in, gain_vec):
    floats = values_in.astype(jnp.float32)
    mean_sq = jnp.mean(floats * floats, axis=-1, keepdims=True)
    return (floats * lax.rsqrt(mean_sq + 1e-06) * gain_vec).astype(jnp.bfloat16)


def shards_by_frame(frames_in, attn_gain, w_qkv, w_out, vit_gain, w_pair, w_act, pair_frames):
    rows_own = frames_in.shape[0]
    model_width = frames_in.shape[1]
    seq_count = lax.axis_size("seq")
    split_count = lax.axis_size(("head", "sub"))
    block_rows = rows_own * split_count
    total_cols = block_rows * seq_count // F
    frames_local = max(1, F // seq_count)
    cols_local = block_rows // frames_local
    frame_step = max(1, seq_count // F)
    heads_local = w_qkv.shape[1]
    triple_dim = w_qkv.shape[2]
    head_dim = triple_dim // 3
    qkv_matrix = w_qkv.reshape(model_width, heads_local * triple_dim)
    normed = lax.all_gather(normalize(frames_in, attn_gain), ("head", "sub"), axis=0, tiled=True)
    qkv_rows = jnp.dot(normed, qkv_matrix, preferred_element_type=jnp.float32).astype(jnp.bfloat16)
    qkv_rows = qkv_rows.reshape(
        frames_local, seq_count, cols_local // seq_count, heads_local, triple_dim
    )
    columns = lax.all_to_all(qkv_rows, "seq", split_axis=1, concat_axis=0, tiled=True)
    item_count = columns.shape[2]
    by_frame = columns.reshape(F, -1, heads_local, triple_dim)
    queries = by_frame[..., :head_dim]
    key_part = by_frame[..., head_dim : 2 * head_dim]
    value_part = by_frame[..., 2 * head_dim :]
    scores = jnp.einsum(
        "fchd,gchd->chfg", queries, key_part, preferred_element_type=jnp.float32
    ) * head_dim ** (-0.5)
    row_peak = jnp.max(scores, axis=-1, keepdims=True)
    weights = jnp.exp(scores - row_peak)
    weights = (weights / jnp.sum(weights, axis=-1, keepdims=True)).astype(jnp.bfloat16)
    mixed_out = jnp.einsum(
        "chfg,gchd->fchd", weights, value_part, preferred_element_type=jnp.float32
    ).astype(jnp.bfloat16)
    mixed_out = mixed_out.reshape(seq_count * frames_local, 1, item_count, heads_local * head_dim)
    attended = lax.all_to_all(mixed_out, "seq", split_axis=0, concat_axis=1, tiled=True)
    attended = attended.reshape(block_rows, heads_local * head_dim)
    branch_sum = lax.psum_scatter(
        jnp.dot(attended, w_out, preferred_element_type=jnp.float32).astype(jnp.bfloat16),
        ("head", "sub"),
        scatter_dimension=0,
        tiled=True,
    ).astype(jnp.float32)
    hidden = (frames_in.astype(jnp.float32) + branch_sum).astype(jnp.bfloat16)
    vit_own = normalize(hidden, vit_gain)
    vit_rows = lax.all_gather(vit_own, ("head", "sub"), axis=0, tiled=True)
    current = jnp.dot(vit_rows, w_pair[0], preferred_element_type=jnp.float32)
    ahead_proj = jnp.dot(vit_rows, w_pair[1], preferred_element_type=jnp.float32)
    ahead_proj = ahead_proj.reshape(frames_local, cols_local, -1)
    arrived = from_behind(ahead_proj[:1].astype(jnp.bfloat16), "seq", -frame_step).astype(
        jnp.float32
    )
    following = jnp.concatenate([ahead_proj[1:], arrived], axis=0).reshape(block_rows, -1)
    embedded = current + following
    activated = jax.nn.gelu(embedded, approximate=False).reshape(frames_local, cols_local, -1)
    seq_index = lax.axis_index("seq")
    first_token = seq_index * block_rows
    frame_first = first_token // total_cols
    col_first = first_token % total_cols
    patches = total_cols // ROLLS
    roll_ids = (col_first + jnp.arange(cols_local, dtype=jnp.int32)) // patches
    member = (roll_ids[None, :] == jnp.arange(ROLLS, dtype=jnp.int32)[:, None]).astype(
        jnp.float32
    ) / patches
    pooled = jnp.einsum("rp,fpe->fre", member, activated, precision=lax.Precision.HIGHEST)
    scored = jnp.einsum("fre,ea->fra", pooled, w_act, precision=lax.Precision.HIGHEST)
    frame_ids = frame_first + jnp.arange(frames_local, dtype=jnp.int32)
    selector = (pair_frames[:, :, None] == frame_ids[None, None, :]).astype(jnp.float32)
    partial_value = jnp.einsum("rjf,fra->rja", selector, scored, precision=lax.Precision.HIGHEST)
    actions = lax.psum(partial_value, ("seq", "head", "sub"))
    return (hidden, actions)


HALVES = 2
PIECES = 2


def nt_dot(lhs, rhs, **kw):
    return lax.dot_general(
        lhs, rhs, (((1,), (1,)), ((), ())), preferred_element_type=jnp.float32, **kw
    )


def tn_dot(lhs, rhs):
    return lax.dot_general(
        lhs, rhs, (((0,), (0,)), ((), ())), preferred_element_type=jnp.float32
    )


def fused_kernel(
    sizes,
    frames,
    attn_gain_in,
    w_qkv,
    w_out,
    vit_gain_in,
    w_pair,
    w_act_in,
    pair_frames_in,
    hidden_out,
    actions_out,
    attn_gain,
    vit_gain,
    w_act,
    pair_frames,
    own_frames,
    outgoing,
    tokens,
    normed,
    wq,
    wo,
    wp,
    qkv,
    mixed,
    branch,
    part_send,
    part_recv,
    part_own,
    head_send,
    head_recv,
    hidden_wide,
    hidden,
    vit,
    scored,
    local_sem,
    a_send,
    a_recv,
    b_send,
    b_recv,
    c_send,
    c_recv,
    d_send,
    d_recv,
    e_send,
    e_recv,
    v_send,
    v_recv,
    o_send,
    o_recv,
    q_send,
    q_recv,
):
    S, H, U, heads, head_dim = sizes
    N = S * H * U
    width = wq.shape[1]
    rows = mixed.shape[1]
    cols = rows // N
    unit = rows // U
    part = cols // HALVES
    half_rows = rows // HALVES
    half_unit = unit // HALVES
    pieces = HALVES * PIECES
    piece_rows = half_unit // PIECES
    piece_seq = S // PIECES
    actions_n, rolls, picks = actions_out.shape
    out_width = wp.shape[2]
    s, h, u = lax.axis_index("seq"), lax.axis_index("head"), lax.axis_index("sub")
    me = (s * H + h) * U + u

    def at(value, size=cols):
        return pl.ds(pl.multiple_of(value, size), size)

    def order(u_, s_, h_):
        return (u_ * S + s_) * H + h_

    def behind(d):
        return lax.rem(s + S - d, S)

    def piece(p):
        return at(p * piece_rows, piece_rows)

    def vit_piece(u_, p):
        half, index = divmod(p, PIECES)
        start = half * half_rows + u_ * half_unit + index * piece_rows
        return at(start, piece_rows)

    def unpack(half, start, count):
        packed = tokens[half, pl.ds(start, count)].astype(jnp.float32)
        packed = packed.reshape(count, HALVES, part, width // HALVES)
        wide = jnp.concatenate([packed[:, index] for index in range(HALVES)], axis=-1)
        return wide.reshape(count * part, width)

    def remote(source, target, send, recv, where):
        return pltpu.make_async_remote_copy(
            src_ref=source,
            dst_ref=target,
            send_sem=send,
            recv_sem=recv,
            device_id=where,
            device_id_type=pl.DeviceIdType.MESH,
        )

    sent = []

    def send(*args):
        copy = remote(*args)
        copy.start()
        sent.append(copy)

    load_q = pltpu.make_async_copy(w_qkv, wq, local_sem.at[0])
    load_o = pltpu.make_async_copy(w_out, wo, local_sem.at[1])
    load_p = pltpu.make_async_copy(w_pair, wp, local_sem.at[2])
    load_own = pltpu.make_async_copy(
        frames, own_frames, local_sem.at[3]
    )
    small = [
        pltpu.make_async_copy(source, target, local_sem.at[5 + index])
        for index, (source, target) in enumerate(
            (
                (attn_gain_in, attn_gain),
                (vit_gain_in, vit_gain),
                (w_act_in, w_act),
                (pair_frames_in, pair_frames),
            )
        )
    ]
    load_own.start()
    for load in small:
        load.start()
    load_q.start()
    load_o.start()
    load_p.start()

    barrier = pltpu.get_barrier_semaphore()

    def greet(step, carry):
        other = lax.rem(me + step, N)
        where = {"seq": other // (H * U), "head": other // U % H, "sub": other % U}
        pl.semaphore_signal(
            barrier, inc=1, device_id=where, device_id_type=pl.DeviceIdType.MESH
        )
        return carry

    lax.fori_loop(1, N, greet, 0)
    load_own.wait()
    for t in range(S):
        for half in range(HALVES):
            start = t * cols
            slab = own_frames[start : start + cols, :].astype(jnp.float32)
            slab = slab[half * part : (half + 1) * part]
            span = width // HALVES
            packed = [slab[:, k * span : (k + 1) * span] for k in range(HALVES)]
            outgoing[half, t] = jnp.concatenate(packed, axis=0).astype(jnp.bfloat16)
    for half in range(HALVES):
        tokens[half, order(u, s, h)] = outgoing[half, s]

    pl.semaphore_wait(barrier, N - 1)

    steps = sorted(range(S), key=lambda d: min(d, S - d))

    def to_seq(half):
        for dz in reversed(steps[1:]):
            t = lax.rem(s + dz, S)
            send(
                outgoing.at[half, t],
                tokens.at[half, order(u, s, h)],
                a_send.at[half, dz - 1],
                a_recv.at[half, dz - 1],
                {"seq": t},
            )

    def to_heads(half, dz):
        place = tokens.at[half, order(u, behind(dz), h)]
        if dz:
            remote(
                place, place, a_send.at[half, dz - 1], a_recv.at[half, dz - 1], {"seq": s}
            ).wait_recv()
        for dh in range(1, H):
            send(
                place,
                place,
                b_send.at[half, dh - 1, dz],
                b_recv.at[half, dh - 1, dz],
                {"head": lax.rem(h + dh, H)},
            )

    def to_subs(half, dz):
        s_ = behind(dz)
        for dh in range(1, H):
            place = tokens.at[half, order(u, s_, lax.rem(h + H - dh, H))]
            remote(
                place, place, b_send.at[half, dh - 1, dz], b_recv.at[half, dh - 1, dz], {"head": h}
            ).wait_recv()
        place = tokens.at[half, pl.ds(order(u, s_, 0), H)]
        for du in range(1, U):
            send(
                place,
                place,
                c_send.at[half, du - 1, dz],
                c_recv.at[half, du - 1, dz],
                {"sub": lax.rem(u + du, U)},
            )

    def scale(values, gain):
        floats = values.astype(jnp.float32)
        mean_sq = jnp.mean(floats * floats, axis=-1, keepdims=True)
        return floats * lax.rsqrt(mean_sq + 1e-06) * gain[...][None, :]

    def normalize_piece(half, u_, s_):
        scaled = scale(unpack(half, order(u_, s_, 0), H), attn_gain)
        target = at(half * half_rows + (u_ * S + s_) * H * part, H * part)
        normed[target, :] = scaled.astype(jnp.bfloat16)

    def normalize_half(half):
        for dz in steps:
            normalize_piece(half, u, behind(dz))
        for dz in steps:
            s_ = behind(dz)
            for du in range(1, U):
                u_ = lax.rem(u + U - du, U)
                place = tokens.at[half, pl.ds(order(u_, s_, 0), H)]
                remote(
                    place,
                    place,
                    c_send.at[half, du - 1, dz],
                    c_recv.at[half, du - 1, dz],
                    {"sub": u},
                ).wait_recv()
                normalize_piece(half, u_, s_)

    for half in range(HALVES):
        to_seq(half)
        to_heads(half, 0)
    for load in small:
        load.wait()
    for dz in steps[1:]:
        to_heads(0, dz)
    for dz in steps:
        to_subs(0, dz)
    normalize_half(0)
    load_q.wait()
    first = lax.broadcasted_iota(jnp.int32, (half_rows, half_rows), 0)
    second = lax.broadcasted_iota(jnp.int32, (half_rows, half_rows), 1)
    together = lax.rem(first, part) == lax.rem(second, part)

    def project(half):
        lanes = slice(half * half_rows, (half + 1) * half_rows)
        qkv[:, lanes] = nt_dot(wq[...], normed[lanes, :]).astype(jnp.bfloat16)

    def attend(half):
        lanes = slice(half * half_rows, (half + 1) * half_rows)

        def cut(head, index):
            base = (head * 3 + index) * head_dim
            return qkv[base : base + head_dim, lanes]

        scores = jnp.stack([tn_dot(cut(head, 1), cut(head, 0)) for head in range(heads)])
        scores = jnp.where(together[None], scores * head_dim ** (-0.5), -1e30)
        weights = jnp.exp(scores - jnp.max(scores, axis=1, keepdims=True))
        total = 1.0 / jnp.sum(weights, axis=1, keepdims=True)
        weights = (weights * total).astype(jnp.bfloat16)
        outs = [
            jnp.dot(cut(head, 2), weights[head], preferred_element_type=jnp.float32)
            for head in range(heads)
        ]
        mixed[:, lanes] = jnp.concatenate(outs, axis=0).astype(jnp.bfloat16)

    def output(half):
        lanes = slice(half * half_rows, (half + 1) * half_rows)
        branch[half] = tn_dot(mixed[:, lanes], wo[...])
        for du in range(1, U):
            u_ = lax.rem(u + du, U)
            for p in range(half * PIECES, (half + 1) * PIECES):
                start = u_ * half_unit + (p % PIECES) * piece_rows
                part_send[du - 1, piece(p), :] = branch[half, at(start, piece_rows), :].astype(
                    jnp.bfloat16
                )
                send(
                    part_send.at[du - 1, piece(p)],
                    part_recv.at[du - 1, piece(p)],
                    d_send.at[du - 1, p],
                    d_recv.at[du - 1, p],
                    {"sub": u_},
                )

    def exchange(half):
        for p in range(half * PIECES, (half + 1) * PIECES):
            place = piece(p)
            start = u * half_unit + (p % PIECES) * piece_rows
            value = branch[half, at(start, piece_rows), :]
            for du in range(1, U):
                landed = part_recv.at[du - 1, place]
                remote(
                    landed, landed, d_send.at[du - 1, p], d_recv.at[du - 1, p], {"sub": u}
                ).wait_recv()
                value = value + part_recv[du - 1, place, :].astype(jnp.float32)
            part_own[place, :] = value
            head_send[place, :] = value.astype(jnp.bfloat16)
            for dh in range(1, H):
                send(
                    head_send.at[place],
                    head_recv.at[dh - 1, place],
                    e_send.at[dh - 1, p],
                    e_recv.at[dh - 1, p],
                    {"head": lax.rem(h + dh, H)},
                )

    for half in range(HALVES):
        later = half + 1 < HALVES
        following = steps[1:] if later else []
        for dz in following[:2]:
            to_heads(half + 1, dz)
        project(half)
        for dz in following[2:]:
            to_heads(half + 1, dz)
        attend(half)
        if half == 0:
            load_o.wait()
        output(half)
        if later:
            for dz in steps:
                to_subs(half + 1, dz)
        early = sent[:]
        sent.clear()
        exchange(half)
        if later:
            sent.extend(early)
            normalize_half(half + 1)
        else:
            for copy in early:
                copy.wait_send()

    def finish(p):
        half, index = divmod(p, PIECES)
        place = piece(p)
        value = part_own[place, :]
        for dh in range(1, H):
            landed = head_recv.at[dh - 1, place]
            remote(
                landed, landed, e_send.at[dh - 1, p], e_recv.at[dh - 1, p], {"head": h}
            ).wait_recv()
            value = value + head_recv[dh - 1, place, :].astype(jnp.float32)
        value = value + unpack(half, order(u, index * piece_seq, 0), piece_seq * H)
        value = value.astype(jnp.bfloat16)
        wide = value.astype(jnp.float32)
        hidden_wide[half, index * piece_seq : (index + 1) * piece_seq] = wide.reshape(
            piece_seq, H, part, width
        )
        mine = vit_piece(u, p)
        vit[mine, :] = scale(value, vit_gain).astype(jnp.bfloat16)
        for du in range(1, U):
            send(
                vit.at[mine],
                vit.at[mine],
                v_send.at[du - 1, p],
                v_recv.at[du - 1, p],
                {"sub": lax.rem(u + du, U)},
            )

    def send_hidden(s_):
        rows_ = [hidden_wide[half, s_, h] for half in range(HALVES)]
        hidden[s_] = jnp.concatenate(rows_, axis=0).astype(jnp.bfloat16)
        own = hidden.at[s_]

        @pl.when(s_ != s)
        def _():
            slot = lax.rem(s_ - s + S, S) - 1
            remote(
                own, hidden_out.at[at(s * cols)], o_send.at[slot], o_recv.at[slot], {"seq": s_}
            ).start()

        @pl.when(s_ == s)
        def _():
            pltpu.make_async_copy(own, hidden_out.at[at(s * cols)], local_sem.at[4]).start()

    def gelu(x):
        return 0.5 * x * (1.0 + lax.erf(x * 0.5**0.5))

    def embed(half):
        for du in range(1, U):
            for p in range(half * PIECES, (half + 1) * PIECES):
                theirs = vit.at[vit_piece(lax.rem(u + U - du, U), p)]
                remote(
                    theirs, theirs, v_send.at[du - 1, p], v_recv.at[du - 1, p], {"sub": u}
                ).wait_recv()
        block = vit[half * half_rows : (half + 1) * half_rows, :]
        now = jnp.dot(block, wp[0], preferred_element_type=jnp.float32)
        then = jnp.dot(block, wp[1], preferred_element_type=jnp.float32)
        pooled = []
        for u_ in range(U):
            start, stop = u_ * half_unit, (u_ + 1) * half_unit
            if u_ + 1 < U:
                active = gelu(now[start:stop] + then[stop : stop + half_unit])
            else:
                active = gelu(now[start : stop - part] + then[part:half_unit])
                active = jnp.concatenate([active, jnp.zeros((part, out_width), jnp.float32)], axis=0)
            pooled.append(jnp.sum(active.reshape(-1, part, out_width), axis=1))
        return jnp.concatenate(pooled, axis=0)

    load_p.wait()
    pooled = jnp.zeros((N, out_width), jnp.float32)
    for half in range(HALVES):
        for p in range(half * PIECES, (half + 1) * PIECES):
            finish(p)
            if half == HALVES - 1:
                index = p % PIECES
                for s_ in range(index * piece_seq, (index + 1) * piece_seq):
                    send_hidden(s_)
        pooled = pooled + embed(half)
    pooled = pooled * (rolls / (cols * S))
    scored[me, :actions_n, :N] = nt_dot(w_act[...], pooled, precision=lax.Precision.HIGHEST)

    early = sent[:]
    sent.clear()
    for step in range(1, N):
        other = lax.rem(me + step, N)
        where = {"seq": other // (H * U), "head": other // U % H, "sub": other % U}
        send(scored.at[me], scored.at[me], q_send.at[step - 1], q_recv.at[step - 1], where)

    for copy in early:
        copy.wait_send()
    for dz in range(1, S):
        s_ = lax.rem(s + dz, S)
        remote(
            hidden.at[s_],
            hidden_out.at[at(s_ * cols)],
            o_send.at[dz - 1],
            o_recv.at[dz - 1],
            {"seq": s},
        ).wait_send()
        from_ = lax.rem(s + S - dz, S)
        remote(
            hidden.at[s_],
            hidden_out.at[at(from_ * cols)],
            o_send.at[dz - 1],
            o_recv.at[dz - 1],
            {"seq": s},
        ).wait_recv()
    pltpu.make_async_copy(
        hidden.at[s], hidden_out.at[at(s * cols)], local_sem.at[4]
    ).wait()

    for step in range(1, N):
        other = lax.rem(me + N - step, N)
        place = scored.at[other]
        remote(
            place, place, q_send.at[step - 1], q_recv.at[step - 1], {"seq": s}
        ).wait_recv()

    row = lax.broadcasted_iota(jnp.int32, (N, picks), 0)
    frame = lax.rem(row, S * H) * U + row // (S * H)
    share = N // rolls
    for roll in range(rolls):
        total = scored[roll * share, :actions_n, :N]
        for index in range(1, share):
            total = total + scored[roll * share + index, :actions_n, :N]
        chosen = (frame == pair_frames[roll : roll + 1, :]).astype(jnp.float32)
        actions_out[:, roll, :] = jnp.dot(
            total, chosen, preferred_element_type=jnp.float32, precision=lax.Precision.HIGHEST
        )

    for copy in sent:
        copy.wait_send()


def write_kernel(hidden_in, actions_in, hidden_out, actions_out):
    hidden_out[...] = hidden_in[...]
    actions_out[...] = actions_in[...]


def shards(frames_in, attn_gain, w_qkv, w_out, vit_gain, w_pair, w_act, pair_frames):
    S, H, U = lax.axis_size("seq"), lax.axis_size("head"), lax.axis_size("sub")
    N = S * H * U
    rows_own, width = frames_in.shape
    heads = w_qkv.shape[1]
    head_dim = w_qkv.shape[2] // 3
    out_width = w_pair.shape[2]
    actions_n = w_act.shape[1]
    rolls, picks = pair_frames.shape
    cols = rows_own // S
    whole = rows_own % S == 0 and cols % 16 == 0 and S % rolls == 0 and S % PIECES == 0
    if N != F or not whole or (H * rows_own) % 128 or (H * U * rows_own) % (128 * HALVES):
        return shards_by_frame(
            frames_in, attn_gain, w_qkv, w_out, vit_gain, w_pair, w_act, pair_frames
        )
    rows = N * cols
    unit = rows // U
    bf16, f32 = jnp.bfloat16, jnp.float32
    vmem = pl.BlockSpec(memory_space=pltpu.VMEM)
    anywhere = pl.BlockSpec(memory_space=pl.ANY)
    dma = pltpu.SemaphoreType.DMA
    hidden, actions = pl.pallas_call(
        functools.partial(fused_kernel, (S, H, U, heads, head_dim)),
        out_shape=(
            jax.ShapeDtypeStruct((rows_own, width), bf16),
            jax.ShapeDtypeStruct((actions_n, rolls, picks), f32),
        ),
        in_specs=[anywhere] * 8,
        out_specs=(anywhere, vmem),
        scratch_shapes=[
            pltpu.VMEM((width,), f32),
            pltpu.VMEM((width,), f32),
            pltpu.VMEM((actions_n, out_width), f32),
            pltpu.VMEM((rolls, picks), jnp.int32),
            pltpu.VMEM((rows_own, width), bf16),
            pltpu.VMEM((HALVES, S, cols, width // HALVES), bf16),
            pltpu.VMEM((HALVES, N, cols, width // HALVES), bf16),
            pltpu.VMEM((rows, width), bf16),
            pltpu.VMEM((heads * 3 * head_dim, width), bf16),
            pltpu.VMEM(w_out.shape, bf16),
            pltpu.VMEM(w_pair.shape, bf16),
            pltpu.VMEM((heads * 3 * head_dim, rows), bf16),
            pltpu.VMEM((heads * head_dim, rows), bf16),
            pltpu.VMEM((HALVES, rows // HALVES, width), f32),
            pltpu.VMEM((U - 1, unit, width), bf16),
            pltpu.VMEM((U - 1, unit, width), bf16),
            pltpu.VMEM((unit, width), f32),
            pltpu.VMEM((unit, width), bf16),
            pltpu.VMEM((H - 1, unit, width), bf16),
            pltpu.VMEM((HALVES, S, H, cols // HALVES, width), f32),
            pltpu.VMEM((S, cols, width), bf16),
            pltpu.VMEM((rows, width), bf16),
            pltpu.VMEM((N, -(-actions_n // 8) * 8, -(-N // 128) * 128), f32),
            dma((9,)),
            dma((HALVES, S - 1)),
            dma((HALVES, S - 1)),
            dma((HALVES, H - 1, S)),
            dma((HALVES, H - 1, S)),
            dma((HALVES, U - 1, S)),
            dma((HALVES, U - 1, S)),
            dma((U - 1, HALVES * PIECES)),
            dma((U - 1, HALVES * PIECES)),
            dma((H - 1, HALVES * PIECES)),
            dma((H - 1, HALVES * PIECES)),
            dma((U - 1, HALVES * PIECES)),
            dma((U - 1, HALVES * PIECES)),
            dma((S - 1,)),
            dma((S - 1,)),
            dma((N - 1,)),
            dma((N - 1,)),
        ],
        compiler_params=pltpu.CompilerParams(
            collective_id=0, has_side_effects=True, vmem_limit_bytes=60 * 1024 * 1024
        ),
    )(
        frames_in,
        attn_gain,
        jnp.transpose(w_qkv, (1, 2, 0)).reshape(heads * 3 * head_dim, width),
        w_out,
        vit_gain,
        w_pair,
        jnp.transpose(w_act, (1, 0)),
        pair_frames,
    )
    hidden, actions = pl.pallas_call(
        write_kernel,
        out_shape=(
            jax.ShapeDtypeStruct(hidden.shape, bf16),
            jax.ShapeDtypeStruct(actions.shape, f32),
        ),
        in_specs=[vmem] * 2,
        out_specs=(vmem, vmem),
    )(hidden, actions)
    return (hidden, jnp.transpose(actions, (1, 2, 0)))


def solution(mesh):
    in_specs = (
        P(("groups", "seq", "head", "sub"), None),
        P(),
        P(None, ("head", "sub"), None),
        P(("head", "sub"), None),
        P(),
        P(None, None, ("head", "sub")),
        P(("head", "sub"), None),
        P("groups", None),
    )
    out_specs = (P(("groups", "seq", "head", "sub"), None), P("groups", None, None))
    return jax.shard_map(shards, mesh=mesh, in_specs=in_specs, out_specs=out_specs, check_vma=False)
```

```python
import functools
import jax
import jax.numpy as jnp
from jax import lax
from jax.experimental import pallas as pl
from jax.experimental.pallas import tpu as pltpu
from jax.sharding import PartitionSpec as P

F = 16
ROLLS = 2


def from_behind(value, axis, steps):
    count = lax.axis_size(axis)
    leading, last = (max(0, -steps), min(count, count - steps))
    return lax.ppermute(value, axis, [(source, source + steps) for source in range(leading, last)])


def normalize(values_in, gain_vec):
    floats = values_in.astype(jnp.float32)
    mean_sq = jnp.mean(floats * floats, axis=-1, keepdims=True)
    return (floats * lax.rsqrt(mean_sq + 1e-06) * gain_vec).astype(jnp.bfloat16)


def shards_by_frame(frames_in, attn_gain, w_qkv, w_out, vit_gain, w_pair, w_act, pair_frames):
    rows_own = frames_in.shape[0]
    model_width = frames_in.shape[1]
    seq_count = lax.axis_size("seq")
    split_count = lax.axis_size(("head", "sub"))
    block_rows = rows_own * split_count
    total_cols = block_rows * seq_count // F
    frames_local = max(1, F // seq_count)
    cols_local = block_rows // frames_local
    frame_step = max(1, seq_count // F)
    heads_local = w_qkv.shape[1]
    triple_dim = w_qkv.shape[2]
    head_dim = triple_dim // 3
    qkv_matrix = w_qkv.reshape(model_width, heads_local * triple_dim)
    normed = lax.all_gather(normalize(frames_in, attn_gain), ("head", "sub"), axis=0, tiled=True)
    qkv_rows = jnp.dot(normed, qkv_matrix, preferred_element_type=jnp.float32).astype(jnp.bfloat16)
    qkv_rows = qkv_rows.reshape(
        frames_local, seq_count, cols_local // seq_count, heads_local, triple_dim
    )
    columns = lax.all_to_all(qkv_rows, "seq", split_axis=1, concat_axis=0, tiled=True)
    item_count = columns.shape[2]
    by_frame = columns.reshape(F, -1, heads_local, triple_dim)
    queries = by_frame[..., :head_dim]
    key_part = by_frame[..., head_dim : 2 * head_dim]
    value_part = by_frame[..., 2 * head_dim :]
    scores = jnp.einsum(
        "fchd,gchd->chfg", queries, key_part, preferred_element_type=jnp.float32
    ) * head_dim ** (-0.5)
    row_peak = jnp.max(scores, axis=-1, keepdims=True)
    weights = jnp.exp(scores - row_peak)
    weights = (weights / jnp.sum(weights, axis=-1, keepdims=True)).astype(jnp.bfloat16)
    mixed_out = jnp.einsum(
        "chfg,gchd->fchd", weights, value_part, preferred_element_type=jnp.float32
    ).astype(jnp.bfloat16)
    mixed_out = mixed_out.reshape(seq_count * frames_local, 1, item_count, heads_local * head_dim)
    attended = lax.all_to_all(mixed_out, "seq", split_axis=0, concat_axis=1, tiled=True)
    attended = attended.reshape(block_rows, heads_local * head_dim)
    branch_sum = lax.psum_scatter(
        jnp.dot(attended, w_out, preferred_element_type=jnp.float32).astype(jnp.bfloat16),
        ("head", "sub"),
        scatter_dimension=0,
        tiled=True,
    ).astype(jnp.float32)
    hidden = (frames_in.astype(jnp.float32) + branch_sum).astype(jnp.bfloat16)
    vit_own = normalize(hidden, vit_gain)
    vit_rows = lax.all_gather(vit_own, ("head", "sub"), axis=0, tiled=True)
    current = jnp.dot(vit_rows, w_pair[0], preferred_element_type=jnp.float32)
    ahead_proj = jnp.dot(vit_rows, w_pair[1], preferred_element_type=jnp.float32)
    ahead_proj = ahead_proj.reshape(frames_local, cols_local, -1)
    arrived = from_behind(ahead_proj[:1].astype(jnp.bfloat16), "seq", -frame_step).astype(
        jnp.float32
    )
    following = jnp.concatenate([ahead_proj[1:], arrived], axis=0).reshape(block_rows, -1)
    embedded = current + following
    activated = jax.nn.gelu(embedded, approximate=False).reshape(frames_local, cols_local, -1)
    seq_index = lax.axis_index("seq")
    first_token = seq_index * block_rows
    frame_first = first_token // total_cols
    col_first = first_token % total_cols
    patches = total_cols // ROLLS
    roll_ids = (col_first + jnp.arange(cols_local, dtype=jnp.int32)) // patches
    member = (roll_ids[None, :] == jnp.arange(ROLLS, dtype=jnp.int32)[:, None]).astype(
        jnp.float32
    ) / patches
    pooled = jnp.einsum("rp,fpe->fre", member, activated, precision=lax.Precision.HIGHEST)
    scored = jnp.einsum("fre,ea->fra", pooled, w_act, precision=lax.Precision.HIGHEST)
    frame_ids = frame_first + jnp.arange(frames_local, dtype=jnp.int32)
    selector = (pair_frames[:, :, None] == frame_ids[None, None, :]).astype(jnp.float32)
    partial_value = jnp.einsum("rjf,fra->rja", selector, scored, precision=lax.Precision.HIGHEST)
    actions = lax.psum(partial_value, ("seq", "head", "sub"))
    return (hidden, actions)


HALVES = 2
PIECES = 4


def nt_dot(lhs, rhs, **kw):
    return lax.dot_general(
        lhs, rhs, (((1,), (1,)), ((), ())), preferred_element_type=jnp.float32, **kw
    )


def tn_dot(lhs, rhs):
    return lax.dot_general(
        lhs, rhs, (((0,), (0,)), ((), ())), preferred_element_type=jnp.float32
    )


def fused_kernel(
    sizes,
    frames,
    attn_gain_in,
    w_qkv,
    w_out,
    vit_gain_in,
    w_pair,
    w_act_in,
    pair_frames_in,
    hidden_out,
    actions_out,
    attn_gain,
    vit_gain,
    w_act,
    pair_frames,
    own_frames,
    outgoing,
    tokens,
    normed,
    wq,
    wo,
    wp,
    qkv,
    mixed,
    branch,
    part_send,
    part_recv,
    part_own,
    head_send,
    head_recv,
    hidden_wide,
    hidden,
    vit,
    scored,
    local_sem,
    a_send,
    a_recv,
    b_send,
    b_recv,
    c_send,
    c_recv,
    d_send,
    d_recv,
    e_send,
    e_recv,
    v_send,
    v_recv,
    o_send,
    o_recv,
    q_send,
    q_recv,
):
    S, H, U, heads, head_dim = sizes
    N = S * H * U
    width = wq.shape[1]
    rows = mixed.shape[1]
    cols = rows // N
    unit = rows // U
    part = cols // HALVES
    half_rows = rows // HALVES
    half_unit = unit // HALVES
    pieces = HALVES * PIECES
    piece_rows = half_unit // PIECES
    piece_seq = S // PIECES
    actions_n, rolls, picks = actions_out.shape
    out_width = wp.shape[2]
    s, h, u = lax.axis_index("seq"), lax.axis_index("head"), lax.axis_index("sub")
    me = (s * H + h) * U + u

    def at(value, size=cols):
        return pl.ds(pl.multiple_of(value, size), size)

    def order(u_, s_, h_):
        return (u_ * S + s_) * H + h_

    def behind(d):
        return lax.rem(s + S - d, S)

    def piece(p):
        return at(p * piece_rows, piece_rows)

    def vit_piece(u_, p):
        half, index = divmod(p, PIECES)
        start = half * half_rows + u_ * half_unit + index * piece_rows
        return at(start, piece_rows)

    def unpack(half, start, count):
        packed = tokens[half, pl.ds(start, count)].astype(jnp.float32)
        packed = packed.reshape(count, HALVES, part, width // HALVES)
        wide = jnp.concatenate([packed[:, index] for index in range(HALVES)], axis=-1)
        return wide.reshape(count * part, width)

    def remote(source, target, send, recv, where):
        return pltpu.make_async_remote_copy(
            src_ref=source,
            dst_ref=target,
            send_sem=send,
            recv_sem=recv,
            device_id=where,
            device_id_type=pl.DeviceIdType.MESH,
        )

    sent = []

    def send(*args):
        copy = remote(*args)
        copy.start()
        sent.append(copy)

    load_q = pltpu.make_async_copy(w_qkv, wq, local_sem.at[0])
    load_o = pltpu.make_async_copy(w_out, wo, local_sem.at[1])
    load_p = pltpu.make_async_copy(w_pair, wp, local_sem.at[2])
    load_own = pltpu.make_async_copy(
        frames, own_frames, local_sem.at[3]
    )
    small = [
        pltpu.make_async_copy(source, target, local_sem.at[5 + index])
        for index, (source, target) in enumerate(
            (
                (attn_gain_in, attn_gain),
                (vit_gain_in, vit_gain),
                (w_act_in, w_act),
                (pair_frames_in, pair_frames),
            )
        )
    ]
    load_own.start()
    for load in small:
        load.start()
    load_q.start()
    load_o.start()
    load_p.start()

    barrier = pltpu.get_barrier_semaphore()

    def greet(step, carry):
        other = lax.rem(me + step, N)
        where = {"seq": other // (H * U), "head": other // U % H, "sub": other % U}
        pl.semaphore_signal(
            barrier, inc=1, device_id=where, device_id_type=pl.DeviceIdType.MESH
        )
        return carry

    lax.fori_loop(1, N, greet, 0)
    load_own.wait()
    for t in range(S):
        for half in range(HALVES):
            start = t * cols
            slab = own_frames[start : start + cols, :].astype(jnp.float32)
            slab = slab[half * part : (half + 1) * part]
            span = width // HALVES
            packed = [slab[:, k * span : (k + 1) * span] for k in range(HALVES)]
            outgoing[half, t] = jnp.concatenate(packed, axis=0).astype(jnp.bfloat16)
    for half in range(HALVES):
        tokens[half, order(u, s, h)] = outgoing[half, s]

    pl.semaphore_wait(barrier, N - 1)

    steps = sorted(range(S), key=lambda d: min(d, S - d))

    def to_seq(half):
        for dz in reversed(steps[1:]):
            t = lax.rem(s + dz, S)
            send(
                outgoing.at[half, t],
                tokens.at[half, order(u, s, h)],
                a_send.at[half, dz - 1],
                a_recv.at[half, dz - 1],
                {"seq": t},
            )

    def to_heads(half, dz):
        place = tokens.at[half, order(u, behind(dz), h)]
        if dz:
            remote(
                place, place, a_send.at[half, dz - 1], a_recv.at[half, dz - 1], {"seq": s}
            ).wait_recv()
        for dh in range(1, H):
            send(
                place,
                place,
                b_send.at[half, dh - 1, dz],
                b_recv.at[half, dh - 1, dz],
                {"head": lax.rem(h + dh, H)},
            )

    def to_subs(half, dz):
        s_ = behind(dz)
        for dh in range(1, H):
            place = tokens.at[half, order(u, s_, lax.rem(h + H - dh, H))]
            remote(
                place, place, b_send.at[half, dh - 1, dz], b_recv.at[half, dh - 1, dz], {"head": h}
            ).wait_recv()
        place = tokens.at[half, pl.ds(order(u, s_, 0), H)]
        for du in range(1, U):
            send(
                place,
                place,
                c_send.at[half, du - 1, dz],
                c_recv.at[half, du - 1, dz],
                {"sub": lax.rem(u + du, U)},
            )

    def scale(values, gain):
        floats = values.astype(jnp.float32)
        mean_sq = jnp.mean(floats * floats, axis=-1, keepdims=True)
        return floats * lax.rsqrt(mean_sq + 1e-06) * gain[...][None, :]

    def normalize_piece(half, u_, s_):
        scaled = scale(unpack(half, order(u_, s_, 0), H), attn_gain)
        target = at(half * half_rows + (u_ * S + s_) * H * part, H * part)
        normed[target, :] = scaled.astype(jnp.bfloat16)

    def normalize_half(half):
        for dz in steps:
            normalize_piece(half, u, behind(dz))
        for dz in steps:
            s_ = behind(dz)
            for du in range(1, U):
                u_ = lax.rem(u + U - du, U)
                place = tokens.at[half, pl.ds(order(u_, s_, 0), H)]
                remote(
                    place,
                    place,
                    c_send.at[half, du - 1, dz],
                    c_recv.at[half, du - 1, dz],
                    {"sub": u},
                ).wait_recv()
                normalize_piece(half, u_, s_)

    for half in range(HALVES):
        to_seq(half)
        to_heads(half, 0)
    for load in small:
        load.wait()
    for dz in steps[1:]:
        to_heads(0, dz)
    for dz in steps:
        to_subs(0, dz)
    normalize_half(0)
    load_q.wait()
    first = lax.broadcasted_iota(jnp.int32, (half_rows, half_rows), 0)
    second = lax.broadcasted_iota(jnp.int32, (half_rows, half_rows), 1)
    together = lax.rem(first, part) == lax.rem(second, part)

    def project(half):
        lanes = slice(half * half_rows, (half + 1) * half_rows)
        qkv[:, lanes] = nt_dot(wq[...], normed[lanes, :]).astype(jnp.bfloat16)

    def attend(half):
        lanes = slice(half * half_rows, (half + 1) * half_rows)

        def cut(head, index):
            base = (head * 3 + index) * head_dim
            return qkv[base : base + head_dim, lanes]

        scores = jnp.stack([tn_dot(cut(head, 1), cut(head, 0)) for head in range(heads)])
        scores = jnp.where(together[None], scores * head_dim ** (-0.5), -1e30)
        weights = jnp.exp(scores - jnp.max(scores, axis=1, keepdims=True))
        total = 1.0 / jnp.sum(weights, axis=1, keepdims=True)
        weights = (weights * total).astype(jnp.bfloat16)
        outs = [
            jnp.dot(cut(head, 2), weights[head], preferred_element_type=jnp.float32)
            for head in range(heads)
        ]
        mixed[:, lanes] = jnp.concatenate(outs, axis=0).astype(jnp.bfloat16)

    def output(half):
        lanes = slice(half * half_rows, (half + 1) * half_rows)
        branch[half] = tn_dot(mixed[:, lanes], wo[...])
        for du in range(1, U):
            u_ = lax.rem(u + du, U)
            for p in range(half * PIECES, (half + 1) * PIECES):
                start = u_ * half_unit + (p % PIECES) * piece_rows
                part_send[du - 1, piece(p), :] = branch[half, at(start, piece_rows), :].astype(
                    jnp.bfloat16
                )
                send(
                    part_send.at[du - 1, piece(p)],
                    part_recv.at[du - 1, piece(p)],
                    d_send.at[du - 1, p],
                    d_recv.at[du - 1, p],
                    {"sub": u_},
                )

    def exchange(half):
        for p in range(half * PIECES, (half + 1) * PIECES):
            place = piece(p)
            start = u * half_unit + (p % PIECES) * piece_rows
            value = branch[half, at(start, piece_rows), :]
            for du in range(1, U):
                landed = part_recv.at[du - 1, place]
                remote(
                    landed, landed, d_send.at[du - 1, p], d_recv.at[du - 1, p], {"sub": u}
                ).wait_recv()
                value = value + part_recv[du - 1, place, :].astype(jnp.float32)
            part_own[place, :] = value
            head_send[place, :] = value.astype(jnp.bfloat16)
            for dh in range(1, H):
                send(
                    head_send.at[place],
                    head_recv.at[dh - 1, place],
                    e_send.at[dh - 1, p],
                    e_recv.at[dh - 1, p],
                    {"head": lax.rem(h + dh, H)},
                )

    for half in range(HALVES):
        later = half + 1 < HALVES
        following = steps[1:] if later else []
        for dz in following[:2]:
            to_heads(half + 1, dz)
        project(half)
        for dz in following[2:]:
            to_heads(half + 1, dz)
        attend(half)
        if half == 0:
            load_o.wait()
        output(half)
        if later:
            for dz in steps:
                to_subs(half + 1, dz)
        early = sent[:]
        sent.clear()
        exchange(half)
        if later:
            sent.extend(early)
            normalize_half(half + 1)
        else:
            for copy in early:
                copy.wait_send()

    def finish(p):
        half, index = divmod(p, PIECES)
        place = piece(p)
        value = part_own[place, :]
        for dh in range(1, H):
            landed = head_recv.at[dh - 1, place]
            remote(
                landed, landed, e_send.at[dh - 1, p], e_recv.at[dh - 1, p], {"head": h}
            ).wait_recv()
            value = value + head_recv[dh - 1, place, :].astype(jnp.float32)
        value = value + unpack(half, order(u, index * piece_seq, 0), piece_seq * H)
        value = value.astype(jnp.bfloat16)
        wide = value.astype(jnp.float32)
        hidden_wide[half, index * piece_seq : (index + 1) * piece_seq] = wide.reshape(
            piece_seq, H, part, width
        )
        mine = vit_piece(u, p)
        vit[mine, :] = scale(value, vit_gain).astype(jnp.bfloat16)
        for du in range(1, U):
            send(
                vit.at[mine],
                vit.at[mine],
                v_send.at[du - 1, p],
                v_recv.at[du - 1, p],
                {"sub": lax.rem(u + du, U)},
            )

    def send_hidden(s_):
        rows_ = [hidden_wide[half, s_, h] for half in range(HALVES)]
        hidden[s_] = jnp.concatenate(rows_, axis=0).astype(jnp.bfloat16)
        own = hidden.at[s_]

        @pl.when(s_ != s)
        def _():
            slot = lax.rem(s_ - s + S, S) - 1
            remote(
                own, hidden_out.at[at(s * cols)], o_send.at[slot], o_recv.at[slot], {"seq": s_}
            ).start()

        @pl.when(s_ == s)
        def _():
            pltpu.make_async_copy(own, hidden_out.at[at(s * cols)], local_sem.at[4]).start()

    def gelu(x):
        return 0.5 * x * (1.0 + lax.erf(x * 0.5**0.5))

    def embed(half):
        for du in range(1, U):
            for p in range(half * PIECES, (half + 1) * PIECES):
                theirs = vit.at[vit_piece(lax.rem(u + U - du, U), p)]
                remote(
                    theirs, theirs, v_send.at[du - 1, p], v_recv.at[du - 1, p], {"sub": u}
                ).wait_recv()
        block = vit[half * half_rows : (half + 1) * half_rows, :]
        now = jnp.dot(block, wp[0], preferred_element_type=jnp.float32)
        then = jnp.dot(block, wp[1], preferred_element_type=jnp.float32)
        pooled = []
        for u_ in range(U):
            start, stop = u_ * half_unit, (u_ + 1) * half_unit
            if u_ + 1 < U:
                active = gelu(now[start:stop] + then[stop : stop + half_unit])
            else:
                active = gelu(now[start : stop - part] + then[part:half_unit])
                active = jnp.concatenate([active, jnp.zeros((part, out_width), jnp.float32)], axis=0)
            pooled.append(jnp.sum(active.reshape(-1, part, out_width), axis=1))
        return jnp.concatenate(pooled, axis=0)

    load_p.wait()
    pooled = jnp.zeros((N, out_width), jnp.float32)
    for half in range(HALVES):
        for p in range(half * PIECES, (half + 1) * PIECES):
            finish(p)
            if half == HALVES - 1:
                index = p % PIECES
                for s_ in range(index * piece_seq, (index + 1) * piece_seq):
                    send_hidden(s_)
        pooled = pooled + embed(half)
    pooled = pooled * (rolls / (cols * S))
    scored[me, :actions_n, :N] = nt_dot(w_act[...], pooled, precision=lax.Precision.HIGHEST)

    early = sent[:]
    sent.clear()
    for step in range(1, N):
        other = lax.rem(me + step, N)
        where = {"seq": other // (H * U), "head": other // U % H, "sub": other % U}
        send(scored.at[me], scored.at[me], q_send.at[step - 1], q_recv.at[step - 1], where)

    for copy in early:
        copy.wait_send()
    for dz in range(1, S):
        s_ = lax.rem(s + dz, S)
        remote(
            hidden.at[s_],
            hidden_out.at[at(s_ * cols)],
            o_send.at[dz - 1],
            o_recv.at[dz - 1],
            {"seq": s},
        ).wait_send()
        from_ = lax.rem(s + S - dz, S)
        remote(
            hidden.at[s_],
            hidden_out.at[at(from_ * cols)],
            o_send.at[dz - 1],
            o_recv.at[dz - 1],
            {"seq": s},
        ).wait_recv()
    pltpu.make_async_copy(
        hidden.at[s], hidden_out.at[at(s * cols)], local_sem.at[4]
    ).wait()

    for step in range(1, N):
        other = lax.rem(me + N - step, N)
        place = scored.at[other]
        remote(
            place, place, q_send.at[step - 1], q_recv.at[step - 1], {"seq": s}
        ).wait_recv()

    row = lax.broadcasted_iota(jnp.int32, (N, picks), 0)
    frame = lax.rem(row, S * H) * U + row // (S * H)
    share = N // rolls
    for roll in range(rolls):
        total = scored[roll * share, :actions_n, :N]
        for index in range(1, share):
            total = total + scored[roll * share + index, :actions_n, :N]
        chosen = (frame == pair_frames[roll : roll + 1, :]).astype(jnp.float32)
        actions_out[:, roll, :] = jnp.dot(
            total, chosen, preferred_element_type=jnp.float32, precision=lax.Precision.HIGHEST
        )

    for copy in sent:
        copy.wait_send()


def write_kernel(hidden_in, actions_in, hidden_out, actions_out):
    hidden_out[...] = hidden_in[...]
    actions_out[...] = actions_in[...]


def shards(frames_in, attn_gain, w_qkv, w_out, vit_gain, w_pair, w_act, pair_frames):
    S, H, U = lax.axis_size("seq"), lax.axis_size("head"), lax.axis_size("sub")
    N = S * H * U
    rows_own, width = frames_in.shape
    heads = w_qkv.shape[1]
    head_dim = w_qkv.shape[2] // 3
    out_width = w_pair.shape[2]
    actions_n = w_act.shape[1]
    rolls, picks = pair_frames.shape
    cols = rows_own // S
    whole = rows_own % S == 0 and cols % 16 == 0 and S % rolls == 0 and S % PIECES == 0
    if N != F or not whole or (H * rows_own) % 128 or (H * U * rows_own) % (128 * HALVES):
        return shards_by_frame(
            frames_in, attn_gain, w_qkv, w_out, vit_gain, w_pair, w_act, pair_frames
        )
    rows = N * cols
    unit = rows // U
    bf16, f32 = jnp.bfloat16, jnp.float32
    vmem = pl.BlockSpec(memory_space=pltpu.VMEM)
    anywhere = pl.BlockSpec(memory_space=pl.ANY)
    dma = pltpu.SemaphoreType.DMA
    hidden, actions = pl.pallas_call(
        functools.partial(fused_kernel, (S, H, U, heads, head_dim)),
        out_shape=(
            jax.ShapeDtypeStruct((rows_own, width), bf16),
            jax.ShapeDtypeStruct((actions_n, rolls, picks), f32),
        ),
        in_specs=[anywhere] * 8,
        out_specs=(anywhere, vmem),
        scratch_shapes=[
            pltpu.VMEM((width,), f32),
            pltpu.VMEM((width,), f32),
            pltpu.VMEM((actions_n, out_width), f32),
            pltpu.VMEM((rolls, picks), jnp.int32),
            pltpu.VMEM((rows_own, width), bf16),
            pltpu.VMEM((HALVES, S, cols, width // HALVES), bf16),
            pltpu.VMEM((HALVES, N, cols, width // HALVES), bf16),
            pltpu.VMEM((rows, width), bf16),
            pltpu.VMEM((heads * 3 * head_dim, width), bf16),
            pltpu.VMEM(w_out.shape, bf16),
            pltpu.VMEM(w_pair.shape, bf16),
            pltpu.VMEM((heads * 3 * head_dim, rows), bf16),
            pltpu.VMEM((heads * head_dim, rows), bf16),
            pltpu.VMEM((HALVES, rows // HALVES, width), f32),
            pltpu.VMEM((U - 1, unit, width), bf16),
            pltpu.VMEM((U - 1, unit, width), bf16),
            pltpu.VMEM((unit, width), f32),
            pltpu.VMEM((unit, width), bf16),
            pltpu.VMEM((H - 1, unit, width), bf16),
            pltpu.VMEM((HALVES, S, H, cols // HALVES, width), f32),
            pltpu.VMEM((S, cols, width), bf16),
            pltpu.VMEM((rows, width), bf16),
            pltpu.VMEM((N, -(-actions_n // 8) * 8, -(-N // 128) * 128), f32),
            dma((9,)),
            dma((HALVES, S - 1)),
            dma((HALVES, S - 1)),
            dma((HALVES, H - 1, S)),
            dma((HALVES, H - 1, S)),
            dma((HALVES, U - 1, S)),
            dma((HALVES, U - 1, S)),
            dma((U - 1, HALVES * PIECES)),
            dma((U - 1, HALVES * PIECES)),
            dma((H - 1, HALVES * PIECES)),
            dma((H - 1, HALVES * PIECES)),
            dma((U - 1, HALVES * PIECES)),
            dma((U - 1, HALVES * PIECES)),
            dma((S - 1,)),
            dma((S - 1,)),
            dma((N - 1,)),
            dma((N - 1,)),
        ],
        compiler_params=pltpu.CompilerParams(
            collective_id=0, has_side_effects=True, vmem_limit_bytes=60 * 1024 * 1024
        ),
    )(
        frames_in,
        attn_gain,
        jnp.transpose(w_qkv, (1, 2, 0)).reshape(heads * 3 * head_dim, width),
        w_out,
        vit_gain,
        w_pair,
        jnp.transpose(w_act, (1, 0)),
        pair_frames,
    )
    hidden, actions = pl.pallas_call(
        write_kernel,
        out_shape=(
            jax.ShapeDtypeStruct(hidden.shape, bf16),
            jax.ShapeDtypeStruct(actions.shape, f32),
        ),
        in_specs=[vmem] * 2,
        out_specs=(vmem, vmem),
    )(hidden, actions)
    return (hidden, jnp.transpose(actions, (1, 2, 0)))


def solution(mesh):
    in_specs = (
        P(("groups", "seq", "head", "sub"), None),
        P(),
        P(None, ("head", "sub"), None),
        P(("head", "sub"), None),
        P(),
        P(None, None, ("head", "sub")),
        P(("head", "sub"), None),
        P("groups", None),
    )
    out_specs = (P(("groups", "seq", "head", "sub"), None), P("groups", None, None))
    return jax.shard_map(shards, mesh=mesh, in_specs=in_specs, out_specs=out_specs, check_vma=False)
```
